32 devices in a mesh: groups: 2 (over y), scanx: 4 (over z), scany: 2 (over x), pos: 2 (over core).
Axes of the slice: x: 2, y: 2, z: 4, core: 2. Of those that a mesh axis runs over, the one named last changes fastest.
Arguments:
- specimen: float32 [2, 2048, 512], P(None, ('groups', 'scanx'), 'scany'), parts along dimension 1, may hold values from -5 to 5
- probe_wave: float32 [2, 512, 256], P(None, 'groups'), parts along dimension 1, may hold values from -6 to 6
- amplitudes: bfloat16 [64, 256, 256], P(('groups', 'scanx', 'scany', 'pos')), parts along dimension 0, may hold values from 0 to 2
- offsets: int32 [64, 2], P(('groups', 'scanx', 'scany', 'pos')), parts along dimension 0, may hold values from 0 to 255
Outputs:
- new_specimen: float32 [2, 2048, 512], P(None, ('groups', 'scanx'), 'scany'), parts along dimension 1
- new_probe: float32 [2, 512, 256], P(None, 'groups'), parts along dimension 1
The draws below stay inside these ranges and needn't reach their ends.
There are 2 independent parts, one for each index of `groups`. The reference program is written for one: setup_inputs(seed, part) draws one part's arguments, and reference() takes and returns one part's arrays. A program takes and returns all parts, laid end to end along the dimension named above; each array names one. Nothing has to cross between parts.
Inputs may be any that keep to these rules, and one draw needn't show every extreme that they name: offsets are pixels from the top-left corner of the position's tile.
All inputs are finite; a program needn't handle non-finite values.
Results may differ from the reference program's by a relative error of at most 0.002.
The reference program's roundings to bfloat16 on the way count: a program that leaves them out, or rounds other values in their place, can miss the bound.
Values sent between devices are 32-bit elements; how exact they have to be, the bound alone decides.
No kernel may reach another device: no remote copies, remote signals or barrier semaphores. Data moves between devices by JAX's collectives and lax.ppermute only.
A program may use at most 64 MiB of HBM per device.

```python
import math
import jax
import jax.numpy as jnp
from jax import lax

M = 256
TILE = 256
PER_TILE = 4
TILES_Y = 2
POSITIONS = 32
NXO = 1024
NYO = 512


def place_ends(drawn, stream_key, low, largest):
    index_at = [jax.random.randint(jax.random.fold_in(stream_key, axis), (), 0, length) for axis, length in enumerate(drawn.shape)]
    longest = drawn.shape.index(max(drawn.shape))
    neighbour = index_at[:longest] + [(index_at[longest] + 1) % drawn.shape[longest]] + index_at[longest + 1:]
    return drawn.at[tuple(index_at)].set(low).at[tuple(neighbour)].set(largest)


def level_of(rng, extent, pieces, smallest, largest):
    factor_of = 1.0
    for axis_at, shards_of in pieces:
        steps = jax.random.uniform(jax.random.fold_in(jax.random.fold_in(rng, 6), axis_at), (shards_of,), jnp.float32, smallest / len(pieces), largest / len(pieces))
        factor_of = factor_of * jnp.repeat(jnp.exp(steps), extent[axis_at] // shards_of).reshape((-1,) + (1,) * (len(extent) - 1 - axis_at))
    return factor_of


def noise(stream_key, extent, scale, limit, cuts=(), kind=jnp.bfloat16):
    result = scale * jax.random.normal(stream_key, extent, jnp.float32)
    if cuts:
        result = result * level_of(stream_key, extent, cuts, -0.22, 0.18)
    return jnp.clip(result, -limit, limit).astype(kind)


def setup_inputs(seed: int = 0, part: int = 0) -> dict:
    arg_keys = jax.random.split(jax.random.key(seed), 5)
    part_splits = jax.random.split(jax.random.fold_in(arg_keys[4], part), 5)
    specimen = noise(part_splits[0], (2, NXO, NYO), 0.7, 5.0, ((1, 4), (2, 2)), jnp.float32)
    probe_wave = noise(part_splits[1], (2, M, M), 1.0, 6.0, (), jnp.float32)
    amplitudes = jnp.clip(2.0 * jax.random.uniform(part_splits[2], (POSITIONS, M, M), jnp.float32) ** level_of(part_splits[2], (POSITIONS, M, M), ((0, 16),), -0.2, 0.2), 0.0, 2.0).astype(jnp.bfloat16)
    offsets = place_ends(jax.random.randint(part_splits[3], (POSITIONS, 2), 0, TILE), jax.random.fold_in(part_splits[3], 1), 0, TILE - 1).astype(jnp.int32)
    return dict(specimen=specimen, probe_wave=probe_wave, amplitudes=amplitudes, offsets=offsets)


def dft_tables(length):
    positions_index = jnp.arange(length, dtype=jnp.int32)
    phase_index = positions_index[:, None] * positions_index[None, :] % length
    angle_rad = phase_index.astype(jnp.float32) * (2.0 * math.pi / length)
    scale_factor = 1.0 / math.sqrt(length)
    cosine = (jnp.cos(angle_rad) * scale_factor).astype(jnp.bfloat16)
    sine_part = (jnp.sin(angle_rad) * scale_factor).astype(jnp.bfloat16)
    forward_left = jnp.stack([jnp.stack([cosine, sine_part], 1), jnp.stack([-sine_part, cosine], 1)], 0)
    forward_right = jnp.stack([jnp.stack([cosine, -sine_part], 1), jnp.stack([sine_part, cosine], 1)], 0)
    inverse_left = jnp.stack([jnp.stack([cosine, -sine_part], 1), jnp.stack([sine_part, cosine], 1)], 0)
    inverse_right = jnp.stack([jnp.stack([cosine, sine_part], 1), jnp.stack([-sine_part, cosine], 1)], 0)
    return (forward_left, forward_right, inverse_left, inverse_right)

def left_product(matrix, field_in):
    return jnp.einsum('akbr,brv->akv', matrix.astype(jnp.float32), field_in.astype(jnp.float32))

def right_product(field_in, matrix):
    return jnp.einsum('bkv,bval->akl', field_in.astype(jnp.float32), matrix.astype(jnp.float32))

def project_exit(patch_wave, probe_real, probe_imag, amplitude, tables):
    forward_left, forward_right, inverse_left, inverse_right = tables
    patch_real = patch_wave[0]
    patch_imag = patch_wave[1]
    exit_real = probe_real * patch_real - probe_imag * patch_imag
    exit_imag = probe_real * patch_imag + probe_imag * patch_real
    exit_wave = jnp.stack([exit_real, exit_imag]).astype(jnp.bfloat16)
    half_done = left_product(forward_left, exit_wave).astype(jnp.bfloat16)
    far_field = right_product(half_done, forward_right)
    magnitude = jnp.sqrt(far_field[0] * far_field[0] + far_field[1] * far_field[1])
    scale_ratio = amplitude.astype(jnp.float32) / jnp.maximum(magnitude, 0.2)
    projected = (far_field * scale_ratio[None]).astype(jnp.bfloat16)
    back_half = left_product(inverse_left, projected).astype(jnp.bfloat16)
    back_wave = right_product(back_half, inverse_right)
    return (back_wave[0] - exit_real, back_wave[1] - exit_imag, patch_real, patch_imag)

def reference(specimen, probe_wave, amplitudes, offsets):
    margin = M // 2
    tables = dft_tables(M)
    padded = jnp.pad(specimen, ((0, 0), (margin, margin), (margin, margin)))
    probe_real = probe_wave[0]
    probe_imag = probe_wave[1]
    probe_power = probe_real * probe_real + probe_imag * probe_imag
    tile_index = jnp.arange(POSITIONS, dtype=jnp.int32) // PER_TILE
    tile_row = tile_index // TILES_Y
    tile_col = tile_index % TILES_Y
    row_starts = (tile_row * TILE + offsets[:, 0]).astype(jnp.int32)
    col_starts = (tile_col * TILE + offsets[:, 1]).astype(jnp.int32)
    zero_index = jnp.zeros((), jnp.int32)

    def visit_position(carried, inputs):
        object_grad, probe_grad = carried
        amplitude, row_start, col_start = inputs
        patch_wave = lax.dynamic_slice(padded, (zero_index, row_start, col_start), (2, M, M))
        diff_real, diff_imag, patch_real, patch_imag = project_exit(patch_wave, probe_real, probe_imag, amplitude, tables)
        object_term = jnp.stack([probe_real * diff_real + probe_imag * diff_imag, probe_real * diff_imag - probe_imag * diff_real, probe_power])
        current = lax.dynamic_slice(object_grad, (zero_index, row_start, col_start), (3, M, M))
        object_grad = lax.dynamic_update_slice(object_grad, current + object_term, (zero_index, row_start, col_start))
        probe_term = jnp.stack([patch_real * diff_real + patch_imag * diff_imag, patch_real * diff_imag - patch_imag * diff_real])
        return ((object_grad, probe_grad + probe_term), None)
    start_grad = jnp.zeros((3, NXO + M, NYO + M), jnp.float32)
    start_probe = jnp.zeros((2, M, M), jnp.float32)
    (object_grad, probe_grad), unused = lax.scan(visit_position, (start_grad, start_probe), (amplitudes, row_starts, col_starts))
    core_sum = object_grad[:, margin:margin + NXO, margin:margin + NYO]
    new_specimen = specimen + core_sum[0:2] / (core_sum[2:3] + 1.0)
    step_size = 1.0 / math.sqrt(POSITIONS)
    new_probe = probe_wave + probe_grad * step_size
    return (new_specimen, new_probe)
```

```python
import functools
import math

import jax
import jax.numpy as jnp
import numpy as np
from jax import lax
from jax.experimental import pallas as pl
from jax.experimental.pallas import tpu as pltpu
from jax.sharding import PartitionSpec as P

GROUP = ("scanx", "scany", "pos")
PART_SWAP = ((0, 1), (1, 0))
VMEM = pl.BlockSpec(memory_space=pltpu.VMEM)
SMEM = pl.BlockSpec(memory_space=pltpu.SMEM)
OFFSET_ROWS = 8


def f32(*shape):
    return jax.ShapeDtypeStruct(shape, jnp.float32)


def partner(index, way, count):
    step = 1 if (index + way) % 2 == 0 else -1
    return (index + step) % count


def ways_of(count):
    return (0,) if count == 2 else (0, 1)


def side_of(index, way):
    return lax.rem(index + way + 1, 2)


def valid_of(index, way, count):
    neighbour = index + 2 * side_of(index, way) - 1
    return jnp.logical_and(neighbour >= 0, neighbour < count)


def permutation(sizes, target):
    nz, nx, nc = sizes
    pairs = []
    for z in range(nz):
        for x in range(nx):
            for c in range(nc):
                tz, tx, tc = target(z, x, c)
                pairs.append(((z * nx + x) * nc + c, (tz * nx + tx) * nc + tc))
    return pairs


def dft_tables(length):
    index = np.arange(length, dtype=np.int32)
    phase = (index[:, None] * index[None, :]) % length
    angle = phase.astype(np.float32) * np.float32(2.0 * math.pi / length)
    scale = np.float32(1.0 / math.sqrt(length))
    cosine = (np.cos(angle) * scale).astype(jnp.bfloat16)
    sine = (np.sin(angle) * scale).astype(jnp.bfloat16)
    table_a = np.block([[cosine, sine], [-sine, cosine]])
    table_b = np.block([[cosine, -sine], [sine, cosine]])
    return table_a.astype(jnp.bfloat16), table_b.astype(jnp.bfloat16)


def aligned(row):
    return pl.multiple_of((row // 8) * 8, 8), lax.rem(row, 8)


def rows_up(block, shift):
    count, width = block.shape
    groups = pltpu.roll(block.reshape(count // 8, 8, width), lax.rem(8 - shift, 8), axis=1)
    at = lax.broadcasted_iota(jnp.int32, (count // 8 - 1, 8, width), 1)
    return jnp.where(at < 8 - shift, groups[:-1], groups[1:]).reshape(count - 8, width)


def rows_down(block, shift):
    count, width = block.shape
    groups = pltpu.roll(block.reshape(count // 8, 8, width), shift, axis=1)
    blank = jnp.zeros((1, 8, width), block.dtype)
    at = lax.broadcasted_iota(jnp.int32, (count // 8 + 1, 8, width), 1)
    early = jnp.concatenate([groups, blank])
    late = jnp.concatenate([blank, groups])
    return jnp.where(at >= shift, early, late).reshape(count + 8, width)


def halo_blocks_kernel(nz, nx, off_ref, spec_ref, *outs):
    z, x, c = (lax.axis_index(a) for a in GROUP)
    margin = spec_ref.shape[1] // 2
    xways = ways_of(nx)
    rows_at = pl.multiple_of(side_of(z, c) * margin, margin)

    def note(width):
        lane = lax.broadcasted_iota(jnp.int32, (OFFSET_ROWS, width), 1)
        row = jnp.zeros((OFFSET_ROWS, width), jnp.float32)
        for k in range(off_ref.shape[0]):
            row = jnp.where(lane == k, off_ref[k].astype(jnp.float32), row)
        return row

    own = note(margin)
    for k, way in enumerate(xways):
        cols_at = pl.multiple_of(side_of(x, way) * margin, margin)
        out = outs[k]
        out[: 2 * margin, :] = spec_ref[c, :, pl.ds(cols_at, margin)]
        out[2 * margin :, :] = own
        corner = outs[len(xways) + 1 + k]
        for p in range(2):
            corner[p, :margin, :] = spec_ref[p, pl.ds(rows_at, margin), pl.ds(cols_at, margin)]
            corner[p, margin:, :] = own
    wide = note(2 * margin)
    out = outs[len(xways)]
    for p in range(2):
        out[p, :margin, :] = spec_ref[p, pl.ds(rows_at, margin), :]
        out[p, margin:, :] = wide


def positions_kernel(nz, nx, off_ref, spec_ref, probe_ref, amp_ref, ta_ref, tb_ref, *refs):
    z, x, c = (lax.axis_index(a) for a in GROUP)
    xways = ways_of(nx)
    nw = len(xways)
    recv_x, recv_z, recv_c = refs[:nw], refs[nw], refs[nw + 1 : 2 * nw + 1]
    refs = refs[2 * nw + 1 :]
    other_x, other_z, other_c = refs[:nw], refs[nw], refs[nw + 1 : 2 * nw + 1]
    obj_own, obj_other, probe_own, probe_other, padded = refs[2 * nw + 1 :]
    size = probe_ref.shape[1]
    margin = size // 2
    tile = spec_ref.shape[1]
    npos = amp_ref.shape[0]

    blank = jnp.zeros((margin, tile + size), jnp.float32)
    slim = jnp.zeros((tile, margin), jnp.float32)
    for p in range(2):
        padded[p, :margin, :] = blank
        padded[p, margin + tile :, :] = blank
        if nw == 1:
            padded[p, margin : margin + tile, :margin] = slim
            padded[p, margin : margin + tile, margin + tile :] = slim
        padded[p, margin : margin + tile, margin : margin + tile] = spec_ref[p]

    def place(part, rows_at, height, cols_at, width, valid, value):
        @pl.when(valid)
        def _():
            padded[part, pl.ds(rows_at, height), pl.ds(cols_at, width)] = value()

    def halo_at(index, way):
        return pl.multiple_of(side_of(index, way) * (margin + tile), margin)

    for k, way in enumerate(xways):
        cols_at = halo_at(x, way)
        x_ok = valid_of(x, way, nx)
        if nw > 1:
            @pl.when(jnp.logical_not(x_ok))
            def _():
                for p in range(2):
                    padded[p, margin : margin + tile, pl.ds(cols_at, margin)] = slim
        place(c, margin, tile, cols_at, margin, x_ok, lambda: recv_x[k][:tile, :])
        place(1 - c, margin, tile, cols_at, margin, x_ok, lambda: other_x[k][:tile, :])
        for zway, corner in ((c, recv_c[k]), (1 - c, other_c[k])):
            ok = jnp.logical_and(x_ok, valid_of(z, zway, nz))
            for p in range(2):
                place(p, halo_at(z, zway), margin, cols_at, margin, ok, lambda: corner[p, :margin, :])
    for zway, edge in ((c, recv_z), (1 - c, other_z)):
        for p in range(2):
            place(p, halo_at(z, zway), margin, margin, tile, valid_of(z, zway, nz), lambda: edge[p, :margin, :])

    lane = lax.broadcasted_iota(jnp.int32, (size + 8, size), 1)
    first = c == 0
    table_a = ta_ref[...]
    table_b = tb_ref[...]
    probe_real = probe_ref[0]
    probe_imag = probe_ref[1]

    def side_by_side(both):
        return jnp.concatenate([both[:size], both[size:]], axis=1)

    grad_real = jnp.zeros((size, size), jnp.float32)
    grad_imag = jnp.zeros((size, size), jnp.float32)
    for j in range(npos):
        row, col = off_ref[j, 0], off_ref[j, 1]

        base, shift = aligned(row)

        def patch(part):
            rows = padded[part, pl.ds(base, size + 8), :]
            mixed = rows_up(jnp.where(lane >= col, rows[:, :size], rows[:, size:]), shift)
            return pltpu.roll(mixed, lax.rem(size - col, size), axis=1)

        patch_real, patch_imag = patch(0), patch(1)
        exit_real = probe_real * patch_real - probe_imag * patch_imag
        exit_imag = probe_real * patch_imag + probe_imag * patch_real
        wave = jnp.concatenate([exit_real, exit_imag], axis=0).astype(jnp.bfloat16)
        half = jnp.dot(table_a, wave, preferred_element_type=jnp.float32).astype(jnp.bfloat16)
        far = jnp.dot(side_by_side(half), table_b, preferred_element_type=jnp.float32)
        far_real, far_imag = far[:, :size], far[:, size:]
        power = far_real * far_real + far_imag * far_imag
        ratio = amp_ref[j].astype(jnp.float32) * jnp.minimum(lax.rsqrt(power), 1.0 / 0.2)
        projected = jnp.concatenate([far_real * ratio, far_imag * ratio], axis=0).astype(jnp.bfloat16)
        back_half = jnp.dot(table_b, projected, preferred_element_type=jnp.float32).astype(jnp.bfloat16)
        back = jnp.dot(side_by_side(back_half), table_a, preferred_element_type=jnp.float32)
        diff_real = back[:, :size] - exit_real
        diff_imag = back[:, size:] - exit_imag
        term_real = probe_real * diff_real + probe_imag * diff_imag
        term_imag = probe_real * diff_imag - probe_imag * diff_real
        obj_own[j] = jnp.where(first, term_real, term_imag)
        obj_other[j] = jnp.where(first, term_imag, term_real)
        grad_real += patch_real * diff_real + patch_imag * diff_imag
        grad_imag += patch_real * diff_imag - patch_imag * diff_real
    probe_own[...] = jnp.where(first, grad_real, grad_imag)
    probe_other[...] = jnp.where(first, grad_imag, grad_real)


def gather_kernel(nz, nx, off_ref, own_ref, other_ref, center_ref, *refs):
    z, x = lax.axis_index("scanx"), lax.axis_index("scany")
    xways = ways_of(nx)
    *blocks, grad = refs
    npos, size, _ = own_ref.shape
    margin = size // 2
    tile = center_ref.shape[0]
    lane = lax.broadcasted_iota(jnp.int32, (size + 8, size), 1)
    grad[...] = jnp.zeros_like(grad)
    for j in range(2 * npos):
        row, col = off_ref[2 * j], off_ref[2 * j + 1]
        term = own_ref[j] if j < npos else other_ref[j - npos]
        base, shift = aligned(row)
        term = rows_down(pltpu.roll(term, col, axis=1), shift)
        low = jnp.where(lane >= col, term, 0.0)
        rows = pl.ds(base, size + 8)
        grad[rows, :size] += low
        grad[rows, size:] += term - low
    center_ref[...] = grad[margin : margin + tile, margin : margin + tile]

    def halo_at(index, way):
        return pl.multiple_of(side_of(index, way) * (margin + tile), margin)

    blocks = iter(blocks)
    for xway in xways:
        next(blocks)[...] = grad[margin : margin + tile, pl.ds(halo_at(x, xway), margin)]
    for zway in (0, 1):
        next(blocks)[...] = grad[pl.ds(halo_at(z, zway), margin), margin : margin + tile]
    for xway in xways:
        for zway in (0, 1):
            next(blocks)[...] = grad[pl.ds(halo_at(z, zway), margin), pl.ds(halo_at(x, xway), margin)]


def light_kernel(nz, nx, npos, off_ref, probe_ref, light_ref, power_ref, total):
    z, x, c = (lax.axis_index(a) for a in GROUP)
    xways = ways_of(nx)
    size = probe_ref.shape[1]
    margin = size // 2
    tile = light_ref.shape[0]
    power_ref[...] = probe_ref[0] * probe_ref[0] + probe_ref[1] * probe_ref[1]
    total[...] = jnp.zeros_like(total)
    lane = lax.broadcasted_iota(jnp.int32, (size, size), 1)

    def add(row, col, ok):
        ok = jnp.logical_and(ok, jnp.logical_and(jnp.abs(row) < tile, jnp.abs(col) < tile))

        @pl.when(ok)
        def _():
            base, shift = aligned(row + tile)
            moved = pltpu.roll(power_ref[...], lax.rem(col + size, size), axis=1)
            keep = jnp.logical_and(lane >= col, lane < col + size)
            total[pl.ds(base, size + 8), :] += rows_down(jnp.where(keep, moved, 0.0), shift)

    def visit(at, count, dz, dx, ok):
        for j in range(count):
            add(off_ref[at + 2 * j] + dz * tile - margin, off_ref[at + 2 * j + 1] + dx * tile - margin, ok)

    zero = jnp.int32(0)
    span = 4 * npos
    visit(0, npos, zero, zero, True)
    zstep = 2 * side_of(z, c) - 1
    z_ok = valid_of(z, c, nz)
    at = span
    for way in xways:
        visit(at, npos, zero, 2 * side_of(x, way) - 1, valid_of(x, way, nx))
        at += span
    visit(at, 2 * npos, zstep, zero, z_ok)
    at += span
    for way in xways:
        visit(at, 2 * npos, zstep, 2 * side_of(x, way) - 1, jnp.logical_and(z_ok, valid_of(x, way, nx)))
        at += span
    light_ref[...] = total[tile : 2 * tile, :]


def update_kernel(nz, nx, spec_ref, center_ref, light_ref, other_light_ref, *refs):
    z, x, c = (lax.axis_index(a) for a in GROUP)
    xways = ways_of(nx)
    *blocks, out_ref, grad = refs
    tile = center_ref.shape[0]
    margin = tile // 2
    grad[...] = center_ref[...]

    def edge_at(index, way):
        return pl.multiple_of(side_of(index, way) * (tile - margin), margin)

    def add(rows, cols, ok, block):
        @pl.when(ok)
        def _():
            grad[rows, cols] += block[...]

    blocks = iter(blocks)
    for xway in xways:
        add(pl.ds(0, tile), pl.ds(edge_at(x, xway), margin), valid_of(x, xway, nx), next(blocks))
    for zway in (0, 1):
        add(pl.ds(edge_at(z, zway), margin), pl.ds(0, tile), valid_of(z, zway, nz), next(blocks))
    for xway in xways:
        for zway in (0, 1):
            ok = jnp.logical_and(valid_of(x, xway, nx), valid_of(z, zway, nz))
            add(pl.ds(edge_at(z, zway), margin), pl.ds(edge_at(x, xway), margin), ok, next(blocks))
    out_ref[...] = spec_ref[c] + grad[...] / (light_ref[...] + other_light_ref[...] + 1.0)


def call(kernel, out_shape, specs, scratch=()):
    return pl.pallas_call(
        kernel,
        out_shape=out_shape,
        in_specs=specs,
        out_specs=jax.tree.map(lambda _: VMEM, out_shape),
        scratch_shapes=list(scratch),
        compiler_params=pltpu.CompilerParams(vmem_limit_bytes=32 * 1024 * 1024),
    )


def shards(sizes, specimen, probe_wave, amplitudes, offsets):
    nz, nx, nc = sizes
    size = probe_wave.shape[1]
    margin = size // 2
    tile = specimen.shape[1]
    npos = offsets.shape[0]
    xways = ways_of(nx)
    z, x, c = (lax.axis_index(a) for a in GROUP)

    def send(value, target):
        return lax.ppermute(value, GROUP, permutation(sizes, target))

    def to_core(value):
        return lax.ppermute(value, "pos", PART_SWAP)

    def zto(index, way):
        return partner(index, way, nz)

    def xto(index, way):
        return partner(index, way, nx)

    flat = jnp.concatenate([offsets.reshape(-1), to_core(offsets).reshape(-1)])

    high = OFFSET_ROWS + margin
    blocks = call(
        functools.partial(halo_blocks_kernel, nz, nx),
        [f32(tile + OFFSET_ROWS, margin)] * len(xways) + [f32(2, high, tile)] + [f32(2, high, margin)] * len(xways),
        [SMEM, VMEM],
    )(flat, specimen)
    nw = len(xways)
    recv = [send(blocks[k], lambda z, x, c, w=way: (z, xto(x, w), c)) for k, way in enumerate(xways)]
    recv.append(send(blocks[nw], lambda z, x, c: (zto(z, c), x, c)))
    recv += [
        send(blocks[nw + 1 + k], lambda z, x, c, w=way: (zto(z, c), xto(x, w), c)) for k, way in enumerate(xways)
    ]
    other = [to_core(block) for block in recv]

    table_a, table_b = dft_tables(size)
    obj_own, obj_other, probe_own, probe_other = call(
        functools.partial(positions_kernel, nz, nx),
        [f32(npos, size, size), f32(npos, size, size), f32(size, size), f32(size, size)],
        [SMEM] + [VMEM] * (5 + 2 * len(recv)),
        [pltpu.VMEM((2, tile + size, tile + size), jnp.float32)],
    )(offsets, specimen, probe_wave, amplitudes, jnp.asarray(table_a), jnp.asarray(table_b), *recv, *other)

    held = probe_own + to_core(probe_other)
    obj_recv = to_core(obj_other)
    zbits = [("z", 1 << k) for k in range(nz.bit_length() - 1)]
    xbits = [("x", 1 << k) for k in range(nx.bit_length() - 1)]
    orders = (xbits[:1] + zbits + xbits[1:], zbits + xbits)

    def stage(k):
        def target(z, x, c):
            axis, bit = orders[c][k]
            return (z ^ bit, x, c) if axis == "z" else (z, x ^ bit, c)

        return target

    rows = size // 2
    mine = jnp.where(c == 0, lax.rem(x, 2), lax.rem(z, 2))
    keep = lax.dynamic_slice_in_dim(held, mine * rows, rows, 0)
    give = lax.dynamic_slice_in_dim(held, (1 - mine) * rows, rows, 0)
    keep = keep + send(give, stage(0))
    for k in range(1, len(orders[0])):
        keep = keep + send(keep, stage(k))
    away = send(keep, stage(0))
    summed = jnp.where(mine == 0, jnp.concatenate([keep, away]), jnp.concatenate([away, keep]))
    summed_other = to_core(summed)
    total_grad = jnp.where(c == 0, jnp.stack([summed, summed_other]), jnp.stack([summed_other, summed]))
    step_size = 1.0 / math.sqrt(npos * nz * nx * nc)
    new_probe = probe_wave + total_grad * step_size

    grad_shapes = (
        [f32(tile, tile)] + [f32(tile, margin)] * nw + [f32(margin, tile)] * 2 + [f32(margin, margin)] * (2 * nw)
    )
    center, *pieces = call(
        functools.partial(gather_kernel, nz, nx),
        grad_shapes,
        [SMEM, VMEM, VMEM],
        [pltpu.VMEM((tile + size, tile + size), jnp.float32)],
    )(flat, obj_own, obj_recv)
    targets = [lambda z, x, c, w=way: (z, xto(x, w), c) for way in xways]
    targets += [lambda z, x, c, w=way: (zto(z, w), x, c) for way in (0, 1)]
    targets += [lambda z, x, c, v=xway, w=zway: (zto(z, w), xto(x, v), c) for xway in xways for zway in (0, 1)]
    arrived = [send(piece, target) for piece, target in zip(pieces, targets)]

    notes = [flat]
    for k, block in enumerate(recv):
        notes.append((block[tile, : 4 * npos] if k < nw else block[0, margin, : 4 * npos]).astype(jnp.int32))
    light, unused = call(
        functools.partial(light_kernel, nz, nx, npos),
        [f32(tile, tile), f32(size, size)],
        [SMEM, VMEM],
        [pltpu.VMEM((3 * tile, size), jnp.float32)],
    )(jnp.concatenate(notes), probe_wave)
    other_light = to_core(light)

    part = call(
        functools.partial(update_kernel, nz, nx),
        [f32(tile, tile)],
        [VMEM] * (4 + len(arrived)),
        [pltpu.VMEM((tile, tile), jnp.float32)],
    )(specimen, center, light, other_light, *arrived)[0]
    part_other = to_core(part)
    new_specimen = jnp.where(c == 0, jnp.stack([part, part_other]), jnp.stack([part_other, part]))
    return (new_specimen, new_probe)


def solution(mesh):
    sizes = tuple(mesh.shape[a] for a in GROUP)
    placed = (
        P(None, ("groups", "scanx"), "scany"),
        P(None, "groups", None),
        P(("groups", "scanx", "scany", "pos"), None, None),
        P(("groups", "scanx", "scany", "pos"), None),
    )
    return jax.shard_map(
        functools.partial(shards, sizes),
        mesh=mesh,
        in_specs=placed,
        out_specs=(P(None, ("groups", "scanx"), "scany"), P(None, "groups", None)),
        check_vma=False,
    )
```

```python
import functools
import math

import jax
import jax.numpy as jnp
import numpy as np
from jax import lax
from jax.experimental import pallas as pl
from jax.experimental.pallas import tpu as pltpu
from jax.sharding import PartitionSpec as P

GROUP = ("scanx", "scany", "pos")
PART_SWAP = ((0, 1), (1, 0))
VMEM = pl.BlockSpec(memory_space=pltpu.VMEM)
SMEM = pl.BlockSpec(memory_space=pltpu.SMEM)
ANY = pl.BlockSpec(memory_space=pl.ANY)
OFFSET_ROWS = 8


def f32(*shape):
    return jax.ShapeDtypeStruct(shape, jnp.float32)


def ways_of(count):
    return (0,) if count == 2 else (0, 1)


def side_of(index, way):
    return lax.rem(index + way + 1, 2)


def valid_of(index, way, count):
    neighbour = index + 2 * side_of(index, way) - 1
    return jnp.logical_and(neighbour >= 0, neighbour < count)


def block_ways(nz, nx):
    xways, zways = ways_of(nx), (0, 1)
    order = [(None, w) for w in xways] + [(w, None) for w in zways]
    return order + [(v, w) for w in xways for v in zways]


def block_places(z, x, nz, nx, origin, extent, margin):
    places = []
    for zway, xway in block_ways(nz, nx):
        span = []
        for index, way in ((z, zway), (x, xway)):
            if way is None:
                span.append(pl.ds(origin, 2 * margin))
            else:
                span.append(pl.ds(pl.multiple_of(side_of(index, way) * extent, margin), margin))
        places.append(tuple(span))
    return places


def block_valid(z, x, nz, nx):
    result = []
    for zway, xway in block_ways(nz, nx):
        ok = True
        if zway is not None:
            ok = valid_of(z, zway, nz)
        if xway is not None:
            ok = jnp.logical_and(ok, valid_of(x, xway, nx))
        result.append(ok)
    return result


def block_targets(nz, nx):
    def step(index, way, count):
        if way is None:
            return index
        to = index + (1 if (index + way) % 2 == 0 else -1)
        return to if 0 <= to < count else None

    def target(ways, z, x, c):
        tz, tx = step(z, ways[0], nz), step(x, ways[1], nx)
        return (z, x, 1 - c) if tz is None or tx is None else (tz, tx, c)

    return [functools.partial(target, ways) for ways in block_ways(nz, nx)]


def pack_places(shapes):
    lanes = min(width for _, width in shapes)
    at, places = 0, []
    for height, width in shapes:
        height -= OFFSET_ROWS
        places.append([])
        for col in range(0, width, lanes):
            places[-1].append((at, col, height))
            at += height
    return places


def permutation(sizes, target):
    nz, nx, nc = sizes
    pairs = []
    for z in range(nz):
        for x in range(nx):
            for c in range(nc):
                tz, tx, tc = target(z, x, c)
                pairs.append(((z * nx + x) * nc + c, (tz * nx + tx) * nc + tc))
    return pairs


def dft_tables(length):
    index = np.arange(length, dtype=np.int32)
    phase = (index[:, None] * index[None, :]) % length
    angle = phase.astype(np.float32) * np.float32(2.0 * math.pi / length)
    scale = np.float32(1.0 / math.sqrt(length))
    cosine = (np.cos(angle) * scale).astype(jnp.bfloat16)
    sine = (np.sin(angle) * scale).astype(jnp.bfloat16)
    table_a = np.block([[cosine, sine], [-sine, cosine]])
    table_b = np.block([[cosine, -sine], [sine, cosine]])
    return table_a.astype(jnp.bfloat16), table_b.astype(jnp.bfloat16)


def aligned(row):
    return pl.multiple_of((row // 8) * 8, 8), lax.rem(row, 8)


def rows_up(block, shift):
    count, width = block.shape
    groups = pltpu.roll(block.reshape(count // 8, 8, width), lax.rem(8 - shift, 8), axis=1)
    at = lax.broadcasted_iota(jnp.int32, (count // 8 - 1, 8, width), 1)
    return jnp.where(at < 8 - shift, groups[:-1], groups[1:]).reshape(count - 8, width)


def rows_down(block, shift):
    count, width = block.shape
    groups = pltpu.roll(block.reshape(count // 8, 8, width), shift, axis=1)
    blank = jnp.zeros((1, 8, width), block.dtype)
    at = lax.broadcasted_iota(jnp.int32, (count // 8 + 1, 8, width), 1)
    early = jnp.concatenate([groups, blank])
    late = jnp.concatenate([blank, groups])
    return jnp.where(at >= shift, early, late).reshape(count + 8, width)


def halo_blocks_kernel(nz, nx, off_ref, spec_ref, *refs):
    z, x, c = (lax.axis_index(a) for a in GROUP)
    *outs, sems = refs
    margin = spec_ref.shape[1] // 2
    copies = []
    for k, (rows, cols) in enumerate(block_places(z, x, nz, nx, 0, margin, margin)):
        height, width = outs[k].shape
        height -= OFFSET_ROWS
        copies.append(
            pltpu.make_async_copy(spec_ref.at[c, rows, cols], outs[k].at[pl.ds(0, height), :], sems.at[k])
        )
        copies[-1].start()
    for out in outs:
        height, width = out.shape
        lane = lax.broadcasted_iota(jnp.int32, (OFFSET_ROWS, width), 1)
        note = jnp.zeros((OFFSET_ROWS, width), jnp.float32)
        for j in range(off_ref.shape[0]):
            for k in range(2):
                note = jnp.where(lane == 2 * j + k, off_ref[j, k].astype(jnp.float32), note)
        out[height - OFFSET_ROWS :, :] = note
    for copy in copies:
        copy.wait()


def fetch_kernel(*refs):
    *refs, sems = refs
    count = len(refs) // 2
    copies = [pltpu.make_async_copy(refs[k], refs[count + k], sems.at[k]) for k in range(count)]
    for copy in copies:
        copy.start()
    for copy in copies:
        copy.wait()


def pack_kernel(unused_ref, *refs):
    *blocks, out = refs
    for part, places in zip(blocks, pack_places([b.shape for b in blocks])):
        for at, col, height in places:
            out[at : at + height, :] = part[:height, col : col + out.shape[1]]


def positions_kernel(nz, nx, off_ref, spec_ref, probe_ref, amp_ref, ta_ref, tb_ref, unused_ref, packed_ref, *refs):
    z, x, c = (lax.axis_index(a) for a in GROUP)
    *blocks, obj_own, obj_other, probe_own, probe_other, padded = refs
    size = probe_ref.shape[1]
    margin = size // 2
    tile = spec_ref.shape[1]
    npos = amp_ref.shape[0]

    padded[:, margin : margin + tile, margin : margin + tile] = spec_ref[...]
    ways = block_ways(nz, nx)
    if len(ways_of(nx)) == 1:
        far_cols = pl.ds(pl.multiple_of((1 - side_of(x, 0)) * (margin + tile), margin), margin)
        padded[:, :, far_cols] = jnp.zeros((2, tile + size, margin), jnp.float32)
    places = block_places(z, x, nz, nx, margin, margin + tile, margin)
    for block, (rows, cols), ok, packed in zip(
        blocks, places, block_valid(z, x, nz, nx), pack_places([b.shape for b in blocks])
    ):
        height, width = block.shape[0] - OFFSET_ROWS, block.shape[1]

        @pl.when(ok)
        def _():
            padded[c, rows, cols] = block[:height, :]
            pieces = [packed_ref[at : at + height, :] for at, _, _ in packed]
            padded[1 - c, rows, cols] = jnp.concatenate(pieces, axis=1) if len(pieces) > 1 else pieces[0]

        @pl.when(jnp.logical_not(ok))
        def _():
            padded[:, rows, cols] = jnp.zeros((2, height, width), jnp.float32)

    lane = lax.broadcasted_iota(jnp.int32, (size + 8, size), 1)
    first = c == 0
    table_a = ta_ref[...]
    table_b = tb_ref[...]
    probe_real = probe_ref[0]
    probe_imag = probe_ref[1]

    def side_by_side(both):
        return jnp.concatenate([both[:size], both[size:]], axis=1)

    grad_real = jnp.zeros((size, size), jnp.float32)
    grad_imag = jnp.zeros((size, size), jnp.float32)
    for j in range(npos):
        row, col = off_ref[j, 0], off_ref[j, 1]

        base, shift = aligned(row)

        def patch(part):
            rows = padded[part, pl.ds(base, size + 8), :]
            mixed = rows_up(jnp.where(lane >= col, rows[:, :size], rows[:, size:]), shift)
            return pltpu.roll(mixed, lax.rem(size - col, size), axis=1)

        patch_real, patch_imag = patch(0), patch(1)
        exit_real = probe_real * patch_real - probe_imag * patch_imag
        exit_imag = probe_real * patch_imag + probe_imag * patch_real
        wave = jnp.concatenate([exit_real, exit_imag], axis=0).astype(jnp.bfloat16)
        half = jnp.dot(table_a, wave, preferred_element_type=jnp.float32).astype(jnp.bfloat16)
        far = jnp.dot(side_by_side(half), table_b, preferred_element_type=jnp.float32)
        far_real, far_imag = far[:, :size], far[:, size:]
        power = far_real * far_real + far_imag * far_imag
        ratio = amp_ref[j].astype(jnp.float32) * jnp.minimum(lax.rsqrt(power), 1.0 / 0.2)
        projected = jnp.concatenate([far_real * ratio, far_imag * ratio], axis=0).astype(jnp.bfloat16)
        back_half = jnp.dot(table_b, projected, preferred_element_type=jnp.float32).astype(jnp.bfloat16)
        back = jnp.dot(side_by_side(back_half), table_a, preferred_element_type=jnp.float32)
        diff_real = back[:, :size] - exit_real
        diff_imag = back[:, size:] - exit_imag
        term_real = probe_real * diff_real + probe_imag * diff_imag
        term_imag = probe_real * diff_imag - probe_imag * diff_real
        obj_own[j] = jnp.where(first, term_real, term_imag)
        obj_other[j] = jnp.where(first, term_imag, term_real)
        grad_real += patch_real * diff_real + patch_imag * diff_imag
        grad_imag += patch_real * diff_imag - patch_imag * diff_real
    probe_own[...] = jnp.where(first, grad_real, grad_imag)
    probe_other[...] = jnp.where(first, grad_imag, grad_real)


def gather_kernel(nz, nx, off_ref, off_other_ref, own_ref, other_ref, center_ref, *refs):
    z, x = lax.axis_index("scanx"), lax.axis_index("scany")
    *blocks, grad = refs
    npos, size, _ = own_ref.shape
    margin = size // 2
    tile = center_ref.shape[0]
    lane = lax.broadcasted_iota(jnp.int32, (size + 8, size), 1)
    grad[...] = jnp.zeros_like(grad)
    for offs, terms in ((off_ref, own_ref), (off_other_ref, other_ref)):
        for j in range(npos):
            row, col = offs[j, 0], offs[j, 1]
            base, shift = aligned(row)
            term = rows_down(pltpu.roll(terms[j], col, axis=1), shift)
            low = jnp.where(lane >= col, term, 0.0)
            rows = pl.ds(base, size + 8)
            grad[rows, :size] += low
            grad[rows, size:] += term - low
    center_ref[...] = grad[margin : margin + tile, margin : margin + tile]
    for block, (rows, cols) in zip(blocks, block_places(z, x, nz, nx, margin, margin + tile, margin)):
        block[...] = grad[rows, cols]


def light_kernel(nz, nx, off_ref, note_ref, probe_ref, unused_ref, light_ref, power_ref, total):
    z, x, c = (lax.axis_index(a) for a in GROUP)
    size = probe_ref.shape[1]
    margin = size // 2
    tile = light_ref.shape[0]
    npos = off_ref.shape[0]
    power_ref[...] = probe_ref[0] * probe_ref[0] + probe_ref[1] * probe_ref[1]
    total[...] = jnp.zeros_like(total)
    lane = lax.broadcasted_iota(jnp.int32, (size, size), 1)

    def add(row, col, ok):
        ok = jnp.logical_and(ok, jnp.logical_and(jnp.abs(row) < tile, jnp.abs(col) < tile))

        @pl.when(ok)
        def _():
            base, shift = aligned(row + tile)
            moved = pltpu.roll(power_ref[...], lax.rem(col + size, size), axis=1)
            keep = jnp.logical_and(lane >= col, lane < col + size)
            total[pl.ds(base, size + 8), :] += rows_down(jnp.where(keep, moved, 0.0), shift)

    for j in range(npos):
        add(off_ref[j, 0] - margin, off_ref[j, 1] - margin, True)
    for k, ((zway, xway), ok) in enumerate(zip(block_ways(nz, nx), block_valid(z, x, nz, nx))):
        down = 0 if zway is None else (2 * side_of(z, zway) - 1) * tile
        right = 0 if xway is None else (2 * side_of(x, xway) - 1) * tile
        for j in range(npos):
            at = 2 * (k * npos + j)
            add(note_ref[at] + down - margin, note_ref[at + 1] + right - margin, ok)
    light_ref[...] = total[tile : 2 * tile, :]


def update_kernel(nz, nx, spec_ref, center_ref, light_ref, other_light_ref, *refs):
    z, x, c = (lax.axis_index(a) for a in GROUP)
    *blocks, out_ref, grad = refs
    tile = center_ref.shape[0]
    margin = tile // 2
    grad[...] = center_ref[...]
    places = block_places(z, x, nz, nx, 0, tile - margin, margin)
    for block, (rows, cols), ok in zip(blocks, places, block_valid(z, x, nz, nx)):

        @pl.when(ok)
        def _():
            grad[rows, cols] += block[...]

    out_ref[...] = spec_ref[c] + grad[...] / (light_ref[...] + other_light_ref[...] + 1.0)


def add_kernel(a_ref, b_ref, *refs):
    refs[-1][...] = a_ref[...] + b_ref[...]


def add_after(a, b, *earlier):
    return call(add_kernel, [f32(*a.shape)], [VMEM, VMEM] + [ANY] * len(earlier))(a, b, *earlier)[0]


def call(kernel, out_shape, specs, scratch=()):
    return pl.pallas_call(
        kernel,
        out_shape=out_shape,
        in_specs=specs,
        out_specs=jax.tree.map(lambda _: VMEM, out_shape),
        scratch_shapes=list(scratch),
        compiler_params=pltpu.CompilerParams(vmem_limit_bytes=32 * 1024 * 1024),
    )


def shards(sizes, specimen, probe_wave, amplitudes, offsets):
    nz, nx, nc = sizes
    size = probe_wave.shape[1]
    margin = size // 2
    tile = specimen.shape[1]
    npos = offsets.shape[0]
    z, x, c = (lax.axis_index(a) for a in GROUP)
    ways = block_ways(nz, nx)
    targets = block_targets(nz, nx)

    def send(value, target):
        return lax.ppermute(value, GROUP, permutation(sizes, target))

    def to_core(value):
        return lax.ppermute(value, "pos", PART_SWAP)

    shapes = [(tile if v is None else margin, tile if w is None else margin) for v, w in ways]
    blocks = call(
        functools.partial(halo_blocks_kernel, nz, nx),
        [f32(h + OFFSET_ROWS, w) for h, w in shapes],
        [SMEM, ANY],
        [pltpu.SemaphoreType.DMA((len(ways),))],
    )(offsets, specimen)
    recv = [send(block, target) for block, target in zip(blocks, targets)]

    table_a, table_b = (jnp.asarray(t) for t in dft_tables(size))
    late = (specimen, probe_wave, amplitudes, table_a, table_b)
    specimen_v, probe_v, amp_v, ta_v, tb_v = call(
        fetch_kernel,
        [jax.ShapeDtypeStruct(a.shape, a.dtype) for a in late],
        [ANY] * len(late),
        [pltpu.SemaphoreType.DMA((len(late),))],
    )(*late)

    lanes = min(w for _, w in shapes)
    packed = call(
        pack_kernel,
        [f32(sum(h * w for h, w in shapes) // lanes, lanes)],
        [ANY] + [VMEM] * len(recv),
    )(probe_v, *recv)[0]
    packed_other = to_core(packed)
    off_other = to_core(offsets)

    notes = jnp.concatenate([r[h, : 2 * npos] for r, (h, _) in zip(recv, shapes)]).astype(jnp.int32)
    light = call(
        functools.partial(light_kernel, nz, nx),
        [f32(tile, tile)],
        [SMEM, SMEM, VMEM, ANY],
        [pltpu.VMEM((size, size), jnp.float32), pltpu.VMEM((3 * tile, size), jnp.float32)],
    )(offsets, notes, probe_v, packed)[0]

    obj_own, obj_other, probe_own, probe_other = call(
        functools.partial(positions_kernel, nz, nx),
        [f32(npos, size, size), f32(npos, size, size), f32(size, size), f32(size, size)],
        [SMEM] + [VMEM] * 5 + [ANY] + [VMEM] * (1 + len(recv)),
        [pltpu.VMEM((2, tile + size, tile + size), jnp.float32)],
    )(offsets, specimen_v, probe_v, amp_v, ta_v, tb_v, light, packed_other, *recv)

    obj_recv = to_core(obj_other)
    held = probe_own + to_core(probe_other)
    other_light = to_core(light)
    zbits = [("z", 1 << k) for k in range(nz.bit_length() - 1)]
    xbits = [("x", 1 << k) for k in range(nx.bit_length() - 1)]
    orders = (xbits[:1] + zbits + xbits[1:], zbits + xbits)

    def stage(k):
        def target(z, x, c):
            axis, bit = orders[c][k]
            return (z ^ bit, x, c) if axis == "z" else (z, x ^ bit, c)

        return target

    center, *pieces = call(
        functools.partial(gather_kernel, nz, nx),
        [f32(tile, tile)] + [f32(h, w) for h, w in shapes],
        [SMEM, SMEM, VMEM, VMEM],
        [pltpu.VMEM((tile + size, tile + size), jnp.float32)],
    )(offsets, off_other, obj_own, obj_recv)
    arrived = [send(piece, target) for piece, target in zip(pieces, targets)]

    rows = size // 2
    mine = jnp.where(c == 0, lax.rem(x, 2), lax.rem(z, 2))
    keep = lax.dynamic_slice_in_dim(held, mine * rows, rows, 0)
    give = lax.dynamic_slice_in_dim(held, (1 - mine) * rows, rows, 0)
    earlier = [(center,), tuple(arrived[:2])]
    keep = add_after(keep, send(give, stage(0)), *earlier[0])
    for k in range(1, len(orders[0])):
        keep = add_after(keep, send(keep, stage(k)), *(earlier[k] if k < len(earlier) else ()))
    away = send(keep, stage(0))
    summed = jnp.where(mine == 0, jnp.concatenate([keep, away]), jnp.concatenate([away, keep]))
    summed_other = to_core(summed)
    total_grad = jnp.where(c == 0, jnp.stack([summed, summed_other]), jnp.stack([summed_other, summed]))
    step_size = 1.0 / math.sqrt(npos * nz * nx * nc)
    new_probe = probe_wave + total_grad * step_size

    part = call(
        functools.partial(update_kernel, nz, nx),
        [f32(tile, tile)],
        [VMEM] * (4 + len(arrived)),
        [pltpu.VMEM((tile, tile), jnp.float32)],
    )(specimen_v, center, light, other_light, *arrived)[0]
    part_other = to_core(part)
    new_specimen = jnp.where(c == 0, jnp.stack([part, part_other]), jnp.stack([part_other, part]))
    return (new_specimen, new_probe)


def solution(mesh):
    sizes = tuple(mesh.shape[a] for a in GROUP)
    placed = (
        P(None, ("groups", "scanx"), "scany"),
        P(None, "groups", None),
        P(("groups", "scanx", "scany", "pos"), None, None),
        P(("groups", "scanx", "scany", "pos"), None),
    )
    return jax.shard_map(
        functools.partial(shards, sizes),
        mesh=mesh,
        in_specs=placed,
        out_specs=(P(None, ("groups", "scanx"), "scany"), P(None, "groups", None)),
        check_vma=False,
    )
```

```python
import functools
import math

import jax
import jax.numpy as jnp
import numpy as np
from jax import lax
from jax.experimental import pallas as pl
from jax.experimental.pallas import tpu as pltpu
from jax.sharding import PartitionSpec as P

GROUP = ("scanx", "scany", "pos")
PART_SWAP = ((0, 1), (1, 0))
VMEM = pl.BlockSpec(memory_space=pltpu.VMEM)
SMEM = pl.BlockSpec(memory_space=pltpu.SMEM)
ANY = pl.BlockSpec(memory_space=pl.ANY)
HBM = pl.BlockSpec(memory_space=pltpu.HBM)
OFFSET_ROWS = 8


def f32(*shape):
    return jax.ShapeDtypeStruct(shape, jnp.float32)


def ways_of(count):
    return (0,) if count == 2 else (0, 1)


def side_of(index, way):
    return lax.rem(index + way + 1, 2)


def valid_of(index, way, count):
    neighbour = index + 2 * side_of(index, way) - 1
    return jnp.logical_and(neighbour >= 0, neighbour < count)


def block_ways(nz, nx):
    xways, zways = ways_of(nx), (0, 1)
    order = [(None, w) for w in xways] + [(w, None) for w in zways]
    return order + [(v, w) for w in xways for v in zways]


def block_places(z, x, nz, nx, origin, extent, margin):
    places = []
    for zway, xway in block_ways(nz, nx):
        span = []
        for index, way in ((z, zway), (x, xway)):
            if way is None:
                span.append(pl.ds(origin, 2 * margin))
            else:
                span.append(pl.ds(pl.multiple_of(side_of(index, way) * extent, margin), margin))
        places.append(tuple(span))
    return places


def block_valid(z, x, nz, nx):
    result = []
    for zway, xway in block_ways(nz, nx):
        ok = True
        if zway is not None:
            ok = valid_of(z, zway, nz)
        if xway is not None:
            ok = jnp.logical_and(ok, valid_of(x, xway, nx))
        result.append(ok)
    return result


def block_targets(nz, nx):
    def step(index, way, count):
        if way is None:
            return index
        to = index + (1 if (index + way) % 2 == 0 else -1)
        return to if 0 <= to < count else None

    def target(ways, z, x, c):
        tz, tx = step(z, ways[0], nz), step(x, ways[1], nx)
        return (z, x, 1 - c) if tz is None or tx is None else (tz, tx, c)

    return [functools.partial(target, ways) for ways in block_ways(nz, nx)]


def pack_places(shapes):
    lanes = min(width for _, width in shapes)
    at, places = 0, []
    for height, width in shapes:
        height -= OFFSET_ROWS
        places.append([])
        for col in range(0, width, lanes):
            places[-1].append((at, col, height))
            at += height
    return places


def permutation(sizes, target):
    nz, nx, nc = sizes
    pairs = []
    for z in range(nz):
        for x in range(nx):
            for c in range(nc):
                tz, tx, tc = target(z, x, c)
                pairs.append(((z * nx + x) * nc + c, (tz * nx + tx) * nc + tc))
    return pairs


def dft_tables(length):
    index = np.arange(length, dtype=np.int32)
    phase = (index[:, None] * index[None, :]) % length
    angle = phase.astype(np.float32) * np.float32(2.0 * math.pi / length)
    scale = np.float32(1.0 / math.sqrt(length))
    cosine = (np.cos(angle) * scale).astype(jnp.bfloat16)
    sine = (np.sin(angle) * scale).astype(jnp.bfloat16)
    table_a = np.block([[cosine, sine], [-sine, cosine]])
    table_b = np.block([[cosine, -sine], [sine, cosine]])
    return table_a.astype(jnp.bfloat16), table_b.astype(jnp.bfloat16)


def aligned(row):
    return pl.multiple_of((row // 8) * 8, 8), lax.rem(row, 8)


def rows_up(block, shift):
    count, width = block.shape
    groups = pltpu.roll(block.reshape(count // 8, 8, width), lax.rem(8 - shift, 8), axis=1)
    at = lax.broadcasted_iota(jnp.int32, (count // 8 - 1, 8, width), 1)
    return jnp.where(at < 8 - shift, groups[:-1], groups[1:]).reshape(count - 8, width)


def rows_down(block, shift):
    count, width = block.shape
    groups = pltpu.roll(block.reshape(count // 8, 8, width), shift, axis=1)
    blank = jnp.zeros((1, 8, width), block.dtype)
    at = lax.broadcasted_iota(jnp.int32, (count // 8 + 1, 8, width), 1)
    early = jnp.concatenate([groups, blank])
    late = jnp.concatenate([blank, groups])
    return jnp.where(at >= shift, early, late).reshape(count + 8, width)


def halo_blocks_kernel(nz, nx, off_hbm, spec_ref, *refs):
    z, x, c = (lax.axis_index(a) for a in GROUP)
    *outs, off_ref, off_sem, sems = refs
    margin = spec_ref.shape[1] // 2
    off_copy = pltpu.make_async_copy(off_hbm, off_ref, off_sem)
    off_copy.start()
    copies = []
    for k, (rows, cols) in enumerate(block_places(z, x, nz, nx, 0, margin, margin)):
        height, width = outs[k].shape
        height -= OFFSET_ROWS
        copies.append(
            pltpu.make_async_copy(spec_ref.at[c, rows, cols], outs[k].at[pl.ds(0, height), :], sems.at[k])
        )
        copies[-1].start()
    off_copy.wait()
    for out in outs:
        height, width = out.shape
        lane = lax.broadcasted_iota(jnp.int32, (OFFSET_ROWS, width), 1)
        note = jnp.zeros((OFFSET_ROWS, width), jnp.float32)
        for j in range(off_ref.shape[0]):
            for k in range(2):
                note = jnp.where(lane == 2 * j + k, off_ref[j, k].astype(jnp.float32), note)
        out[height - OFFSET_ROWS :, :] = note
    for copy in copies:
        copy.wait()


def fetch_kernel(*refs):
    *refs, sems = refs
    count = len(refs) // 2
    copies = [pltpu.make_async_copy(refs[k], refs[count + k], sems.at[k]) for k in range(count)]
    for copy in copies:
        copy.start()
    for copy in copies:
        copy.wait()


def pack_kernel(unused_ref, *refs):
    *blocks, out = refs
    for part, places in zip(blocks, pack_places([b.shape for b in blocks])):
        for at, col, height in places:
            out[at : at + height, :] = part[:height, col : col + out.shape[1]]


def positions_kernel(nz, nx, off_hbm, spec_ref, probe_ref, amp_ref, ta_ref, tb_ref, unused_ref, packed_ref, *refs):
    z, x, c = (lax.axis_index(a) for a in GROUP)
    *blocks, obj_own, obj_other, probe_own, probe_other, padded, off_ref, off_sem = refs
    off_copy = pltpu.make_async_copy(off_hbm, off_ref, off_sem)
    off_copy.start()
    size = probe_ref.shape[1]
    margin = size // 2
    tile = spec_ref.shape[1]
    npos = amp_ref.shape[0]

    padded[:, margin : margin + tile, margin : margin + tile] = spec_ref[...]
    ways = block_ways(nz, nx)
    if len(ways_of(nx)) == 1:
        far_cols = pl.ds(pl.multiple_of((1 - side_of(x, 0)) * (margin + tile), margin), margin)
        padded[:, :, far_cols] = jnp.zeros((2, tile + size, margin), jnp.float32)
    places = block_places(z, x, nz, nx, margin, margin + tile, margin)
    for block, (rows, cols), ok, packed in zip(
        blocks, places, block_valid(z, x, nz, nx), pack_places([b.shape for b in blocks])
    ):
        height, width = block.shape[0] - OFFSET_ROWS, block.shape[1]

        @pl.when(ok)
        def _():
            padded[c, rows, cols] = block[:height, :]
            pieces = [packed_ref[at : at + height, :] for at, _, _ in packed]
            padded[1 - c, rows, cols] = jnp.concatenate(pieces, axis=1) if len(pieces) > 1 else pieces[0]

        @pl.when(jnp.logical_not(ok))
        def _():
            padded[:, rows, cols] = jnp.zeros((2, height, width), jnp.float32)

    lane = lax.broadcasted_iota(jnp.int32, (size + 8, size), 1)
    first = c == 0
    off_copy.wait()
    table_a = ta_ref[...]
    table_b = tb_ref[...]
    probe_real = probe_ref[0]
    probe_imag = probe_ref[1]

    def side_by_side(both):
        return jnp.concatenate([both[:size], both[size:]], axis=1)

    grad_real = jnp.zeros((size, size), jnp.float32)
    grad_imag = jnp.zeros((size, size), jnp.float32)
    for j in range(npos):
        row, col = off_ref[j, 0], off_ref[j, 1]

        base, shift = aligned(row)

        def patch(part):
            rows = padded[part, pl.ds(base, size + 8), :]
            mixed = rows_up(jnp.where(lane >= col, rows[:, :size], rows[:, size:]), shift)
            return pltpu.roll(mixed, lax.rem(size - col, size), axis=1)

        patch_real, patch_imag = patch(0), patch(1)
        exit_real = probe_real * patch_real - probe_imag * patch_imag
        exit_imag = probe_real * patch_imag + probe_imag * patch_real
        wave = jnp.concatenate([exit_real, exit_imag], axis=0).astype(jnp.bfloat16)
        half = jnp.dot(table_a, wave, preferred_element_type=jnp.float32).astype(jnp.bfloat16)
        far = jnp.dot(side_by_side(half), table_b, preferred_element_type=jnp.float32)
        far_real, far_imag = far[:, :size], far[:, size:]
        power = far_real * far_real + far_imag * far_imag
        ratio = amp_ref[j].astype(jnp.float32) * jnp.minimum(lax.rsqrt(power), 1.0 / 0.2)
        projected = jnp.concatenate([far_real * ratio, far_imag * ratio], axis=0).astype(jnp.bfloat16)
        back_half = jnp.dot(table_b, projected, preferred_element_type=jnp.float32).astype(jnp.bfloat16)
        back = jnp.dot(side_by_side(back_half), table_a, preferred_element_type=jnp.float32)
        diff_real = back[:, :size] - exit_real
        diff_imag = back[:, size:] - exit_imag
        term_real = probe_real * diff_real + probe_imag * diff_imag
        term_imag = probe_real * diff_imag - probe_imag * diff_real
        obj_own[j] = jnp.where(first, term_real, term_imag)
        obj_other[j] = jnp.where(first, term_imag, term_real)
        grad_real += patch_real * diff_real + patch_imag * diff_imag
        grad_imag += patch_real * diff_imag - patch_imag * diff_real
    probe_own[...] = jnp.where(first, grad_real, grad_imag)
    probe_other[...] = jnp.where(first, grad_imag, grad_real)


def gather_kernel(nz, nx, off_hbm, off_other_hbm, own_ref, other_ref, middle_ref, *refs):
    x = lax.axis_index("scany")
    *blocks, grad, off_ref, off_other_ref, sems = refs
    copies = [
        pltpu.make_async_copy(off_hbm, off_ref, sems.at[0]),
        pltpu.make_async_copy(off_other_hbm, off_other_ref, sems.at[1]),
    ]
    for copy in copies:
        copy.start()
    npos, size, _ = own_ref.shape
    margin = size // 2
    tile = middle_ref.shape[1]
    lane = lax.broadcasted_iota(jnp.int32, (size + 8, size), 1)
    grad[...] = jnp.zeros_like(grad)
    for copy, offs, terms in zip(copies, (off_ref, off_other_ref), (own_ref, other_ref)):
        copy.wait()
        for j in range(npos):
            row, col = offs[j, 0], offs[j, 1]
            base, shift = aligned(row)
            term = rows_down(pltpu.roll(terms[j], col, axis=1), shift)
            low = jnp.where(lane >= col, term, 0.0)
            rows = pl.ds(base, size + 8)
            grad[rows, :size] += low
            grad[rows, size:] += term - low
    middle_ref[...] = grad[:, margin : margin + tile]
    for block, way in zip(blocks, ways_of(nx)):
        at = pl.multiple_of(side_of(x, way) * (margin + tile), margin)
        block[...] = grad[:, pl.ds(at, margin)]


def fold_kernel(nz, nx, middle_ref, *refs):
    z, x = lax.axis_index("scanx"), lax.axis_index("scany")
    ways = ways_of(nx)
    blocks, (center_ref, *edges, total) = refs[: len(ways)], refs[len(ways) :]
    tile = center_ref.shape[0]
    margin = tile // 2
    total[...] = middle_ref[...]
    for block, way in zip(blocks, ways):
        at = pl.multiple_of(side_of(x, way) * (tile - margin), margin)

        @pl.when(valid_of(x, way, nx))
        def _():
            total[:, pl.ds(at, margin)] += block[...]

    center_ref[...] = total[margin : margin + tile, :]
    for way, edge in enumerate(edges):
        edge[...] = total[pl.ds(pl.multiple_of(side_of(z, way) * (margin + tile), margin), margin), :]


def light_kernel(nz, nx, off_hbm, note_ref, probe_ref, unused_ref, light_ref, power_ref, total, off_ref, off_sem):
    off_copy = pltpu.make_async_copy(off_hbm, off_ref, off_sem)
    off_copy.start()
    z, x, c = (lax.axis_index(a) for a in GROUP)
    size = probe_ref.shape[1]
    margin = size // 2
    tile = light_ref.shape[0]
    npos = off_ref.shape[0]
    power_ref[...] = probe_ref[0] * probe_ref[0] + probe_ref[1] * probe_ref[1]
    total[...] = jnp.zeros_like(total)
    lane = lax.broadcasted_iota(jnp.int32, (size, size), 1)

    def add(row, col, ok):
        ok = jnp.logical_and(ok, jnp.logical_and(jnp.abs(row) < tile, jnp.abs(col) < tile))

        @pl.when(ok)
        def _():
            base, shift = aligned(row + tile)
            moved = pltpu.roll(power_ref[...], lax.rem(col + size, size), axis=1)
            keep = jnp.logical_and(lane >= col, lane < col + size)
            total[pl.ds(base, size + 8), :] += rows_down(jnp.where(keep, moved, 0.0), shift)

    off_copy.wait()
    for j in range(npos):
        add(off_ref[j, 0] - margin, off_ref[j, 1] - margin, True)
    for k, ((zway, xway), ok) in enumerate(zip(block_ways(nz, nx), block_valid(z, x, nz, nx))):
        down = 0 if zway is None else (2 * side_of(z, zway) - 1) * tile
        right = 0 if xway is None else (2 * side_of(x, xway) - 1) * tile
        for j in range(npos):
            at = 2 * (k * npos + j)
            add(note_ref[at] + down - margin, note_ref[at + 1] + right - margin, ok)
    light_ref[...] = total[tile : 2 * tile, :]


def update_kernel(nz, spec_ref, center_ref, light_ref, other_light_ref, *refs):
    z, c = lax.axis_index("scanx"), lax.axis_index("pos")
    *edges, out_ref, grad = refs
    tile = center_ref.shape[0]
    margin = tile // 2
    grad[...] = center_ref[...]
    for way, edge in enumerate(edges):
        at = pl.multiple_of(side_of(z, way) * (tile - margin), margin)

        @pl.when(valid_of(z, way, nz))
        def _():
            grad[pl.ds(at, margin), :] += edge[...]

    out_ref[...] = spec_ref[c] + grad[...] / (light_ref[...] + other_light_ref[...] + 1.0)


def add_kernel(a_ref, b_ref, *refs):
    refs[-1][...] = a_ref[...] + b_ref[...]


def add_after(a, b, *earlier):
    return call(add_kernel, [f32(*a.shape)], [VMEM, VMEM] + [ANY] * len(earlier))(a, b, *earlier)[0]


def call(kernel, out_shape, specs, scratch=()):
    return pl.pallas_call(
        kernel,
        out_shape=out_shape,
        in_specs=specs,
        out_specs=jax.tree.map(lambda _: VMEM, out_shape),
        scratch_shapes=list(scratch),
        compiler_params=pltpu.CompilerParams(vmem_limit_bytes=16 * 1024 * 1024),
    )


def shards(sizes, specimen, probe_wave, amplitudes, offsets):
    nz, nx, nc = sizes
    size = probe_wave.shape[1]
    margin = size // 2
    tile = specimen.shape[1]
    npos = offsets.shape[0]
    z, x, c = (lax.axis_index(a) for a in GROUP)
    ways = block_ways(nz, nx)
    targets = block_targets(nz, nx)

    def send(value, target):
        return lax.ppermute(value, GROUP, permutation(sizes, target))

    def to_core(value):
        return lax.ppermute(value, "pos", PART_SWAP)

    off_scratch = pltpu.SMEM(offsets.shape, jnp.int32)
    shapes = [(tile if v is None else margin, tile if w is None else margin) for v, w in ways]
    blocks = call(
        functools.partial(halo_blocks_kernel, nz, nx),
        [f32(h + OFFSET_ROWS, w) for h, w in shapes],
        [HBM, HBM],
        [off_scratch, pltpu.SemaphoreType.DMA, pltpu.SemaphoreType.DMA((len(ways),))],
    )(offsets, specimen)
    recv = [send(block, target) for block, target in zip(blocks, targets)]

    table_a, table_b = (jnp.asarray(t) for t in dft_tables(size))
    late = (specimen, probe_wave, amplitudes, table_a, table_b)
    specimen_v, probe_v, amp_v, ta_v, tb_v = call(
        fetch_kernel,
        [jax.ShapeDtypeStruct(a.shape, a.dtype) for a in late],
        [HBM] * len(late),
        [pltpu.SemaphoreType.DMA((len(late),))],
    )(*late)

    lanes = min(w for _, w in shapes)
    packed = call(
        pack_kernel,
        [f32(sum(h * w for h, w in shapes) // lanes, lanes)],
        [ANY] + [VMEM] * len(recv),
    )(probe_v, *recv)[0]
    packed_other = to_core(packed)
    off_other = to_core(offsets)

    notes = jnp.concatenate([r[h, : 2 * npos] for r, (h, _) in zip(recv, shapes)]).astype(jnp.int32)
    light = call(
        functools.partial(light_kernel, nz, nx),
        [f32(tile, tile)],
        [HBM, SMEM, VMEM, ANY],
        [
            pltpu.VMEM((size, size), jnp.float32),
            pltpu.VMEM((3 * tile, size), jnp.float32),
            off_scratch,
            pltpu.SemaphoreType.DMA,
        ],
    )(offsets, notes, probe_v, packed)[0]

    obj_own, obj_other, probe_own, probe_other = call(
        functools.partial(positions_kernel, nz, nx),
        [f32(npos, size, size), f32(npos, size, size), f32(size, size), f32(size, size)],
        [HBM] + [VMEM] * 5 + [ANY] + [VMEM] * (1 + len(recv)),
        [pltpu.VMEM((2, tile + size, tile + size), jnp.float32), off_scratch, pltpu.SemaphoreType.DMA],
    )(offsets, specimen_v, probe_v, amp_v, ta_v, tb_v, light, packed_other, *recv)

    obj_recv = to_core(obj_other)
    held = probe_own + to_core(probe_other)
    other_light = to_core(light)
    zbits = [("z", 1 << k) for k in range(nz.bit_length() - 1)]
    xbits = [("x", 1 << k) for k in range(nx.bit_length() - 1)]
    orders = (xbits[:1] + zbits + xbits[1:], zbits + xbits)

    def stage(k):
        def target(z, x, c):
            axis, bit = orders[c][k]
            return (z ^ bit, x, c) if axis == "z" else (z, x ^ bit, c)

        return target

    xways = ways_of(nx)
    middle, *beyond = call(
        functools.partial(gather_kernel, nz, nx),
        [f32(tile + size, tile)] + [f32(tile + size, margin)] * len(xways),
        [HBM, HBM, VMEM, VMEM],
        [
            pltpu.VMEM((tile + size, tile + size), jnp.float32),
            off_scratch,
            off_scratch,
            pltpu.SemaphoreType.DMA((2,)),
        ],
    )(offsets, off_other, obj_own, obj_recv)
    beside = [send(piece, targets[ways.index((None, way))]) for piece, way in zip(beyond, xways)]
    center, *edges = call(
        functools.partial(fold_kernel, nz, nx),
        [f32(tile, tile)] + [f32(margin, tile)] * 2,
        [VMEM] * (1 + len(beside)),
        [pltpu.VMEM((tile + size, tile), jnp.float32)],
    )(middle, *beside)
    arrived = [send(edge, targets[ways.index((way, None))]) for way, edge in enumerate(edges)]

    rows = size // 2
    halves = (lax.rem(x, 2), lax.rem(z, 2))
    mine = jnp.where(c == 0, halves[0], halves[1])
    theirs = jnp.where(c == 0, halves[1], halves[0])
    keep = lax.dynamic_slice_in_dim(held, mine * rows, rows, 0)
    give = lax.dynamic_slice_in_dim(held, (1 - mine) * rows, rows, 0)
    last = len(orders[0]) - 1
    earlier = {0: (middle,), 1: (center,), last: tuple(arrived)}
    for k in range(last + 1):
        keep = add_after(keep, send(give if k == 0 else keep, stage(k)), *earlier.get(k, ()))
    away = send(keep, stage(0))

    def joined(half, keep, away):
        return jnp.where(half == 0, jnp.concatenate([keep, away]), jnp.concatenate([away, keep]))

    def in_order(own, other):
        return jnp.where(c == 0, jnp.stack([own, other]), jnp.stack([other, own]))

    part = call(
        functools.partial(update_kernel, nz),
        [f32(tile, tile)],
        [VMEM] * (4 + len(arrived)),
        [pltpu.VMEM((tile, tile), jnp.float32)],
    )(specimen_v, center, light, other_light, *arrived)[0]
    new_specimen = in_order(part, to_core(part))

    step_size = 1.0 / math.sqrt(npos * nz * nx * nc)
    total_grad = in_order(joined(mine, keep, away), joined(theirs, to_core(keep), to_core(away)))
    new_probe = probe_v + total_grad * step_size
    return (new_specimen, new_probe)


def solution(mesh):
    sizes = tuple(mesh.shape[a] for a in GROUP)
    placed = (
        P(None, ("groups", "scanx"), "scany"),
        P(None, "groups", None),
        P(("groups", "scanx", "scany", "pos"), None, None),
        P(("groups", "scanx", "scany", "pos"), None),
    )
    return jax.shard_map(
        functools.partial(shards, sizes),
        mesh=mesh,
        in_specs=placed,
        out_specs=(P(None, ("groups", "scanx"), "scany"), P(None, "groups", None)),
        check_vma=False,
    )
```

```python
import functools
import math

import jax
import jax.numpy as jnp
import numpy as np
from jax import lax
from jax.experimental import pallas as pl
from jax.experimental.pallas import tpu as pltpu
from jax.sharding import PartitionSpec as P

GROUP = ("scanx", "scany", "pos")
PART_SWAP = ((0, 1), (1, 0))
VMEM = pl.BlockSpec(memory_space=pltpu.VMEM)
ANY = pl.BlockSpec(memory_space=pl.ANY)
HBM = pl.BlockSpec(memory_space=pltpu.HBM)
NOTE = (8, 128)
NOTE_SMEM = pltpu.SMEM(NOTE, jnp.float32)


def f32(*shape):
    return jax.ShapeDtypeStruct(shape, jnp.float32)


def ways_of(count):
    return (0,) if count == 2 else (0, 1)


def side_of(index, way):
    return lax.rem(index + way + 1, 2)


def valid_of(index, way, count):
    neighbour = index + 2 * side_of(index, way) - 1
    return jnp.logical_and(neighbour >= 0, neighbour < count)


def block_ways(nz, nx):
    xways, zways = ways_of(nx), (0, 1)
    order = [(None, w) for w in xways] + [(w, None) for w in zways]
    return order + [(v, w) for w in xways for v in zways]


def block_places(z, x, nz, nx, origin, extent, margin):
    places = []
    for zway, xway in block_ways(nz, nx):
        span = []
        for index, way in ((z, zway), (x, xway)):
            if way is None:
                span.append(pl.ds(origin, 2 * margin))
            else:
                span.append(pl.ds(pl.multiple_of(side_of(index, way) * extent, margin), margin))
        places.append(tuple(span))
    return places


def block_valid(z, x, nz, nx):
    result = []
    for zway, xway in block_ways(nz, nx):
        ok = True
        if zway is not None:
            ok = valid_of(z, zway, nz)
        if xway is not None:
            ok = jnp.logical_and(ok, valid_of(x, xway, nx))
        result.append(ok)
    return result


def block_targets(nz, nx):
    def step(index, way, count):
        if way is None:
            return index
        to = index + (1 if (index + way) % 2 == 0 else -1)
        return to if 0 <= to < count else None

    def target(ways, z, x, c):
        tz, tx = step(z, ways[0], nz), step(x, ways[1], nx)
        return (z, x, 1 - c) if tz is None or tx is None else (tz, tx, c)

    return [functools.partial(target, ways) for ways in block_ways(nz, nx)]


def permutation(sizes, target):
    nz, nx, nc = sizes
    pairs = []
    for z in range(nz):
        for x in range(nx):
            for c in range(nc):
                tz, tx, tc = target(z, x, c)
                pairs.append(((z * nx + x) * nc + c, (tz * nx + tx) * nc + tc))
    return pairs


def dft_tables(length):
    index = np.arange(length, dtype=np.int32)
    phase = (index[:, None] * index[None, :]) % length
    angle = phase.astype(np.float32) * np.float32(2.0 * math.pi / length)
    scale = np.float32(1.0 / math.sqrt(length))
    cosine = (np.cos(angle) * scale).astype(jnp.bfloat16)
    sine = (np.sin(angle) * scale).astype(jnp.bfloat16)
    table_a = np.block([[cosine, sine], [-sine, cosine]])
    table_b = np.block([[cosine, -sine], [sine, cosine]])
    return table_a.astype(jnp.bfloat16), table_b.astype(jnp.bfloat16)


def aligned(row):
    return pl.multiple_of((row // 8) * 8, 8), lax.rem(row, 8)


def rows_up(block, shift):
    count, width = block.shape
    groups = pltpu.roll(block.reshape(count // 8, 8, width), lax.rem(8 - shift, 8), axis=1)
    at = lax.broadcasted_iota(jnp.int32, (count // 8 - 1, 8, width), 1)
    return jnp.where(at < 8 - shift, groups[:-1], groups[1:]).reshape(count - 8, width)


def rows_down(block, shift):
    count, width = block.shape
    groups = pltpu.roll(block.reshape(count // 8, 8, width), shift, axis=1)
    blank = jnp.zeros((1, 8, width), block.dtype)
    at = lax.broadcasted_iota(jnp.int32, (count // 8 + 1, 8, width), 1)
    early = jnp.concatenate([groups, blank])
    late = jnp.concatenate([blank, groups])
    return jnp.where(at >= shift, early, late).reshape(count + 8, width)


def halo_blocks_kernel(nz, nx, off_hbm, spec_ref, *refs):
    z, x, c = (lax.axis_index(a) for a in GROUP)
    *outs, note_ref, off_ref, sems = refs
    margin = spec_ref.shape[1] // 2
    off_copy = pltpu.make_async_copy(off_hbm, off_ref, sems.at[len(outs)])
    off_copy.start()
    copies = []
    for k, (rows, cols) in enumerate(block_places(z, x, nz, nx, 0, margin, margin)):
        height = outs[k].shape[0] - NOTE[0]
        copies.append(
            pltpu.make_async_copy(spec_ref.at[c, rows, cols], outs[k].at[pl.ds(0, height), :], sems.at[k])
        )
        copies[-1].start()
    off_copy.wait()
    lane = lax.broadcasted_iota(jnp.int32, NOTE, 1)
    note = jnp.zeros(NOTE, jnp.float32)
    for j in range(off_ref.shape[0]):
        for k in range(2):
            note = jnp.where(lane == 2 * j + k, off_ref[j, k].astype(jnp.float32), note)
    note_ref[...] = note
    for out in outs:
        out[out.shape[0] - NOTE[0] :, : NOTE[1]] = note
    for copy in copies:
        copy.wait()


def read_notes(notes, smems, sems):
    copies = [pltpu.make_async_copy(note, smem, sems.at[k]) for k, (note, smem) in enumerate(zip(notes, smems))]
    for copy in copies:
        copy.start()
    return copies


def note_of(block):
    return block.at[pl.ds(block.shape[0] - NOTE[0], NOTE[0]), pl.ds(0, NOTE[1])]


def offset_in(note, j):
    return note[0, 2 * j].astype(jnp.int32), note[0, 2 * j + 1].astype(jnp.int32)


def fetch_kernel(*refs):
    *refs, sems = refs
    count = len(refs) // 2
    copies = [pltpu.make_async_copy(refs[k], refs[count + k], sems.at[k]) for k in range(count)]
    for copy in copies:
        copy.start()
    for copy in copies:
        copy.wait()


def cut_patches(note, padded, out):
    npos, size, _ = out.shape
    lane = lax.broadcasted_iota(jnp.int32, (size + 8, size), 1)
    for j in range(npos):
        row, col = offset_in(note, j)
        base, shift = aligned(row)
        rows = padded[pl.ds(base, size + 8), :]
        mixed = rows_up(jnp.where(lane >= col, rows[:, :size], rows[:, size:]), shift)
        out[j] = pltpu.roll(mixed, lax.rem(size - col, size), axis=1)


def other_patches_kernel(nz, nx, note_ref, spec_ref, *refs):
    z, x, c = (lax.axis_index(a) for a in GROUP)
    *blocks, out, padded, note, sems = refs
    copies = read_notes([note_ref], [note], sems)
    tile = spec_ref.shape[1]
    margin = (padded.shape[0] - tile) // 2
    padded[margin : margin + tile, margin : margin + tile] = spec_ref[c]
    if len(ways_of(nx)) == 1:
        far_cols = pl.ds(pl.multiple_of((1 - side_of(x, 0)) * (margin + tile), margin), margin)
        padded[:, far_cols] = jnp.zeros((padded.shape[0], margin), jnp.float32)
    places = block_places(z, x, nz, nx, margin, margin + tile, margin)
    for block, (rows, cols), ok in zip(blocks, places, block_valid(z, x, nz, nx)):
        height, width = block.shape[0] - NOTE[0], block.shape[1]

        @pl.when(ok)
        def _():
            padded[rows, cols] = block[:height, :]

        @pl.when(jnp.logical_not(ok))
        def _():
            padded[rows, cols] = jnp.zeros((height, width), jnp.float32)

    copies[0].wait()
    cut_patches(note, padded, out)


def own_patches_kernel(note_ref, padded, unused_ref, out, note, sems):
    read_notes([note_ref], [note], sems)[0].wait()
    cut_patches(note, padded, out)


def positions_kernel(patch_ref, patch_other_ref, probe_ref, amp_ref, ta_ref, tb_ref, own_ref, other_ref):
    first = lax.axis_index("pos") == 0
    npos, size, _ = patch_ref.shape
    table_a = ta_ref[...]
    table_b = tb_ref[...]
    probe_real = probe_ref[0]
    probe_imag = probe_ref[1]

    def side_by_side(both):
        return jnp.concatenate([both[:size], both[size:]], axis=1)

    grad_real = jnp.zeros((size, size), jnp.float32)
    grad_imag = jnp.zeros((size, size), jnp.float32)
    for j in range(npos):
        patch_real = jnp.where(first, patch_ref[j], patch_other_ref[j])
        patch_imag = jnp.where(first, patch_other_ref[j], patch_ref[j])
        exit_real = probe_real * patch_real - probe_imag * patch_imag
        exit_imag = probe_real * patch_imag + probe_imag * patch_real
        wave = jnp.concatenate([exit_real, exit_imag], axis=0).astype(jnp.bfloat16)
        half = jnp.dot(table_a, wave, preferred_element_type=jnp.float32).astype(jnp.bfloat16)
        far = jnp.dot(side_by_side(half), table_b, preferred_element_type=jnp.float32)
        far_real, far_imag = far[:, :size], far[:, size:]
        power = far_real * far_real + far_imag * far_imag
        ratio = amp_ref[j].astype(jnp.float32) * jnp.minimum(lax.rsqrt(power), 1.0 / 0.2)
        projected = jnp.concatenate([far_real * ratio, far_imag * ratio], axis=0).astype(jnp.bfloat16)
        back_half = jnp.dot(table_b, projected, preferred_element_type=jnp.float32).astype(jnp.bfloat16)
        back = jnp.dot(side_by_side(back_half), table_a, preferred_element_type=jnp.float32)
        diff_real = back[:, :size] - exit_real
        diff_imag = back[:, size:] - exit_imag
        term_real = probe_real * diff_real + probe_imag * diff_imag
        term_imag = probe_real * diff_imag - probe_imag * diff_real
        own_ref[j] = jnp.where(first, term_real, term_imag)
        other_ref[j] = jnp.where(first, term_imag, term_real)
        grad_real += patch_real * diff_real + patch_imag * diff_imag
        grad_imag += patch_real * diff_imag - patch_imag * diff_real
    own_ref[npos] = jnp.where(first, grad_real, grad_imag)
    other_ref[npos] = jnp.where(first, grad_imag, grad_real)


def half_of(z, x, c):
    return jnp.where(c == 0, lax.rem(x, 2), lax.rem(z, 2))


def halve_kernel(own_ref, recv_ref, keep_ref, give_ref):
    half = half_of(*(lax.axis_index(a) for a in GROUP))
    rows = keep_ref.shape[0]
    last = own_ref.shape[0] - 1
    for at, out in ((half, keep_ref), (1 - half, give_ref)):
        span = pl.ds(pl.multiple_of(at * rows, rows), rows)
        out[...] = own_ref[last, span, :] + recv_ref[last, span, :]


def gather_kernel(note_ref, other_note_ref, own_ref, recv_ref, unused_ref, grad, note, other_note, sems):
    copies = read_notes([note_ref, other_note_ref], [note, other_note], sems)
    count, size, _ = own_ref.shape
    lane = lax.broadcasted_iota(jnp.int32, (size + 8, size), 1)
    grad[...] = jnp.zeros_like(grad)
    for copy, offs, terms in zip(copies, (note, other_note), (own_ref, recv_ref)):
        copy.wait()
        for j in range(count - 1):
            row, col = offset_in(offs, j)
            base, shift = aligned(row)
            term = rows_down(pltpu.roll(terms[j], col, axis=1), shift)
            low = jnp.where(lane >= col, term, 0.0)
            rows = pl.ds(base, size + 8)
            grad[rows, :size] += low
            grad[rows, size:] += term - low


def cut_step_kernel(nx, keep_ref, recv_ref, grad_ref, out_ref, middle_ref, *blocks):
    x = lax.axis_index("scany")
    out_ref[...] = keep_ref[...] + recv_ref[...]
    tile = middle_ref.shape[1]
    margin = (middle_ref.shape[0] - tile) // 2
    middle_ref[...] = grad_ref[:, margin : margin + tile]
    for block, way in zip(blocks, ways_of(nx)):
        block[...] = grad_ref[:, pl.ds(pl.multiple_of(side_of(x, way) * (margin + tile), margin), margin)]


def fold_step_kernel(nz, nx, keep_ref, recv_ref, unused_ref, middle_ref, *refs):
    z, x = lax.axis_index("scanx"), lax.axis_index("scany")
    ways = ways_of(nx)
    blocks, (out_ref, center_ref, *edges, total) = refs[: len(ways)], refs[len(ways) :]
    out_ref[...] = keep_ref[...] + recv_ref[...]
    tile = center_ref.shape[0]
    margin = (middle_ref.shape[0] - tile) // 2
    total[...] = middle_ref[...]
    for block, way in zip(blocks, ways):
        at = pl.multiple_of(side_of(x, way) * (tile - margin), margin)

        @pl.when(valid_of(x, way, nx))
        def _():
            total[:, pl.ds(at, margin)] += block[...]

    center_ref[...] = total[margin : margin + tile, :]
    for way, edge in enumerate(edges):
        edge[...] = total[pl.ds(pl.multiple_of(side_of(z, way) * (margin + tile), margin), margin), :]


def update_step_kernel(nz, keep_ref, recv_ref, spec_ref, center_ref, light_ref, other_light_ref, *refs):
    z, c = lax.axis_index("scanx"), lax.axis_index("pos")
    *edges, out_ref, part_ref, grad = refs
    out_ref[...] = keep_ref[...] + recv_ref[...]
    tile = center_ref.shape[0]
    grad[...] = center_ref[...]
    for way, edge in enumerate(edges):
        margin = edge.shape[0]
        at = pl.multiple_of(side_of(z, way) * (tile - margin), margin)

        @pl.when(valid_of(z, way, nz))
        def _():
            grad[pl.ds(at, margin), :] += edge[...]

    part_ref[...] = spec_ref[c] + grad[...] / (light_ref[...] + other_light_ref[...] + 1.0)


def add_kernel(a_ref, b_ref, out_ref):
    out_ref[...] = a_ref[...] + b_ref[...]


def specimen_kernel(part_ref, part_other_ref, out_ref):
    c = lax.axis_index("pos")
    out_ref[c] = part_ref[...]
    out_ref[1 - c] = part_other_ref[...]


def probe_kernel(step_size, probe_ref, keep_ref, away_ref, keep_other_ref, away_other_ref, out_ref):
    z, x, c = (lax.axis_index(a) for a in GROUP)
    rows = keep_ref.shape[0]
    for part, keep, away in ((c, keep_ref, away_ref), (1 - c, keep_other_ref, away_other_ref)):
        half = half_of(z, x, part)
        for at, term in ((half, keep), (1 - half, away)):
            span = pl.ds(pl.multiple_of(at * rows, rows), rows)
            out_ref[part, span, :] = probe_ref[part, span, :] + term[...] * step_size


def light_kernel(npos, nz, nx, note_ref, probe_ref, unused_ref, *refs):
    z, x, c = (lax.axis_index(a) for a in GROUP)
    ways = block_ways(nz, nx)
    blocks, (light_ref, power_ref, total, *notes, sems) = refs[: len(ways)], refs[len(ways) :]
    copies = read_notes([note_ref] + [note_of(b) for b in blocks], notes, sems)
    size = probe_ref.shape[1]
    margin = size // 2
    tile = light_ref.shape[0]
    power_ref[...] = probe_ref[0] * probe_ref[0] + probe_ref[1] * probe_ref[1]
    total[...] = jnp.zeros_like(total)
    lane = lax.broadcasted_iota(jnp.int32, (size, size), 1)

    def add(row, col, ok):
        ok = jnp.logical_and(ok, jnp.logical_and(jnp.abs(row) < tile, jnp.abs(col) < tile))

        @pl.when(ok)
        def _():
            base, shift = aligned(row + tile)
            moved = pltpu.roll(power_ref[...], lax.rem(col + size, size), axis=1)
            keep = jnp.logical_and(lane >= col, lane < col + size)
            total[pl.ds(base, size + 8), :] += rows_down(jnp.where(keep, moved, 0.0), shift)

    places = [((None, None), True)] + list(zip(ways, block_valid(z, x, nz, nx)))
    for copy, note, ((zway, xway), ok) in zip(copies, notes, places):
        copy.wait()
        down = 0 if zway is None else (2 * side_of(z, zway) - 1) * tile
        right = 0 if xway is None else (2 * side_of(x, xway) - 1) * tile
        for j in range(npos):
            row, col = offset_in(note, j)
            add(row + down - margin, col + right - margin, ok)
    light_ref[...] = total[tile : 2 * tile, :]


def call(kernel, out_shape, specs, *operands, scratch=(), vmem=16):
    return pl.pallas_call(
        kernel,
        out_shape=out_shape,
        in_specs=specs,
        out_specs=[VMEM] * len(out_shape),
        scratch_shapes=list(scratch),
        compiler_params=pltpu.CompilerParams(vmem_limit_bytes=vmem * 1024 * 1024),
    )(*operands)


def dma(count):
    return pltpu.SemaphoreType.DMA((count,))


def shards(sizes, specimen, probe_wave, amplitudes, offsets):
    nz, nx, nc = sizes
    size = probe_wave.shape[1]
    margin = size // 2
    tile = specimen.shape[1]
    npos = offsets.shape[0]
    ways = block_ways(nz, nx)
    xways = ways_of(nx)
    targets = block_targets(nz, nx)

    def send(value, target):
        return lax.ppermute(value, GROUP, permutation(sizes, target))

    def to_core(value):
        return lax.ppermute(value, "pos", PART_SWAP)

    shapes = [(tile if v is None else margin, tile if w is None else margin) for v, w in ways]
    *blocks, note = call(
        functools.partial(halo_blocks_kernel, nz, nx),
        [f32(h + NOTE[0], w) for h, w in shapes] + [f32(*NOTE)],
        [HBM, HBM],
        offsets,
        specimen,
        scratch=[pltpu.SMEM(offsets.shape, jnp.int32), dma(len(ways) + 1)],
    )
    recv = [send(block, target) for block, target in zip(blocks, targets)]
    other_note = to_core(note)

    table_a, table_b = (jnp.asarray(t) for t in dft_tables(size))
    late = (specimen, probe_wave, amplitudes, table_a, table_b)
    specimen_v, probe_v, amp_v, ta_v, tb_v = call(
        fetch_kernel,
        [jax.ShapeDtypeStruct(a.shape, a.dtype) for a in late],
        [HBM] * len(late),
        *late,
        scratch=[dma(len(late))],
    )

    give, padded = call(
        functools.partial(other_patches_kernel, nz, nx),
        [f32(npos, size, size), f32(tile + size, tile + size)],
        [VMEM] * (2 + len(recv)),
        other_note,
        specimen_v,
        *recv,
        scratch=[NOTE_SMEM, dma(1)],
    )
    patches_other = to_core(give)
    (patches,) = call(
        own_patches_kernel,
        [f32(npos, size, size)],
        [VMEM, VMEM, ANY],
        note,
        padded,
        give,
        scratch=[NOTE_SMEM, dma(1)],
    )
    own, other = call(
        positions_kernel,
        [f32(npos + 1, size, size)] * 2,
        [VMEM] * 6,
        patches,
        patches_other,
        probe_v,
        amp_v,
        ta_v,
        tb_v,
    )
    terms = to_core(other)

    zbits = [("z", 1 << k) for k in range(nz.bit_length() - 1)]
    xbits = [("x", 1 << k) for k in range(nx.bit_length() - 1)]
    orders = (xbits[:1] + zbits + xbits[1:], zbits + xbits)

    def stage(k):
        def target(z, x, c):
            axis, bit = orders[c][k]
            return (z ^ bit, x, c) if axis == "z" else (z, x ^ bit, c)

        return target

    half = f32(size // 2, size)
    keep, away = call(halve_kernel, [half] * 2, [VMEM] * 2, own, terms)
    (grad,) = call(
        gather_kernel,
        [f32(tile + size, tile + size)],
        [VMEM] * 4 + [ANY],
        note,
        other_note,
        own,
        terms,
        keep,
        scratch=[NOTE_SMEM, NOTE_SMEM, dma(2)],
    )
    keep, middle, *beyond = call(
        functools.partial(cut_step_kernel, nx),
        [half, f32(tile + size, tile)] + [f32(tile + size, margin)] * len(xways),
        [VMEM] * 3,
        keep,
        send(away, stage(0)),
        grad,
    )
    (light,) = call(
        functools.partial(light_kernel, npos, nz, nx),
        [f32(tile, tile)],
        [VMEM, VMEM, ANY] + [VMEM] * len(recv),
        note,
        probe_v,
        keep,
        *recv,
        scratch=[
            pltpu.VMEM((size, size), jnp.float32),
            pltpu.VMEM((3 * tile, size), jnp.float32),
            *[NOTE_SMEM] * (1 + len(recv)),
            dma(1 + len(recv)),
        ],
    )
    beside = [send(piece, targets[ways.index((None, way))]) for piece, way in zip(beyond, xways)]
    keep, center, *edges = call(
        functools.partial(fold_step_kernel, nz, nx),
        [half, f32(tile, tile)] + [f32(margin, tile)] * 2,
        [VMEM, VMEM, ANY, VMEM] + [VMEM] * len(beside),
        keep,
        send(keep, stage(1)),
        light,
        middle,
        *beside,
        scratch=[pltpu.VMEM((tile + size, tile), jnp.float32)],
    )
    arrived = [send(edge, targets[ways.index((way, None))]) for way, edge in enumerate(edges)]
    keep, part = call(
        functools.partial(update_step_kernel, nz),
        [half, f32(tile, tile)],
        [VMEM] * (6 + len(arrived)),
        keep,
        send(keep, stage(2)),
        specimen_v,
        center,
        light,
        to_core(light),
        *arrived,
        scratch=[pltpu.VMEM((tile, tile), jnp.float32)],
    )
    for k in range(3, len(orders[0])):
        (keep,) = call(add_kernel, [half], [VMEM] * 2, keep, send(keep, stage(k)))
    away = send(keep, stage(0))
    (new_specimen,) = call(specimen_kernel, [f32(2, tile, tile)], [VMEM] * 2, part, to_core(part))
    step_size = 1.0 / math.sqrt(npos * nz * nx * nc)
    (new_probe,) = call(
        functools.partial(probe_kernel, step_size),
        [f32(2, size, size)],
        [VMEM] * 5,
        probe_v,
        keep,
        away,
        to_core(keep),
        to_core(away),
    )
    return (new_specimen, new_probe)


def solution(mesh):
    sizes = tuple(mesh.shape[a] for a in GROUP)
    placed = (
        P(None, ("groups", "scanx"), "scany"),
        P(None, "groups", None),
        P(("groups", "scanx", "scany", "pos"), None, None),
        P(("groups", "scanx", "scany", "pos"), None),
    )
    return jax.shard_map(
        functools.partial(shards, sizes),
        mesh=mesh,
        in_specs=placed,
        out_specs=(P(None, ("groups", "scanx"), "scany"), P(None, "groups", None)),
        check_vma=False,
    )
```

```python
import functools
import math

import jax
import jax.numpy as jnp
import numpy as np
from jax import lax
from jax.experimental import pallas as pl
from jax.experimental.pallas import tpu as pltpu
from jax.sharding import PartitionSpec as P

GROUP = ("scanx", "scany", "pos")
KEEP_IN_HBM = 64 * 1024 * 1024 - 448 * 1024
PART_SWAP = ((0, 1), (1, 0))
VMEM = pl.BlockSpec(memory_space=pltpu.VMEM)
ANY = pl.BlockSpec(memory_space=pl.ANY)
HBM = pl.BlockSpec(memory_space=pltpu.HBM)
NOTE = (8, 128)
NOTE_SMEM = pltpu.SMEM(NOTE, jnp.float32)


def f32(*shape):
    return jax.ShapeDtypeStruct(shape, jnp.float32)


def ways_of(count):
    return (0,) if count == 2 else (0, 1)


def side_of(index, way):
    return lax.rem(index + way + 1, 2)


def valid_of(index, way, count):
    neighbour = index + 2 * side_of(index, way) - 1
    return jnp.logical_and(neighbour >= 0, neighbour < count)


def block_ways(nz, nx):
    xways, zways = ways_of(nx), (0, 1)
    order = [(None, w) for w in xways] + [(w, None) for w in zways]
    return order + [(v, w) for w in xways for v in zways]


def block_places(z, x, nz, nx, origin, extent, margin):
    places = []
    for zway, xway in block_ways(nz, nx):
        span = []
        for index, way in ((z, zway), (x, xway)):
            if way is None:
                span.append(pl.ds(origin, 2 * margin))
            else:
                span.append(pl.ds(pl.multiple_of(side_of(index, way) * extent, margin), margin))
        places.append(tuple(span))
    return places


def block_shapes(nz, nx, tile):
    return [tuple(tile if way is None else tile // 2 for way in ways) for ways in block_ways(nz, nx)]


def packed_places(shapes):
    lanes = min(width for _, width in shapes)
    at, places = 0, []
    for height, width in shapes:
        places.append([])
        for col in range(0, width, lanes):
            places[-1].append((at, col, height))
            at += height
    return places


def block_valid(z, x, nz, nx):
    result = []
    for zway, xway in block_ways(nz, nx):
        ok = True
        if zway is not None:
            ok = valid_of(z, zway, nz)
        if xway is not None:
            ok = jnp.logical_and(ok, valid_of(x, xway, nx))
        result.append(ok)
    return result


def block_targets(nz, nx):
    def step(index, way, count):
        if way is None:
            return index
        to = index + (1 if (index + way) % 2 == 0 else -1)
        return to if 0 <= to < count else None

    def target(ways, z, x, c):
        tz, tx = step(z, ways[0], nz), step(x, ways[1], nx)
        return (z, x, 1 - c) if tz is None or tx is None else (tz, tx, c)

    return [functools.partial(target, ways) for ways in block_ways(nz, nx)]


def permutation(sizes, target):
    nz, nx, nc = sizes
    pairs = []
    for z in range(nz):
        for x in range(nx):
            for c in range(nc):
                tz, tx, tc = target(z, x, c)
                pairs.append(((z * nx + x) * nc + c, (tz * nx + tx) * nc + tc))
    return pairs


def dft_waves(length):
    index = np.arange(length, dtype=np.int32)
    phase = (index[:, None] * index[None, :]) % length
    angle = phase.astype(np.float32) * np.float32(2.0 * math.pi / length)
    scale = np.float32(1.0 / math.sqrt(length))
    sine = np.sin(angle) * scale
    return np.stack([np.cos(angle) * scale, sine, -sine]).astype(jnp.bfloat16)


def aligned(row):
    return pl.multiple_of((row // 8) * 8, 8), lax.rem(row, 8)


def rows_up(block, shift):
    count, width = block.shape
    groups = pltpu.roll(block.reshape(count // 8, 8, width), lax.rem(8 - shift, 8), axis=1)
    at = lax.broadcasted_iota(jnp.int32, (count // 8 - 1, 8, width), 1)
    return jnp.where(at < 8 - shift, groups[:-1], groups[1:]).reshape(count - 8, width)


def rows_down(block, shift):
    count, width = block.shape
    groups = pltpu.roll(block.reshape(count // 8, 8, width), shift, axis=1)
    blank = jnp.zeros((1, 8, width), block.dtype)
    at = lax.broadcasted_iota(jnp.int32, (count // 8 + 1, 8, width), 1)
    early = jnp.concatenate([groups, blank])
    late = jnp.concatenate([blank, groups])
    return jnp.where(at >= shift, early, late).reshape(count + 8, width)


def halo_blocks_kernel(nz, nx, off_hbm, spec_ref, *refs):
    z, x, c = (lax.axis_index(a) for a in GROUP)
    *outs, note_ref, off_ref, sems = refs
    tile = spec_ref.shape[1]
    margin = tile // 2
    off_copy = pltpu.make_async_copy(off_hbm, off_ref, sems.at[len(outs)])
    off_copy.start()
    copies = []
    places = block_places(z, x, nz, nx, 0, margin, margin)
    for k, (out, (height, _), (rows, cols)) in enumerate(zip(outs, block_shapes(nz, nx, tile), places)):
        copies.append(pltpu.make_async_copy(spec_ref.at[c, rows, cols], out.at[pl.ds(0, height), :], sems.at[k]))
        copies[-1].start()
    off_copy.wait()
    lane = lax.broadcasted_iota(jnp.int32, NOTE, 1)
    note = jnp.zeros(NOTE, jnp.float32)
    for j in range(off_ref.shape[0]):
        for k in range(2):
            note = jnp.where(lane == 2 * j + k, off_ref[j, k].astype(jnp.float32), note)
    note_ref[...] = note
    for out in outs:
        out[out.shape[0] - NOTE[0] :, : NOTE[1]] = note
    for copy in copies:
        copy.wait()


def read_notes(notes, smems, sems):
    copies = [pltpu.make_async_copy(note, smem, sems.at[k]) for k, (note, smem) in enumerate(zip(notes, smems))]
    for copy in copies:
        copy.start()
    return copies


def note_of(block):
    return block.at[pl.ds(block.shape[0] - NOTE[0], NOTE[0]), pl.ds(0, NOTE[1])]


def offset_in(note, j):
    return note[0, 2 * j].astype(jnp.int32), note[0, 2 * j + 1].astype(jnp.int32)


def fetch_kernel(*refs):
    *refs, table_a, table_b, sems = refs
    count = len(refs) // 2
    *sources, waves = refs[: count + 1]
    copies = [pltpu.make_async_copy(src, refs[count + 1 + k], sems.at[k]) for k, src in enumerate(sources)]
    for copy in copies:
        copy.start()
    cosine, sine, minus = (waves[k] for k in range(3))
    size = cosine.shape[0]
    for table, blocks in ((table_a, (cosine, sine, minus, cosine)), (table_b, (cosine, minus, sine, cosine))):
        for k, block in enumerate(blocks):
            at, left = k // 2 * size, k % 2 * size
            table[at : at + size, left : left + size] = block
    for copy in copies:
        copy.wait()


def cut_patches(note, padded, out):
    npos, size, _ = out.shape
    lane = lax.broadcasted_iota(jnp.int32, (size + 8, size), 1)
    for j in range(npos):
        row, col = offset_in(note, j)
        base, shift = aligned(row)
        rows = padded[pl.ds(base, size + 8), :]
        mixed = rows_up(jnp.where(lane >= col, rows[:, :size], rows[:, size:]), shift)
        out[j] = pltpu.roll(mixed, lax.rem(size - col, size), axis=1)


def patches_kernel(nz, nx, ours, note_ref, unused_ref, spec_ref, *refs):
    z, x, c = (lax.axis_index(a) for a in GROUP)
    *blocks, out, padded, note, sems = refs
    copies = read_notes([note_ref], [note], sems)
    tile = spec_ref.shape[1]
    margin = (padded.shape[0] - tile) // 2
    padded[margin : margin + tile, margin : margin + tile] = spec_ref[c if ours else 1 - c]
    if len(ways_of(nx)) == 1:
        far_cols = pl.ds(pl.multiple_of((1 - side_of(x, 0)) * (margin + tile), margin), margin)
        padded[:, far_cols] = jnp.zeros((padded.shape[0], margin), jnp.float32)
    places = block_places(z, x, nz, nx, margin, margin + tile, margin)
    shapes = block_shapes(nz, nx, tile)
    pieces = packed_places(shapes)
    for k, ((height, width), (rows, cols), ok) in enumerate(zip(shapes, places, block_valid(z, x, nz, nx))):

        @pl.when(ok)
        def _():
            if ours:
                padded[rows, cols] = blocks[k][:height, :]
            else:
                parts = [blocks[0][at : at + height, :] for at, _, _ in pieces[k]]
                padded[rows, cols] = parts[0] if len(parts) == 1 else jnp.concatenate(parts, axis=1)

        @pl.when(jnp.logical_not(ok))
        def _():
            padded[rows, cols] = jnp.zeros((height, width), jnp.float32)

    copies[0].wait()
    cut_patches(note, padded, out)


def pack_kernel(nz, nx, tile, unused_ref, *refs):
    *blocks, out = refs
    for block, pieces in zip(blocks, packed_places(block_shapes(nz, nx, tile))):
        for at, col, height in pieces:
            out[at : at + height, :] = block[:height, col : col + out.shape[1]]


def positions_kernel(patch_ref, patch_other_ref, probe_ref, amp_ref, ta_ref, tb_ref, own_ref, other_ref, probe_own_ref, probe_other_ref):
    first = lax.axis_index("pos") == 0
    npos, size, _ = patch_ref.shape
    table_a = ta_ref[...]
    table_b = tb_ref[...]
    probe_real = probe_ref[0]
    probe_imag = probe_ref[1]

    def side_by_side(both):
        return jnp.concatenate([both[:size], both[size:]], axis=1)

    grad_real = jnp.zeros((size, size), jnp.float32)
    grad_imag = jnp.zeros((size, size), jnp.float32)
    for j in range(npos):
        patch_real = jnp.where(first, patch_ref[j], patch_other_ref[j])
        patch_imag = jnp.where(first, patch_other_ref[j], patch_ref[j])
        exit_real = probe_real * patch_real - probe_imag * patch_imag
        exit_imag = probe_real * patch_imag + probe_imag * patch_real
        wave = jnp.concatenate([exit_real, exit_imag], axis=0).astype(jnp.bfloat16)
        half = jnp.dot(table_a, wave, preferred_element_type=jnp.float32).astype(jnp.bfloat16)
        far = jnp.dot(side_by_side(half), table_b, preferred_element_type=jnp.float32)
        far_real, far_imag = far[:, :size], far[:, size:]
        power = far_real * far_real + far_imag * far_imag
        ratio = amp_ref[j].astype(jnp.float32) * jnp.minimum(lax.rsqrt(power), 1.0 / 0.2)
        projected = jnp.concatenate([far_real * ratio, far_imag * ratio], axis=0).astype(jnp.bfloat16)
        back_half = jnp.dot(table_b, projected, preferred_element_type=jnp.float32).astype(jnp.bfloat16)
        back = jnp.dot(side_by_side(back_half), table_a, preferred_element_type=jnp.float32)
        diff_real = back[:, :size] - exit_real
        diff_imag = back[:, size:] - exit_imag
        term_real = probe_real * diff_real + probe_imag * diff_imag
        term_imag = probe_real * diff_imag - probe_imag * diff_real
        own_ref[j] = jnp.where(first, term_real, term_imag)
        other_ref[j] = jnp.where(first, term_imag, term_real)
        grad_real += patch_real * diff_real + patch_imag * diff_imag
        grad_imag += patch_real * diff_imag - patch_imag * diff_real
    probe_own_ref[...] = jnp.where(first, grad_real, grad_imag)
    probe_other_ref[...] = jnp.where(first, grad_imag, grad_real)


def half_of(z, x, c):
    return jnp.where(c == 0, lax.rem(x, 2), lax.rem(z, 2))


def halve_kernel(own_ref, recv_ref, keep_ref, give_ref):
    half = half_of(*(lax.axis_index(a) for a in GROUP))
    rows = keep_ref.shape[0]
    for at, out in ((half, keep_ref), (1 - half, give_ref)):
        span = pl.ds(pl.multiple_of(at * rows, rows), rows)
        out[...] = own_ref[span, :] + recv_ref[span, :]


def gather_kernel(note_ref, other_note_ref, own_ref, recv_ref, unused_ref, grad, note, other_note, sems):
    copies = read_notes([note_ref, other_note_ref], [note, other_note], sems)
    npos, size, _ = own_ref.shape
    lane = lax.broadcasted_iota(jnp.int32, (size + 8, size), 1)
    grad[...] = jnp.zeros_like(grad)
    for copy, offs, terms in zip(copies, (note, other_note), (own_ref, recv_ref)):
        copy.wait()
        for j in range(npos):
            row, col = offset_in(offs, j)
            base, shift = aligned(row)
            term = rows_down(pltpu.roll(terms[j], col, axis=1), shift)
            low = jnp.where(lane >= col, term, 0.0)
            rows = pl.ds(base, size + 8)
            grad[rows, :size] += low
            grad[rows, size:] += term - low


def cut_step_kernel(nx, keep_ref, recv_ref, grad_ref, out_ref, middle_ref, *blocks):
    x = lax.axis_index("scany")
    out_ref[...] = keep_ref[...] + recv_ref[...]
    tile = middle_ref.shape[1]
    margin = (middle_ref.shape[0] - tile) // 2
    middle_ref[...] = grad_ref[:, margin : margin + tile]
    for block, way in zip(blocks, ways_of(nx)):
        block[...] = grad_ref[:, pl.ds(pl.multiple_of(side_of(x, way) * (margin + tile), margin), margin)]


def fold_kernel(nz, nx, middle_ref, *refs):
    z, x = lax.axis_index("scanx"), lax.axis_index("scany")
    ways = ways_of(nx)
    blocks, (center_ref, *edges, total) = refs[: len(ways)], refs[len(ways) :]
    tile = center_ref.shape[0]
    margin = (middle_ref.shape[0] - tile) // 2
    total[...] = middle_ref[...]
    for block, way in zip(blocks, ways):
        at = pl.multiple_of(side_of(x, way) * (tile - margin), margin)

        @pl.when(valid_of(x, way, nx))
        def _():
            total[:, pl.ds(at, margin)] += block[...]

    center_ref[...] = total[margin : margin + tile, :]
    for way, edge in enumerate(edges):
        edge[...] = total[pl.ds(pl.multiple_of(side_of(z, way) * (margin + tile), margin), margin), :]


def update_kernel(nz, spec_ref, center_ref, light_ref, other_light_ref, edge_a, edge_b, *refs):
    z, c = lax.axis_index("scanx"), lax.axis_index("pos")
    part_ref, grad = refs
    tile = center_ref.shape[0]
    grad[...] = center_ref[...]
    for way, edge in enumerate((edge_a, edge_b)):
        margin = edge.shape[0]
        at = pl.multiple_of(side_of(z, way) * (tile - margin), margin)

        @pl.when(valid_of(z, way, nz))
        def _():
            grad[pl.ds(at, margin), :] += edge[...]

    part_ref[...] = spec_ref[c] + grad[...] / (light_ref[...] + other_light_ref[...] + 1.0)


def add_kernel(a_ref, b_ref, *refs):
    refs[-1][...] = a_ref[...] + b_ref[...]


def specimen_kernel(part_ref, part_other_ref, out_ref):
    c = lax.axis_index("pos")
    out_ref[c] = part_ref[...]
    out_ref[1 - c] = part_other_ref[...]


def probe_kernel(step_size, probe_ref, keep_ref, away_ref, keep_other_ref, away_other_ref, out_ref):
    z, x, c = (lax.axis_index(a) for a in GROUP)
    rows = keep_ref.shape[0]
    for part, keep, away in ((c, keep_ref, away_ref), (1 - c, keep_other_ref, away_other_ref)):
        half = half_of(z, x, part)
        for at, term in ((half, keep), (1 - half, away)):
            span = pl.ds(pl.multiple_of(at * rows, rows), rows)
            out_ref[part, span, :] = probe_ref[part, span, :] + term[...] * step_size


def light_kernel(npos, nz, nx, note_ref, probe_ref, unused_ref, *refs):
    z, x, c = (lax.axis_index(a) for a in GROUP)
    ways = block_ways(nz, nx)
    blocks, (light_ref, power_ref, total, *notes, sems) = refs[: len(ways)], refs[len(ways) :]
    copies = read_notes([note_ref] + [note_of(b) for b in blocks], notes, sems)
    size = probe_ref.shape[1]
    margin = size // 2
    tile = light_ref.shape[0]
    power_ref[...] = probe_ref[0] * probe_ref[0] + probe_ref[1] * probe_ref[1]
    total[...] = jnp.zeros_like(total)
    lane = lax.broadcasted_iota(jnp.int32, (size, size), 1)

    def add(row, col, ok):
        ok = jnp.logical_and(ok, jnp.logical_and(jnp.abs(row) < tile, jnp.abs(col) < tile))

        @pl.when(ok)
        def _():
            base, shift = aligned(row + tile)
            moved = pltpu.roll(power_ref[...], lax.rem(col + size, size), axis=1)
            keep = jnp.logical_and(lane >= col, lane < col + size)
            total[pl.ds(base, size + 8), :] += rows_down(jnp.where(keep, moved, 0.0), shift)

    places = [((None, None), True)] + list(zip(ways, block_valid(z, x, nz, nx)))
    for copy, note, ((zway, xway), ok) in zip(copies, notes, places):
        copy.wait()
        down = 0 if zway is None else (2 * side_of(z, zway) - 1) * tile
        right = 0 if xway is None else (2 * side_of(x, xway) - 1) * tile
        for j in range(npos):
            row, col = offset_in(note, j)
            add(row + down - margin, col + right - margin, ok)
    light_ref[...] = total[tile : 2 * tile, :]


def call(kernel, out_shape, specs, *operands, scratch=(), outs=VMEM, vmem=16 * 1024 * 1024):
    return pl.pallas_call(
        kernel,
        out_shape=out_shape,
        in_specs=specs,
        out_specs=[outs] * len(out_shape),
        scratch_shapes=list(scratch),
        compiler_params=pltpu.CompilerParams(vmem_limit_bytes=vmem),
    )(*operands)


def dma(count):
    return pltpu.SemaphoreType.DMA((count,))


def shards(sizes, specimen, probe_wave, amplitudes, offsets):
    nz, nx, nc = sizes
    size = probe_wave.shape[1]
    margin = size // 2
    tile = specimen.shape[1]
    npos = offsets.shape[0]
    ways = block_ways(nz, nx)
    xways = ways_of(nx)
    targets = block_targets(nz, nx)

    def send(value, target):
        return lax.ppermute(value, GROUP, permutation(sizes, target))

    def to_core(value):
        return lax.ppermute(value, "pos", PART_SWAP)

    shapes = block_shapes(nz, nx, tile)
    *blocks, note = call(
        functools.partial(halo_blocks_kernel, nz, nx),
        [f32(h + NOTE[0], w) for h, w in shapes] + [f32(*NOTE)],
        [HBM, HBM],
        offsets,
        specimen,
        scratch=[pltpu.SMEM(offsets.shape, jnp.int32), dma(len(ways) + 1)],
        vmem=KEEP_IN_HBM,
    )
    recv = [send(block, target) for block, target in zip(blocks, targets)]

    waves = jnp.asarray(dft_waves(size))
    late = (specimen, probe_wave, amplitudes)
    specimen_v, probe_v, amp_v, ta_v, tb_v = call(
        fetch_kernel,
        [jax.ShapeDtypeStruct(a.shape, a.dtype) for a in late]
        + [jax.ShapeDtypeStruct((2 * size, 2 * size), jnp.bfloat16)] * 2,
        [ANY] * len(late) + [VMEM],
        *late,
        waves,
        scratch=[dma(len(late))],
    )
    lanes = min(w for _, w in shapes)
    (packed,) = call(
        functools.partial(pack_kernel, nz, nx, tile),
        [f32(sum(h * w for h, w in shapes) // lanes, lanes)],
        [ANY] + [VMEM] * len(recv),
        probe_v,
        *recv,
    )

    def patches_from(ours, after, *arrays):
        return call(
            functools.partial(patches_kernel, nz, nx, ours),
            [f32(npos, size, size)],
            [VMEM, ANY] + [VMEM] * (1 + len(arrays)),
            note,
            after,
            specimen_v,
            *arrays,
            scratch=[pltpu.VMEM((tile + size, tile + size), jnp.float32), NOTE_SMEM, dma(1)],
        )[0]

    patches = patches_from(True, packed, *recv)
    patches_other = patches_from(False, patches, to_core(packed))
    own, other, probe_own, probe_other = call(
        positions_kernel,
        [f32(npos, size, size)] * 2 + [f32(size, size)] * 2,
        [VMEM] * 6,
        patches,
        patches_other,
        probe_v,
        amp_v,
        ta_v,
        tb_v,
    )
    terms = to_core(other)
    other_note = to_core(note)

    zbits = [("z", 1 << k) for k in range(nz.bit_length() - 1)]
    xbits = [("x", 1 << k) for k in range(nx.bit_length() - 1)]
    orders = (xbits[:1] + zbits + xbits[1:], zbits + xbits)

    def stage(k):
        def target(z, x, c):
            axis, bit = orders[c][k]
            return (z ^ bit, x, c) if axis == "z" else (z, x ^ bit, c)

        return target

    half = f32(size // 2, size)
    keep, away = call(halve_kernel, [half] * 2, [VMEM] * 2, probe_own, to_core(probe_other))
    (grad,) = call(
        gather_kernel,
        [f32(tile + size, tile + size)],
        [VMEM] * 4 + [ANY],
        note,
        other_note,
        own,
        terms,
        keep,
        scratch=[NOTE_SMEM, NOTE_SMEM, dma(2)],
    )
    keep, middle, *beyond = call(
        functools.partial(cut_step_kernel, nx),
        [half, f32(tile + size, tile)] + [f32(tile + size, margin)] * len(xways),
        [VMEM] * 3,
        keep,
        send(away, stage(0)),
        grad,
    )
    (light,) = call(
        functools.partial(light_kernel, npos, nz, nx),
        [f32(tile, tile)],
        [VMEM, VMEM, ANY] + [VMEM] * len(recv),
        note,
        probe_v,
        keep,
        *recv,
        scratch=[
            pltpu.VMEM((size, size), jnp.float32),
            pltpu.VMEM((3 * tile, size), jnp.float32),
            *[NOTE_SMEM] * (1 + len(recv)),
            dma(1 + len(recv)),
        ],
    )
    beside = [send(piece, targets[ways.index((None, way))]) for piece, way in zip(beyond, xways)]
    (keep,) = call(add_kernel, [half], [VMEM, VMEM, ANY], keep, send(keep, stage(1)), light)
    center, *edges = call(
        functools.partial(fold_kernel, nz, nx),
        [f32(tile, tile)] + [f32(margin, tile)] * 2,
        [VMEM] * (1 + len(beside)),
        middle,
        *beside,
        scratch=[pltpu.VMEM((tile + size, tile), jnp.float32)],
    )
    arrived = [send(edge, targets[ways.index((way, None))]) for way, edge in enumerate(edges)]
    (part,) = call(
        functools.partial(update_kernel, nz),
        [f32(tile, tile)],
        [VMEM] * (4 + len(arrived)),
        specimen_v,
        center,
        light,
        to_core(light),
        *arrived,
        scratch=[pltpu.VMEM((tile, tile), jnp.float32)],
    )
    for k in range(2, len(orders[0])):
        (keep,) = call(add_kernel, [half], [VMEM] * 2, keep, send(keep, stage(k)))
    away = send(keep, stage(0))
    (new_specimen,) = call(specimen_kernel, [f32(2, tile, tile)], [VMEM] * 2, part, to_core(part))
    step_size = 1.0 / math.sqrt(npos * nz * nx * nc)
    (new_probe,) = call(
        functools.partial(probe_kernel, step_size),
        [f32(2, size, size)],
        [VMEM] * 5,
        probe_v,
        keep,
        away,
        to_core(keep),
        to_core(away),
    )
    return (new_specimen, new_probe)


def solution(mesh):
    sizes = tuple(mesh.shape[a] for a in GROUP)
    placed = (
        P(None, ("groups", "scanx"), "scany"),
        P(None, "groups", None),
        P(("groups", "scanx", "scany", "pos"), None, None),
        P(("groups", "scanx", "scany", "pos"), None),
    )
    return jax.shard_map(
        functools.partial(shards, sizes),
        mesh=mesh,
        in_specs=placed,
        out_specs=(P(None, ("groups", "scanx"), "scany"), P(None, "groups", None)),
        check_vma=False,
    )
```

```python
import functools
import math

import jax
import jax.numpy as jnp
import numpy as np
from jax import lax
from jax.experimental import pallas as pl
from jax.experimental.pallas import tpu as pltpu
from jax.sharding import PartitionSpec as P

GROUP = ("scanx", "scany", "pos")
KEEP_IN_HBM = 64 * 1024 * 1024 - 448 * 1024
PART_SWAP = ((0, 1), (1, 0))
VMEM = pl.BlockSpec(memory_space=pltpu.VMEM)
ANY = pl.BlockSpec(memory_space=pl.ANY)
HBM = pl.BlockSpec(memory_space=pltpu.HBM)
NOTE = (8, 128)
NOTE_SMEM = pltpu.SMEM(NOTE, jnp.float32)


def f32(*shape):
    return jax.ShapeDtypeStruct(shape, jnp.float32)


def ways_of(count):
    return (0,) if count == 2 else (0, 1)


def side_of(index, way):
    return lax.rem(index + way + 1, 2)


def valid_of(index, way, count):
    neighbour = index + 2 * side_of(index, way) - 1
    return jnp.logical_and(neighbour >= 0, neighbour < count)


def block_ways(nz, nx):
    xways, zways = ways_of(nx), (0, 1)
    order = [(None, w) for w in xways] + [(w, None) for w in zways]
    return order + [(v, w) for w in xways for v in zways]


def block_places(z, x, nz, nx, origin, extent, margin):
    places = []
    for zway, xway in block_ways(nz, nx):
        span = []
        for index, way in ((z, zway), (x, xway)):
            if way is None:
                span.append(pl.ds(origin, 2 * margin))
            else:
                span.append(pl.ds(pl.multiple_of(side_of(index, way) * extent, margin), margin))
        places.append(tuple(span))
    return places


def block_shapes(nz, nx, tile):
    return [tuple(tile if way is None else tile // 2 for way in ways) for ways in block_ways(nz, nx)]


def packed_places(shapes):
    lanes = min(width for _, width in shapes)
    at, places = 0, []
    for height, width in shapes:
        places.append([])
        for col in range(0, width, lanes):
            places[-1].append((at, col, height))
            at += height
    return places


def block_valid(z, x, nz, nx):
    result = []
    for zway, xway in block_ways(nz, nx):
        ok = True
        if zway is not None:
            ok = valid_of(z, zway, nz)
        if xway is not None:
            ok = jnp.logical_and(ok, valid_of(x, xway, nx))
        result.append(ok)
    return result


def block_targets(nz, nx):
    def step(index, way, count):
        if way is None:
            return index
        to = index + (1 if (index + way) % 2 == 0 else -1)
        return to if 0 <= to < count else None

    def target(ways, z, x, c):
        tz, tx = step(z, ways[0], nz), step(x, ways[1], nx)
        return (z, x, 1 - c) if tz is None or tx is None else (tz, tx, c)

    return [functools.partial(target, ways) for ways in block_ways(nz, nx)]


def permutation(sizes, target):
    nz, nx, nc = sizes
    pairs = []
    for z in range(nz):
        for x in range(nx):
            for c in range(nc):
                tz, tx, tc = target(z, x, c)
                pairs.append(((z * nx + x) * nc + c, (tz * nx + tx) * nc + tc))
    return pairs


def dft_waves(length):
    index = np.arange(length, dtype=np.int32)
    phase = (index[:, None] * index[None, :]) % length
    angle = phase.astype(np.float32) * np.float32(2.0 * math.pi / length)
    scale = np.float32(1.0 / math.sqrt(length))
    sine = np.sin(angle) * scale
    return np.stack([np.cos(angle) * scale, sine, -sine]).astype(jnp.bfloat16)


def aligned(row):
    return pl.multiple_of((row // 8) * 8, 8), lax.rem(row, 8)


def rows_up(block, shift):
    count, width = block.shape
    groups = pltpu.roll(block.reshape(count // 8, 8, width), lax.rem(8 - shift, 8), axis=1)
    at = lax.broadcasted_iota(jnp.int32, (count // 8 - 1, 8, width), 1)
    return jnp.where(at < 8 - shift, groups[:-1], groups[1:]).reshape(count - 8, width)


def rows_down(block, shift):
    count, width = block.shape
    groups = pltpu.roll(block.reshape(count // 8, 8, width), shift, axis=1)
    blank = jnp.zeros((1, 8, width), block.dtype)
    at = lax.broadcasted_iota(jnp.int32, (count // 8 + 1, 8, width), 1)
    early = jnp.concatenate([groups, blank])
    late = jnp.concatenate([blank, groups])
    return jnp.where(at >= shift, early, late).reshape(count + 8, width)


def halo_blocks_kernel(nz, nx, off_hbm, spec_ref, *refs):
    z, x, c = (lax.axis_index(a) for a in GROUP)
    *outs, note_ref, off_ref, sems = refs
    tile = spec_ref.shape[1]
    margin = tile // 2
    off_copy = pltpu.make_async_copy(off_hbm, off_ref, sems.at[len(outs)])
    off_copy.start()
    copies = []
    places = block_places(z, x, nz, nx, 0, margin, margin)
    for k, (out, (height, _), (rows, cols)) in enumerate(zip(outs, block_shapes(nz, nx, tile), places)):
        copies.append(pltpu.make_async_copy(spec_ref.at[c, rows, cols], out.at[pl.ds(0, height), :], sems.at[k]))
        copies[-1].start()
    off_copy.wait()
    lane = lax.broadcasted_iota(jnp.int32, NOTE, 1)
    note = jnp.zeros(NOTE, jnp.float32)
    for j in range(off_ref.shape[0]):
        for k in range(2):
            note = jnp.where(lane == 2 * j + k, off_ref[j, k].astype(jnp.float32), note)
    note_ref[...] = note
    for out in outs:
        out[out.shape[0] - NOTE[0] :, : NOTE[1]] = note
    for copy in copies:
        copy.wait()


def read_notes(notes, smems, sems):
    copies = [pltpu.make_async_copy(note, smem, sems.at[k]) for k, (note, smem) in enumerate(zip(notes, smems))]
    for copy in copies:
        copy.start()
    return copies


def note_of(block):
    return block.at[pl.ds(block.shape[0] - NOTE[0], NOTE[0]), pl.ds(0, NOTE[1])]


def offset_in(note, j):
    return note[0, 2 * j].astype(jnp.int32), note[0, 2 * j + 1].astype(jnp.int32)


def fetch_kernel(*refs):
    *refs, table_a, table_b, sems = refs
    count = len(refs) // 2
    *sources, waves = refs[: count + 1]
    copies = [pltpu.make_async_copy(src, refs[count + 1 + k], sems.at[k]) for k, src in enumerate(sources)]
    for copy in copies:
        copy.start()
    cosine, sine, minus = (waves[k] for k in range(3))
    size = cosine.shape[0]
    for table, blocks in ((table_a, (cosine, sine, minus, cosine)), (table_b, (cosine, minus, sine, cosine))):
        for k, block in enumerate(blocks):
            at, left = k // 2 * size, k % 2 * size
            table[at : at + size, left : left + size] = block
    for copy in copies:
        copy.wait()


def cut_patches(note, padded, out):
    npos, size, _ = out.shape
    lane = lax.broadcasted_iota(jnp.int32, (size + 8, size), 1)
    for j in range(npos):
        row, col = offset_in(note, j)
        base, shift = aligned(row)
        rows = padded[pl.ds(base, size + 8), :]
        mixed = rows_up(jnp.where(lane >= col, rows[:, :size], rows[:, size:]), shift)
        out[j] = pltpu.roll(mixed, lax.rem(size - col, size), axis=1)


def patches_kernel(nz, nx, ours, note_ref, unused_ref, spec_ref, *refs):
    z, x, c = (lax.axis_index(a) for a in GROUP)
    *blocks, out, padded, note, sems = refs
    copies = read_notes([note_ref], [note], sems)
    tile = spec_ref.shape[1]
    margin = (padded.shape[0] - tile) // 2
    padded[margin : margin + tile, margin : margin + tile] = spec_ref[c if ours else 1 - c]
    if len(ways_of(nx)) == 1:
        far_cols = pl.ds(pl.multiple_of((1 - side_of(x, 0)) * (margin + tile), margin), margin)
        padded[:, far_cols] = jnp.zeros((padded.shape[0], margin), jnp.float32)
    places = block_places(z, x, nz, nx, margin, margin + tile, margin)
    shapes = block_shapes(nz, nx, tile)
    pieces = packed_places(shapes)
    for k, ((height, width), (rows, cols), ok) in enumerate(zip(shapes, places, block_valid(z, x, nz, nx))):

        @pl.when(ok)
        def _():
            if ours:
                padded[rows, cols] = blocks[k][:height, :]
            else:
                parts = [blocks[0][at : at + height, :] for at, _, _ in pieces[k]]
                padded[rows, cols] = parts[0] if len(parts) == 1 else jnp.concatenate(parts, axis=1)

        @pl.when(jnp.logical_not(ok))
        def _():
            padded[rows, cols] = jnp.zeros((height, width), jnp.float32)

    copies[0].wait()
    cut_patches(note, padded, out)


def pack_kernel(nz, nx, tile, unused_ref, *refs):
    *blocks, out = refs
    for block, pieces in zip(blocks, packed_places(block_shapes(nz, nx, tile))):
        for at, col, height in pieces:
            out[at : at + height, :] = block[:height, col : col + out.shape[1]]


def positions_kernel(patch_ref, patch_other_ref, probe_ref, amp_ref, ta_ref, tb_ref, own_ref, other_ref, probe_own_ref, probe_other_ref):
    first = lax.axis_index("pos") == 0
    npos, size, _ = patch_ref.shape
    table_a = ta_ref[...]
    table_b = tb_ref[...]
    probe_real = probe_ref[0]
    probe_imag = probe_ref[1]

    def side_by_side(both):
        return jnp.concatenate([both[:size], both[size:]], axis=1)

    grad_real = jnp.zeros((size, size), jnp.float32)
    grad_imag = jnp.zeros((size, size), jnp.float32)
    for j in range(npos):
        patch_real = jnp.where(first, patch_ref[j], patch_other_ref[j])
        patch_imag = jnp.where(first, patch_other_ref[j], patch_ref[j])
        exit_real = probe_real * patch_real - probe_imag * patch_imag
        exit_imag = probe_real * patch_imag + probe_imag * patch_real
        wave = jnp.concatenate([exit_real, exit_imag], axis=0).astype(jnp.bfloat16)
        half = jnp.dot(table_a, wave, preferred_element_type=jnp.float32).astype(jnp.bfloat16)
        far = jnp.dot(side_by_side(half), table_b, preferred_element_type=jnp.float32)
        far_real, far_imag = far[:, :size], far[:, size:]
        power = far_real * far_real + far_imag * far_imag
        ratio = amp_ref[j].astype(jnp.float32) * jnp.minimum(lax.rsqrt(power), 1.0 / 0.2)
        projected = jnp.concatenate([far_real * ratio, far_imag * ratio], axis=0).astype(jnp.bfloat16)
        back_half = jnp.dot(table_b, projected, preferred_element_type=jnp.float32).astype(jnp.bfloat16)
        back = jnp.dot(side_by_side(back_half), table_a, preferred_element_type=jnp.float32)
        diff_real = back[:, :size] - exit_real
        diff_imag = back[:, size:] - exit_imag
        term_real = probe_real * diff_real + probe_imag * diff_imag
        term_imag = probe_real * diff_imag - probe_imag * diff_real
        own_ref[j] = jnp.where(first, term_real, term_imag)
        other_ref[j] = jnp.where(first, term_imag, term_real)
        grad_real += patch_real * diff_real + patch_imag * diff_imag
        grad_imag += patch_real * diff_imag - patch_imag * diff_real
    probe_own_ref[...] = jnp.where(first, grad_real, grad_imag)
    probe_other_ref[...] = jnp.where(first, grad_imag, grad_real)


def half_of(z, x, c):
    return jnp.where(c == 0, lax.rem(x, 2), lax.rem(z, 2))


def halve_kernel(own_ref, recv_ref, unused_ref, unused_light_ref, keep_ref, give_ref, handed_on_ref):
    half = half_of(*(lax.axis_index(a) for a in GROUP))
    rows = keep_ref.shape[0]
    for at, out in ((half, keep_ref), (1 - half, give_ref)):
        span = pl.ds(pl.multiple_of(at * rows, rows), rows)
        out[...] = own_ref[span, :] + recv_ref[span, :]


def gather_kernel(nx, note_ref, other_note_ref, own_ref, recv_ref, unused_ref, middle_ref, *refs):
    x = lax.axis_index("scany")
    *blocks, grad, note, other_note, sems = refs
    copies = read_notes([note_ref, other_note_ref], [note, other_note], sems)
    npos, size, _ = own_ref.shape
    lane = lax.broadcasted_iota(jnp.int32, (size + 8, size), 1)
    grad[...] = jnp.zeros_like(grad)
    for copy, offs, terms in zip(copies, (note, other_note), (own_ref, recv_ref)):
        copy.wait()
        for j in range(npos):
            row, col = offset_in(offs, j)
            base, shift = aligned(row)
            term = rows_down(pltpu.roll(terms[j], col, axis=1), shift)
            low = jnp.where(lane >= col, term, 0.0)
            rows = pl.ds(base, size + 8)
            grad[rows, :size] += low
            grad[rows, size:] += term - low
    tile = middle_ref.shape[1]
    margin = (middle_ref.shape[0] - tile) // 2
    middle_ref[...] = grad[:, margin : margin + tile]
    for block, way in zip(blocks, ways_of(nx)):
        block[...] = grad[:, pl.ds(pl.multiple_of(side_of(x, way) * (margin + tile), margin), margin)]


def fold_kernel(nz, nx, unused_ref, middle_ref, *refs):
    z, x = lax.axis_index("scanx"), lax.axis_index("scany")
    ways = ways_of(nx)
    blocks, (center_ref, *edges, total) = refs[: len(ways)], refs[len(ways) :]
    tile = center_ref.shape[0]
    margin = (middle_ref.shape[0] - tile) // 2
    total[...] = middle_ref[...]
    for block, way in zip(blocks, ways):
        at = pl.multiple_of(side_of(x, way) * (tile - margin), margin)

        @pl.when(valid_of(x, way, nx))
        def _():
            total[:, pl.ds(at, margin)] += block[...]

    center_ref[...] = total[margin : margin + tile, :]
    for way, edge in enumerate(edges):
        edge[...] = total[pl.ds(pl.multiple_of(side_of(z, way) * (margin + tile), margin), margin), :]


def update_kernel(nz, unused_ref, spec_ref, center_ref, light_ref, other_light_ref, edge_a, edge_b, *refs):
    z, c = lax.axis_index("scanx"), lax.axis_index("pos")
    part_ref, grad = refs
    tile = center_ref.shape[0]
    grad[...] = center_ref[...]
    for way, edge in enumerate((edge_a, edge_b)):
        margin = edge.shape[0]
        at = pl.multiple_of(side_of(z, way) * (tile - margin), margin)

        @pl.when(valid_of(z, way, nz))
        def _():
            grad[pl.ds(at, margin), :] += edge[...]

    part_ref[...] = spec_ref[c] + grad[...] / (light_ref[...] + other_light_ref[...] + 1.0)


def add_kernel(a_ref, b_ref, *refs):
    refs[-1][...] = a_ref[...] + b_ref[...]


def specimen_kernel(part_ref, part_other_ref, out_ref, done_ref):
    done_ref[...] = jnp.zeros(done_ref.shape, done_ref.dtype)
    c = lax.axis_index("pos")
    out_ref[c] = part_ref[...]
    out_ref[1 - c] = part_other_ref[...]


def probe_kernel(step_size, probe_ref, keep_ref, away_ref, keep_other_ref, away_other_ref, unused_ref, out_ref):
    z, x, c = (lax.axis_index(a) for a in GROUP)
    rows = keep_ref.shape[0]
    for part, keep, away in ((c, keep_ref, away_ref), (1 - c, keep_other_ref, away_other_ref)):
        half = half_of(z, x, part)
        for at, term in ((half, keep), (1 - half, away)):
            span = pl.ds(pl.multiple_of(at * rows, rows), rows)
            out_ref[part, span, :] = probe_ref[part, span, :] + term[...] * step_size


def light_kernel(npos, nz, nx, which, note_ref, probe_ref, before_ref, unused_ref, *refs):
    z, x, c = (lax.axis_index(a) for a in GROUP)
    blocks, (light_ref, power_ref, total, *notes, sems) = refs[: len(which)], refs[len(which) :]
    own = len(notes) > len(which)
    copies = read_notes(([note_ref] if own else []) + [note_of(b) for b in blocks], notes, sems)
    size = probe_ref.shape[1]
    margin = size // 2
    tile = light_ref.shape[0]
    power_ref[...] = probe_ref[0] * probe_ref[0] + probe_ref[1] * probe_ref[1]
    total[...] = jnp.zeros_like(total)
    lane = lax.broadcasted_iota(jnp.int32, (size, size), 1)

    def add(row, col, ok):
        ok = jnp.logical_and(ok, jnp.logical_and(jnp.abs(row) < tile, jnp.abs(col) < tile))

        @pl.when(ok)
        def _():
            base, shift = aligned(row + tile)
            moved = pltpu.roll(power_ref[...], lax.rem(col + size, size), axis=1)
            keep = jnp.logical_and(lane >= col, lane < col + size)
            total[pl.ds(base, size + 8), :] += rows_down(jnp.where(keep, moved, 0.0), shift)

    ways, valid = block_ways(nz, nx), block_valid(z, x, nz, nx)
    places = [((None, None), True)] * own + [(ways[k], valid[k]) for k in which]
    for copy, note, ((zway, xway), ok) in zip(copies, notes, places):
        copy.wait()
        down = 0 if zway is None else (2 * side_of(z, zway) - 1) * tile
        right = 0 if xway is None else (2 * side_of(x, xway) - 1) * tile
        for j in range(npos):
            row, col = offset_in(note, j)
            add(row + down - margin, col + right - margin, ok)
    if own:
        light_ref[...] = total[tile : 2 * tile, :]
    else:
        light_ref[...] = before_ref[...] + total[tile : 2 * tile, :]


def call(kernel, out_shape, specs, *operands, scratch=(), outs=None, aliases={}, vmem=16 * 1024 * 1024):
    return pl.pallas_call(
        kernel,
        out_shape=out_shape,
        in_specs=specs,
        out_specs=outs or [VMEM] * len(out_shape),
        scratch_shapes=list(scratch),
        input_output_aliases=aliases,
        compiler_params=pltpu.CompilerParams(vmem_limit_bytes=vmem),
    )(*operands)


def dma(count):
    return pltpu.SemaphoreType.DMA((count,))


def shards(sizes, specimen, probe_wave, amplitudes, offsets):
    nz, nx, nc = sizes
    size = probe_wave.shape[1]
    margin = size // 2
    tile = specimen.shape[1]
    npos = offsets.shape[0]
    ways = block_ways(nz, nx)
    xways = ways_of(nx)
    targets = block_targets(nz, nx)

    def send(value, target):
        return lax.ppermute(value, GROUP, permutation(sizes, target))

    def to_core(value):
        return lax.ppermute(value, "pos", PART_SWAP)

    shapes = block_shapes(nz, nx, tile)
    *blocks, note = call(
        functools.partial(halo_blocks_kernel, nz, nx),
        [f32(h + NOTE[0], w) for h, w in shapes] + [f32(*NOTE)],
        [HBM, HBM],
        offsets,
        specimen,
        scratch=[pltpu.SMEM(offsets.shape, jnp.int32), dma(len(ways) + 1)],
        vmem=KEEP_IN_HBM,
    )
    recv = [send(block, target) for block, target in zip(blocks, targets)]

    waves = jnp.asarray(dft_waves(size))
    late = (note, specimen, probe_wave, amplitudes)
    note, specimen_v, probe_v, amp_v, ta_v, tb_v = call(
        fetch_kernel,
        [jax.ShapeDtypeStruct(a.shape, a.dtype) for a in late]
        + [jax.ShapeDtypeStruct((2 * size, 2 * size), jnp.bfloat16)] * 2,
        [ANY] * len(late) + [VMEM],
        *late,
        waves,
        scratch=[dma(len(late))],
    )
    lanes = min(w for _, w in shapes)
    (packed,) = call(
        functools.partial(pack_kernel, nz, nx, tile),
        [f32(sum(h * w for h, w in shapes) // lanes, lanes)],
        [ANY] + [VMEM] * len(recv),
        probe_v,
        *recv,
    )

    def patches_from(ours, after, *arrays):
        return call(
            functools.partial(patches_kernel, nz, nx, ours),
            [f32(npos, size, size)],
            [VMEM, ANY] + [VMEM] * (1 + len(arrays)),
            note,
            after,
            specimen_v,
            *arrays,
            scratch=[pltpu.VMEM((tile + size, tile + size), jnp.float32), NOTE_SMEM, dma(1)],
        )[0]

    def light_from(which, own, before, after):
        return call(
            functools.partial(light_kernel, npos, nz, nx, which),
            [f32(tile, tile)],
            [VMEM, VMEM, ANY if own else VMEM, ANY] + [VMEM] * len(which),
            note,
            probe_v,
            before,
            after,
            *[recv[k] for k in which],
            scratch=[
                pltpu.VMEM((size, size), jnp.float32),
                pltpu.VMEM((3 * tile, size), jnp.float32),
                *[NOTE_SMEM] * (own + len(which)),
                dma(own + len(which)),
            ],
        )[0]

    patches = patches_from(True, packed, *recv)
    light = light_from([k for k, (_, w) in enumerate(ways) if w is None], True, packed, patches)
    patches_other = patches_from(False, light, to_core(packed))
    own, other, probe_own, probe_other = call(
        positions_kernel,
        [f32(npos, size, size)] * 2 + [f32(size, size)] * 2,
        [VMEM] * 6,
        patches,
        patches_other,
        probe_v,
        amp_v,
        ta_v,
        tb_v,
    )
    other_note = to_core(note)
    light = light_from([k for k, (_, w) in enumerate(ways) if w is not None], False, light, own)

    zbits = [("z", 1 << k) for k in range(nz.bit_length() - 1)]
    xbits = [("x", 1 << k) for k in range(nx.bit_length() - 1)]
    orders = (xbits[:1] + zbits + xbits[1:], zbits + xbits)

    def stage(k):
        def target(z, x, c):
            axis, bit = orders[c][k]
            return (z ^ bit, x, c) if axis == "z" else (z, x ^ bit, c)

        return target

    half = f32(size // 2, size)
    keep, away, other = call(
        halve_kernel,
        [half] * 2 + [f32(npos, size, size)],
        [VMEM, VMEM, ANY, ANY],
        probe_own,
        to_core(probe_other),
        other,
        light,
        outs=[VMEM, VMEM, ANY],
        aliases={2: 2},
    )
    terms = to_core(other)
    middle, *beyond = call(
        functools.partial(gather_kernel, nx),
        [f32(tile + size, tile)] + [f32(tile + size, margin)] * len(xways),
        [VMEM] * 4 + [ANY],
        note,
        other_note,
        own,
        terms,
        keep,
        scratch=[pltpu.VMEM((tile + size, tile + size), jnp.float32), NOTE_SMEM, NOTE_SMEM, dma(2)],
    )
    (keep,) = call(add_kernel, [half], [VMEM] * 2 + [ANY], keep, send(away, stage(0)), middle)
    beside = [send(piece, targets[ways.index((None, way))]) for piece, way in zip(beyond, xways)]
    (keep,) = call(add_kernel, [half], [VMEM] * 2, keep, send(keep, stage(1)))
    center, *edges = call(
        functools.partial(fold_kernel, nz, nx),
        [f32(tile, tile)] + [f32(margin, tile)] * 2,
        [ANY] + [VMEM] * (1 + len(beside)),
        keep,
        middle,
        *beside,
        scratch=[pltpu.VMEM((tile + size, tile), jnp.float32)],
    )
    arrived = [send(edge, targets[ways.index((way, None))]) for way, edge in enumerate(edges)]
    for k in range(2, len(orders[0])):
        (keep,) = call(add_kernel, [half], [VMEM] * 2, keep, send(keep, stage(k)))
    (part,) = call(
        functools.partial(update_kernel, nz),
        [f32(tile, tile)],
        [ANY] + [VMEM] * (4 + len(arrived)),
        keep,
        specimen_v,
        center,
        light,
        to_core(light),
        *arrived,
        scratch=[pltpu.VMEM((tile, tile), jnp.float32)],
    )
    away = send(keep, stage(0))
    new_specimen, done = call(specimen_kernel, [f32(2, tile, tile), f32(*NOTE)], [VMEM] * 2, part, to_core(part))
    step_size = 1.0 / math.sqrt(npos * nz * nx * nc)
    (new_probe,) = call(
        functools.partial(probe_kernel, step_size),
        [f32(2, size, size)],
        [VMEM] * 5 + [ANY],
        probe_v,
        keep,
        away,
        to_core(keep),
        to_core(away),
        done,
    )
    return (new_specimen, new_probe)


def solution(mesh):
    sizes = tuple(mesh.shape[a] for a in GROUP)
    placed = (
        P(None, ("groups", "scanx"), "scany"),
        P(None, "groups", None),
        P(("groups", "scanx", "scany", "pos"), None, None),
        P(("groups", "scanx", "scany", "pos"), None),
    )
    return jax.shard_map(
        functools.partial(shards, sizes),
        mesh=mesh,
        in_specs=placed,
        out_specs=(P(None, ("groups", "scanx"), "scany"), P(None, "groups", None)),
        check_vma=False,
    )
```

```python
import functools
import math

import jax
import jax.numpy as jnp
import numpy as np
from jax import lax
from jax.experimental import pallas as pl
from jax.experimental.pallas import tpu as pltpu
from jax.sharding import PartitionSpec as P

GROUP = ("scanx", "scany", "pos")
KEEP_IN_HBM = 64 * 1024 * 1024 - 448 * 1024
PART_SWAP = ((0, 1), (1, 0))
VMEM = pl.BlockSpec(memory_space=pltpu.VMEM)
ANY = pl.BlockSpec(memory_space=pl.ANY)
HBM = pl.BlockSpec(memory_space=pltpu.HBM)
NOTE = (8, 128)
NOTE_SMEM = pltpu.SMEM(NOTE, jnp.float32)


def f32(*shape):
    return jax.ShapeDtypeStruct(shape, jnp.float32)


def ways_of(count):
    return (0,) if count == 2 else (0, 1)


def side_of(index, way):
    return lax.rem(index + way + 1, 2)


def valid_of(index, way, count):
    neighbour = index + 2 * side_of(index, way) - 1
    return jnp.logical_and(neighbour >= 0, neighbour < count)


def block_ways(nz, nx):
    xways, zways = ways_of(nx), (0, 1)
    order = [(None, w) for w in xways] + [(w, None) for w in zways]
    return order + [(v, w) for w in xways for v in zways]


def block_places(z, x, nz, nx, origin, extent, margin):
    places = []
    for zway, xway in block_ways(nz, nx):
        span = []
        for index, way in ((z, zway), (x, xway)):
            if way is None:
                span.append(pl.ds(origin, 2 * margin))
            else:
                span.append(pl.ds(pl.multiple_of(side_of(index, way) * extent, margin), margin))
        places.append(tuple(span))
    return places


def block_shapes(nz, nx, tile):
    return [tuple(tile if way is None else tile // 2 for way in ways) for ways in block_ways(nz, nx)]


def packing_order(nz, nx):
    ways = block_ways(nz, nx)
    return [[k for k, (_, w) in enumerate(ways) if (w is None) == later] for later in (False, True)]


def packed_places(shapes):
    lanes = min(min(shape) for shape in shapes)
    at, places = 0, []
    for height, width in shapes:
        places.append([])
        for col in range(0, width, lanes):
            places[-1].append((at, col, height))
            at += height
    return places


def block_valid(z, x, nz, nx):
    result = []
    for zway, xway in block_ways(nz, nx):
        ok = True
        if zway is not None:
            ok = valid_of(z, zway, nz)
        if xway is not None:
            ok = jnp.logical_and(ok, valid_of(x, xway, nx))
        result.append(ok)
    return result


def block_targets(nz, nx):
    def step(index, way, count):
        if way is None:
            return index
        to = index + (1 if (index + way) % 2 == 0 else -1)
        return to if 0 <= to < count else None

    def target(ways, z, x, c):
        tz, tx = step(z, ways[0], nz), step(x, ways[1], nx)
        return (z, x, 1 - c) if tz is None or tx is None else (tz, tx, c)

    return [functools.partial(target, ways) for ways in block_ways(nz, nx)]


def permutation(sizes, target):
    nz, nx, nc = sizes
    pairs = []
    for z in range(nz):
        for x in range(nx):
            for c in range(nc):
                tz, tx, tc = target(z, x, c)
                pairs.append(((z * nx + x) * nc + c, (tz * nx + tx) * nc + tc))
    return pairs


def dft_waves(length):
    index = np.arange(length, dtype=np.int32)
    phase = (index[:, None] * index[None, :]) % length
    angle = phase.astype(np.float32) * np.float32(2.0 * math.pi / length)
    scale = np.float32(1.0 / math.sqrt(length))
    sine = np.sin(angle) * scale
    return np.stack([np.cos(angle) * scale, sine, -sine]).astype(jnp.bfloat16)


def aligned(row):
    return pl.multiple_of((row // 8) * 8, 8), lax.rem(row, 8)


def rows_up(block, shift):
    count, width = block.shape
    groups = pltpu.roll(block.reshape(count // 8, 8, width), lax.rem(8 - shift, 8), axis=1)
    at = lax.broadcasted_iota(jnp.int32, (count // 8 - 1, 8, width), 1)
    return jnp.where(at < 8 - shift, groups[:-1], groups[1:]).reshape(count - 8, width)


def rows_down(block, shift):
    count, width = block.shape
    groups = pltpu.roll(block.reshape(count // 8, 8, width), shift, axis=1)
    blank = jnp.zeros((1, 8, width), block.dtype)
    at = lax.broadcasted_iota(jnp.int32, (count // 8 + 1, 8, width), 1)
    early = jnp.concatenate([groups, blank])
    late = jnp.concatenate([blank, groups])
    return jnp.where(at >= shift, early, late).reshape(count + 8, width)


def halo_blocks_kernel(nz, nx, off_hbm, spec_ref, *refs):
    z, x, c = (lax.axis_index(a) for a in GROUP)
    *outs, note_ref, off_ref, sems = refs
    tile = spec_ref.shape[1]
    margin = tile // 2
    off_copy = pltpu.make_async_copy(off_hbm, off_ref, sems.at[len(outs)])
    off_copy.start()
    copies = []
    places = block_places(z, x, nz, nx, 0, margin, margin)
    for k, (out, (height, _), (rows, cols)) in enumerate(zip(outs, block_shapes(nz, nx, tile), places)):
        copies.append(pltpu.make_async_copy(spec_ref.at[c, rows, cols], out.at[pl.ds(0, height), :], sems.at[k]))
        copies[-1].start()
    off_copy.wait()
    lane = lax.broadcasted_iota(jnp.int32, NOTE, 1)
    note = jnp.zeros(NOTE, jnp.float32)
    for j in range(off_ref.shape[0]):
        for k in range(2):
            note = jnp.where(lane == 2 * j + k, off_ref[j, k].astype(jnp.float32), note)
    note_ref[...] = note
    for out in outs:
        out[out.shape[0] - NOTE[0] :, : NOTE[1]] = note
    for copy in copies:
        copy.wait()


def read_notes(notes, smems, sems):
    copies = [pltpu.make_async_copy(note, smem, sems.at[k]) for k, (note, smem) in enumerate(zip(notes, smems))]
    for copy in copies:
        copy.start()
    return copies


def note_of(block):
    return block.at[pl.ds(block.shape[0] - NOTE[0], NOTE[0]), pl.ds(0, NOTE[1])]


def offset_in(note, j):
    return note[0, 2 * j].astype(jnp.int32), note[0, 2 * j + 1].astype(jnp.int32)


def fetch_kernel(*refs):
    *refs, table_a, table_b, sems = refs
    count = len(refs) // 2
    *sources, waves = refs[: count + 1]
    copies = [pltpu.make_async_copy(src, refs[count + 1 + k], sems.at[k]) for k, src in enumerate(sources)]
    for copy in copies:
        copy.start()
    cosine, sine, minus = (waves[k] for k in range(3))
    size = cosine.shape[0]
    for table, blocks in ((table_a, (cosine, sine, minus, cosine)), (table_b, (cosine, minus, sine, cosine))):
        for k, block in enumerate(blocks):
            at, left = k // 2 * size, k % 2 * size
            table[at : at + size, left : left + size] = block
    for copy in copies:
        copy.wait()


def cut_patches(note, padded, out):
    npos, size, _ = out.shape
    lane = lax.broadcasted_iota(jnp.int32, (size + 8, size), 1)
    for j in range(npos):
        row, col = offset_in(note, j)
        base, shift = aligned(row)
        rows = padded[pl.ds(base, size + 8), :]
        mixed = rows_up(jnp.where(lane >= col, rows[:, :size], rows[:, size:]), shift)
        out[j] = pltpu.roll(mixed, lax.rem(size - col, size), axis=1)


def patches_kernel(nz, nx, ours, note_ref, unused_ref, spec_ref, *refs):
    z, x, c = (lax.axis_index(a) for a in GROUP)
    *blocks, out, padded, note, sems = refs
    copies = read_notes([note_ref], [note], sems)
    tile = spec_ref.shape[1]
    margin = (padded.shape[0] - tile) // 2
    padded[margin : margin + tile, margin : margin + tile] = spec_ref[c if ours else 1 - c]
    if len(ways_of(nx)) == 1:
        far_cols = pl.ds(pl.multiple_of((1 - side_of(x, 0)) * (margin + tile), margin), margin)
        padded[:, far_cols] = jnp.zeros((padded.shape[0], margin), jnp.float32)
    places = block_places(z, x, nz, nx, margin, margin + tile, margin)
    shapes = block_shapes(nz, nx, tile)
    pieces = {}
    for which, array in zip(packing_order(nz, nx), blocks):
        for k, places_of in zip(which, packed_places([shapes[k] for k in which])):
            pieces[k] = [(array, at) for at, _, _ in places_of]
    for k, ((height, width), (rows, cols), ok) in enumerate(zip(shapes, places, block_valid(z, x, nz, nx))):

        @pl.when(ok)
        def _():
            if ours:
                padded[rows, cols] = blocks[k][:height, :]
            else:
                parts = [array[at : at + height, :] for array, at in pieces[k]]
                padded[rows, cols] = parts[0] if len(parts) == 1 else jnp.concatenate(parts, axis=1)

        @pl.when(jnp.logical_not(ok))
        def _():
            padded[rows, cols] = jnp.zeros((height, width), jnp.float32)

    copies[0].wait()
    cut_patches(note, padded, out)


def pack_kernel(shapes, note_ref, unused_ref, *refs):
    *blocks, out, note_out = refs
    note_out[...] = note_ref[...]
    for block, pieces in zip(blocks, packed_places(shapes)):
        for at, col, height in pieces:
            out[at : at + height, :] = block[:height, col : col + out.shape[1]]


def positions_kernel(patch_ref, patch_other_ref, probe_ref, amp_ref, ta_ref, tb_ref, own_ref, other_ref, probe_own_ref, probe_other_ref):
    first = lax.axis_index("pos") == 0
    npos, size, _ = patch_ref.shape
    table_a = ta_ref[...]
    table_b = tb_ref[...]
    probe_real = probe_ref[0]
    probe_imag = probe_ref[1]

    def side_by_side(both):
        return jnp.concatenate([both[:size], both[size:]], axis=1)

    grad_real = jnp.zeros((size, size), jnp.float32)
    grad_imag = jnp.zeros((size, size), jnp.float32)
    for j in range(npos):
        patch_real = jnp.where(first, patch_ref[j], patch_other_ref[j])
        patch_imag = jnp.where(first, patch_other_ref[j], patch_ref[j])
        exit_real = probe_real * patch_real - probe_imag * patch_imag
        exit_imag = probe_real * patch_imag + probe_imag * patch_real
        wave = jnp.concatenate([exit_real, exit_imag], axis=0).astype(jnp.bfloat16)
        half = jnp.dot(table_a, wave, preferred_element_type=jnp.float32).astype(jnp.bfloat16)
        far = jnp.dot(side_by_side(half), table_b, preferred_element_type=jnp.float32)
        far_real, far_imag = far[:, :size], far[:, size:]
        power = far_real * far_real + far_imag * far_imag
        ratio = amp_ref[j].astype(jnp.float32) * jnp.minimum(lax.rsqrt(power), 1.0 / 0.2)
        projected = jnp.concatenate([far_real * ratio, far_imag * ratio], axis=0).astype(jnp.bfloat16)
        back_half = jnp.dot(table_b, projected, preferred_element_type=jnp.float32).astype(jnp.bfloat16)
        back = jnp.dot(side_by_side(back_half), table_a, preferred_element_type=jnp.float32)
        diff_real = back[:, :size] - exit_real
        diff_imag = back[:, size:] - exit_imag
        term_real = probe_real * diff_real + probe_imag * diff_imag
        term_imag = probe_real * diff_imag - probe_imag * diff_real
        own_ref[j] = jnp.where(first, term_real, term_imag)
        other_ref[j] = jnp.where(first, term_imag, term_real)
        grad_real += patch_real * diff_real + patch_imag * diff_imag
        grad_imag += patch_real * diff_imag - patch_imag * diff_real
    probe_own_ref[...] = jnp.where(first, grad_real, grad_imag)
    probe_other_ref[...] = jnp.where(first, grad_imag, grad_real)


def half_of(z, x, c):
    return jnp.where(c == 0, lax.rem(x, 2), lax.rem(z, 2))


def halve_kernel(own_ref, recv_ref, unused_ref, unused_light_ref, keep_ref, give_ref, handed_on_ref):
    half = half_of(*(lax.axis_index(a) for a in GROUP))
    rows = keep_ref.shape[0]
    for at, out in ((half, keep_ref), (1 - half, give_ref)):
        span = pl.ds(pl.multiple_of(at * rows, rows), rows)
        out[...] = own_ref[span, :] + recv_ref[span, :]


def gather_kernel(nx, note_ref, other_note_ref, own_ref, recv_ref, unused_ref, middle_ref, *refs):
    x = lax.axis_index("scany")
    *blocks, grad, note, other_note, sems = refs
    copies = read_notes([note_ref, other_note_ref], [note, other_note], sems)
    npos, size, _ = own_ref.shape
    lane = lax.broadcasted_iota(jnp.int32, (size + 8, size), 1)
    grad[...] = jnp.zeros_like(grad)
    for copy, offs, terms in zip(copies, (note, other_note), (own_ref, recv_ref)):
        copy.wait()
        for j in range(npos):
            row, col = offset_in(offs, j)
            base, shift = aligned(row)
            term = rows_down(pltpu.roll(terms[j], col, axis=1), shift)
            low = jnp.where(lane >= col, term, 0.0)
            rows = pl.ds(base, size + 8)
            grad[rows, :size] += low
            grad[rows, size:] += term - low
    tile = middle_ref.shape[1]
    margin = (middle_ref.shape[0] - tile) // 2
    middle_ref[...] = grad[:, margin : margin + tile]
    for block, way in zip(blocks, ways_of(nx)):
        block[...] = grad[:, pl.ds(pl.multiple_of(side_of(x, way) * (margin + tile), margin), margin)]


def fold_kernel(nz, nx, unused_ref, middle_ref, *refs):
    z, x = lax.axis_index("scanx"), lax.axis_index("scany")
    ways = ways_of(nx)
    blocks, (center_ref, *edges, total) = refs[: len(ways)], refs[len(ways) :]
    tile = center_ref.shape[0]
    margin = (middle_ref.shape[0] - tile) // 2
    total[...] = middle_ref[...]
    for block, way in zip(blocks, ways):
        at = pl.multiple_of(side_of(x, way) * (tile - margin), margin)

        @pl.when(valid_of(x, way, nx))
        def _():
            total[:, pl.ds(at, margin)] += block[...]

    center_ref[...] = total[margin : margin + tile, :]
    for way, edge in enumerate(edges):
        edge[...] = total[pl.ds(pl.multiple_of(side_of(z, way) * (margin + tile), margin), margin), :]


def update_kernel(nz, unused_ref, spec_ref, center_ref, light_ref, other_light_ref, edge_a, edge_b, *refs):
    z, c = lax.axis_index("scanx"), lax.axis_index("pos")
    upper_ref, lower_ref, grad = refs
    tile = center_ref.shape[0]
    grad[...] = center_ref[...]
    for way, edge in enumerate((edge_a, edge_b)):
        margin = edge.shape[0]
        at = pl.multiple_of(side_of(z, way) * (tile - margin), margin)

        @pl.when(valid_of(z, way, nz))
        def _():
            grad[pl.ds(at, margin), :] += edge[...]

    for at, out in ((0, upper_ref), (tile // 2, lower_ref)):
        span = pl.ds(at, tile // 2)
        out[...] = spec_ref[c, span, :] + grad[span, :] / (light_ref[span, :] + other_light_ref[span, :] + 1.0)


def add_kernel(a_ref, b_ref, *refs):
    refs[-1][...] = a_ref[...] + b_ref[...]


def specimen_kernel(upper_ref, lower_ref, other_upper_ref, other_lower_ref, out_ref, done_ref):
    c = lax.axis_index("pos")
    rows = upper_ref.shape[0]
    for part, upper, lower in ((c, upper_ref, lower_ref), (1 - c, other_upper_ref, other_lower_ref)):
        out_ref[part, :rows, :] = upper[...]
        out_ref[part, rows:, :] = lower[...]
    done_ref[...] = jnp.zeros(done_ref.shape, done_ref.dtype)


def probe_kernel(step_size, probe_ref, keep_ref, away_ref, keep_other_ref, away_other_ref, unused_ref, out_ref):
    z, x, c = (lax.axis_index(a) for a in GROUP)
    rows = keep_ref.shape[0]
    for part, keep, away in ((c, keep_ref, away_ref), (1 - c, keep_other_ref, away_other_ref)):
        half = half_of(z, x, part)
        for at, term in ((half, keep), (1 - half, away)):
            span = pl.ds(pl.multiple_of(at * rows, rows), rows)
            out_ref[part, span, :] = probe_ref[part, span, :] + term[...] * step_size


def light_kernel(npos, nz, nx, which, note_ref, probe_ref, before_ref, unused_ref, *refs):
    z, x, c = (lax.axis_index(a) for a in GROUP)
    blocks, (light_ref, power_ref, total, *notes, sems) = refs[: len(which)], refs[len(which) :]
    own = len(notes) > len(which)
    copies = read_notes(([note_ref] if own else []) + [note_of(b) for b in blocks], notes, sems)
    size = probe_ref.shape[1]
    margin = size // 2
    tile = light_ref.shape[0]
    power_ref[...] = probe_ref[0] * probe_ref[0] + probe_ref[1] * probe_ref[1]
    total[...] = jnp.zeros_like(total)
    lane = lax.broadcasted_iota(jnp.int32, (size, size), 1)

    def add(row, col, ok):
        ok = jnp.logical_and(ok, jnp.logical_and(jnp.abs(row) < tile, jnp.abs(col) < tile))

        @pl.when(ok)
        def _():
            base, shift = aligned(row + tile)
            moved = pltpu.roll(power_ref[...], lax.rem(col + size, size), axis=1)
            keep = jnp.logical_and(lane >= col, lane < col + size)
            total[pl.ds(base, size + 8), :] += rows_down(jnp.where(keep, moved, 0.0), shift)

    ways, valid = block_ways(nz, nx), block_valid(z, x, nz, nx)
    places = [((None, None), True)] * own + [(ways[k], valid[k]) for k in which]
    for copy, note, ((zway, xway), ok) in zip(copies, notes, places):
        copy.wait()
        down = 0 if zway is None else (2 * side_of(z, zway) - 1) * tile
        right = 0 if xway is None else (2 * side_of(x, xway) - 1) * tile
        for j in range(npos):
            row, col = offset_in(note, j)
            add(row + down - margin, col + right - margin, ok)
    if own:
        light_ref[...] = total[tile : 2 * tile, :]
    else:
        light_ref[...] = before_ref[...] + total[tile : 2 * tile, :]


def call(kernel, out_shape, specs, *operands, scratch=(), outs=None, aliases={}, vmem=16 * 1024 * 1024):
    return pl.pallas_call(
        kernel,
        out_shape=out_shape,
        in_specs=specs,
        out_specs=outs or [VMEM] * len(out_shape),
        scratch_shapes=list(scratch),
        input_output_aliases=aliases,
        compiler_params=pltpu.CompilerParams(vmem_limit_bytes=vmem),
    )(*operands)


def dma(count):
    return pltpu.SemaphoreType.DMA((count,))


def shards(sizes, specimen, probe_wave, amplitudes, offsets):
    nz, nx, nc = sizes
    size = probe_wave.shape[1]
    margin = size // 2
    tile = specimen.shape[1]
    npos = offsets.shape[0]
    ways = block_ways(nz, nx)
    xways = ways_of(nx)
    targets = block_targets(nz, nx)

    def send(value, target):
        return lax.ppermute(value, GROUP, permutation(sizes, target))

    def to_core(value):
        return lax.ppermute(value, "pos", PART_SWAP)

    shapes = block_shapes(nz, nx, tile)
    *blocks, note = call(
        functools.partial(halo_blocks_kernel, nz, nx),
        [f32(h + NOTE[0], w) for h, w in shapes] + [f32(*NOTE)],
        [HBM, HBM],
        offsets,
        specimen,
        scratch=[pltpu.SMEM(offsets.shape, jnp.int32), dma(len(ways) + 1)],
        vmem=KEEP_IN_HBM,
    )
    recv = [send(block, target) for block, target in zip(blocks, targets)]

    waves = jnp.asarray(dft_waves(size))
    late = (note, specimen, probe_wave, amplitudes)
    note, specimen_v, probe_v, amp_v, ta_v, tb_v = call(
        fetch_kernel,
        [jax.ShapeDtypeStruct(a.shape, a.dtype) for a in late]
        + [jax.ShapeDtypeStruct((2 * size, 2 * size), jnp.bfloat16)] * 2,
        [ANY] * len(late) + [VMEM],
        *late,
        waves,
        scratch=[dma(len(late))],
    )
    def packed(which, note, after):
        chosen = [shapes[k] for k in which]
        return call(
            functools.partial(pack_kernel, chosen),
            [f32(sum(h * w for h, w in chosen) // margin, margin), f32(*NOTE)],
            [VMEM, ANY] + [VMEM] * len(which),
            note,
            after,
            *[recv[k] for k in which],
        )

    def patches_from(ours, after, *arrays):
        return call(
            functools.partial(patches_kernel, nz, nx, ours),
            [f32(npos, size, size)],
            [VMEM, ANY] + [VMEM] * (1 + len(arrays)),
            note,
            after,
            specimen_v,
            *arrays,
            scratch=[pltpu.VMEM((tile + size, tile + size), jnp.float32), NOTE_SMEM, dma(1)],
        )[0]

    def light_from(which, own, before, after):
        return call(
            functools.partial(light_kernel, npos, nz, nx, which),
            [f32(tile, tile)],
            [VMEM, VMEM, ANY if own else VMEM, ANY] + [VMEM] * len(which),
            note,
            probe_v,
            before,
            after,
            *[recv[k] for k in which],
            scratch=[
                pltpu.VMEM((size, size), jnp.float32),
                pltpu.VMEM((3 * tile, size), jnp.float32),
                *[NOTE_SMEM] * (own + len(which)),
                dma(own + len(which)),
            ],
        )[0]

    along_x, along_z = packing_order(nz, nx)
    packed_x, handed_on = packed(along_x, note, probe_v)
    light = light_from(along_x, True, packed_x, packed_x)
    packed_z, other_note = packed(along_z, to_core(handed_on), light)
    patches = patches_from(True, packed_z, *recv)
    patches_other = patches_from(False, patches, to_core(packed_x), to_core(packed_z))
    own, other, probe_own, probe_other = call(
        positions_kernel,
        [f32(npos, size, size)] * 2 + [f32(size, size)] * 2,
        [VMEM] * 6,
        patches,
        patches_other,
        probe_v,
        amp_v,
        ta_v,
        tb_v,
    )
    light = light_from(along_z, False, light, own)

    zbits = [("z", 1 << k) for k in range(nz.bit_length() - 1)]
    xbits = [("x", 1 << k) for k in range(nx.bit_length() - 1)]
    orders = (xbits[:1] + zbits + xbits[1:], zbits + xbits)

    def stage(k):
        def target(z, x, c):
            axis, bit = orders[c][k]
            return (z ^ bit, x, c) if axis == "z" else (z, x ^ bit, c)

        return target

    half = f32(size // 2, size)
    keep, away, other = call(
        halve_kernel,
        [half] * 2 + [f32(npos, size, size)],
        [VMEM, VMEM, ANY, ANY],
        probe_own,
        to_core(probe_other),
        other,
        light,
        outs=[VMEM, VMEM, ANY],
        aliases={2: 2},
    )
    terms = to_core(other)
    middle, *beyond = call(
        functools.partial(gather_kernel, nx),
        [f32(tile + size, tile)] + [f32(tile + size, margin)] * len(xways),
        [VMEM] * 4 + [ANY],
        note,
        other_note,
        own,
        terms,
        keep,
        scratch=[pltpu.VMEM((tile + size, tile + size), jnp.float32), NOTE_SMEM, NOTE_SMEM, dma(2)],
    )
    (keep,) = call(add_kernel, [half], [VMEM] * 2 + [ANY], keep, send(away, stage(0)), middle)
    beside = [send(piece, targets[ways.index((None, way))]) for piece, way in zip(beyond, xways)]
    (keep,) = call(add_kernel, [half], [VMEM] * 2, keep, send(keep, stage(1)))
    center, *edges = call(
        functools.partial(fold_kernel, nz, nx),
        [f32(tile, tile)] + [f32(margin, tile)] * 2,
        [ANY] + [VMEM] * (1 + len(beside)),
        keep,
        middle,
        *beside,
        scratch=[pltpu.VMEM((tile + size, tile), jnp.float32)],
    )
    arrived = [send(edge, targets[ways.index((way, None))]) for way, edge in enumerate(edges)]
    for k in range(2, len(orders[0])):
        (keep,) = call(add_kernel, [half], [VMEM] * 2, keep, send(keep, stage(k)))
    updated = call(
        functools.partial(update_kernel, nz),
        [f32(tile // 2, tile)] * 2,
        [ANY] + [VMEM] * (4 + len(arrived)),
        keep,
        specimen_v,
        center,
        light,
        to_core(light),
        *arrived,
        scratch=[pltpu.VMEM((tile, tile), jnp.float32)],
    )
    away = send(keep, stage(0))
    new_specimen, done = call(
        specimen_kernel, [f32(2, tile, tile), f32(*NOTE)], [VMEM] * 4, *updated, *[to_core(u) for u in updated]
    )
    step_size = 1.0 / math.sqrt(npos * nz * nx * nc)
    (new_probe,) = call(
        functools.partial(probe_kernel, step_size),
        [f32(2, size, size)],
        [VMEM] * 5 + [ANY],
        probe_v,
        keep,
        away,
        to_core(keep),
        to_core(away),
        done,
    )
    return (new_specimen, new_probe)


def solution(mesh):
    sizes = tuple(mesh.shape[a] for a in GROUP)
    placed = (
        P(None, ("groups", "scanx"), "scany"),
        P(None, "groups", None),
        P(("groups", "scanx", "scany", "pos"), None, None),
        P(("groups", "scanx", "scany", "pos"), None),
    )
    return jax.shard_map(
        functools.partial(shards, sizes),
        mesh=mesh,
        in_specs=placed,
        out_specs=(P(None, ("groups", "scanx"), "scany"), P(None, "groups", None)),
        check_vma=False,
    )
```

```python
import functools
import math

import jax
import jax.numpy as jnp
import numpy as np
from jax import lax
from jax.experimental import pallas as pl
from jax.experimental.pallas import tpu as pltpu
from jax.sharding import PartitionSpec as P

GROUP = ("scanx", "scany", "pos")
KEEP_IN_HBM = 64 * 1024 * 1024 - 448 * 1024
PART_SWAP = ((0, 1), (1, 0))
VMEM = pl.BlockSpec(memory_space=pltpu.VMEM)
ANY = pl.BlockSpec(memory_space=pl.ANY)
HBM = pl.BlockSpec(memory_space=pltpu.HBM)
NOTE = (8, 128)
FILL_ROWS = 16
NOTE_SMEM = pltpu.SMEM(NOTE, jnp.float32)


def f32(*shape):
    return jax.ShapeDtypeStruct(shape, jnp.float32)


def ways_of(count):
    return (0,) if count == 2 else (0, 1)


def side_of(index, way):
    return lax.rem(index + way + 1, 2)


def valid_of(index, way, count):
    neighbour = index + 2 * side_of(index, way) - 1
    return jnp.logical_and(neighbour >= 0, neighbour < count)


def block_ways(nz, nx):
    xways, zways = ways_of(nx), (0, 1)
    order = [(None, w) for w in xways] + [(w, None) for w in zways]
    return order + [(v, w) for w in xways for v in zways]


def block_places(z, x, nz, nx, origin, extent, margin):
    places = []
    for zway, xway in block_ways(nz, nx):
        span = []
        for index, way in ((z, zway), (x, xway)):
            if way is None:
                span.append(pl.ds(origin, 2 * margin))
            else:
                span.append(pl.ds(pl.multiple_of(side_of(index, way) * extent, margin), margin))
        places.append(tuple(span))
    return places


def block_shapes(nz, nx, tile):
    return [tuple(tile if way is None else tile // 2 for way in ways) for ways in block_ways(nz, nx)]


def packing_order(nz, nx):
    ways = block_ways(nz, nx)
    kinds = [(v is not None, w is not None) for v, w in ways]
    return [[k for k, kind in enumerate(kinds) if kind == which] for which in ((True, True), (True, False), (False, True))]


def packed_places(shapes):
    lanes = min(min(shape) for shape in shapes)
    at, places = 0, []
    for height, width in shapes:
        places.append([])
        for col in range(0, width, lanes):
            places[-1].append((at, col, height))
            at += height
    return places


def block_valid(z, x, nz, nx):
    result = []
    for zway, xway in block_ways(nz, nx):
        ok = True
        if zway is not None:
            ok = valid_of(z, zway, nz)
        if xway is not None:
            ok = jnp.logical_and(ok, valid_of(x, xway, nx))
        result.append(ok)
    return result


def block_targets(nz, nx):
    def step(index, way, count):
        if way is None:
            return index
        to = index + (1 if (index + way) % 2 == 0 else -1)
        return to if 0 <= to < count else None

    def target(ways, z, x, c):
        tz, tx = step(z, ways[0], nz), step(x, ways[1], nx)
        return (z, x, 1 - c) if tz is None or tx is None else (tz, tx, c)

    return [functools.partial(target, ways) for ways in block_ways(nz, nx)]


def permutation(sizes, target):
    nz, nx, nc = sizes
    pairs = []
    for z in range(nz):
        for x in range(nx):
            for c in range(nc):
                tz, tx, tc = target(z, x, c)
                pairs.append(((z * nx + x) * nc + c, (tz * nx + tx) * nc + tc))
    return pairs


def dft_waves(length):
    index = np.arange(length, dtype=np.int32)
    phase = (index[:, None] * index[None, :]) % length
    angle = phase.astype(np.float32) * np.float32(2.0 * math.pi / length)
    scale = np.float32(1.0 / math.sqrt(length))
    sine = np.sin(angle) * scale
    return np.stack([np.cos(angle) * scale, sine, -sine]).astype(jnp.bfloat16)


def aligned(row):
    return pl.multiple_of((row // 8) * 8, 8), lax.rem(row, 8)


def rows_up(block, shift):
    count, width = block.shape
    groups = pltpu.roll(block.reshape(count // 8, 8, width), lax.rem(8 - shift, 8), axis=1)
    at = lax.broadcasted_iota(jnp.int32, (count // 8 - 1, 8, width), 1)
    return jnp.where(at < 8 - shift, groups[:-1], groups[1:]).reshape(count - 8, width)


def rows_down(block, shift):
    count, width = block.shape
    groups = pltpu.roll(block.reshape(count // 8, 8, width), shift, axis=1)
    blank = jnp.zeros((1, 8, width), block.dtype)
    at = lax.broadcasted_iota(jnp.int32, (count // 8 + 1, 8, width), 1)
    early = jnp.concatenate([groups, blank])
    late = jnp.concatenate([blank, groups])
    return jnp.where(at >= shift, early, late).reshape(count + 8, width)


def halo_blocks_kernel(nz, nx, off_hbm, spec_ref, *refs):
    z, x, c = (lax.axis_index(a) for a in GROUP)
    *outs, note_ref, off_ref, sems = refs
    tile = spec_ref.shape[1]
    margin = tile // 2
    off_copy = pltpu.make_async_copy(off_hbm, off_ref, sems.at[len(outs)])
    off_copy.start()
    copies = []
    places = block_places(z, x, nz, nx, 0, margin, margin)
    for k, (out, (height, _), (rows, cols)) in enumerate(zip(outs, block_shapes(nz, nx, tile), places)):
        copies.append(pltpu.make_async_copy(spec_ref.at[c, rows, cols], out.at[pl.ds(0, height), :], sems.at[k]))
        copies[-1].start()
    off_copy.wait()
    lane = lax.broadcasted_iota(jnp.int32, NOTE, 1)
    note = jnp.zeros(NOTE, jnp.float32)
    for j in range(off_ref.shape[0]):
        for k in range(2):
            note = jnp.where(lane == 2 * j + k, off_ref[j, k].astype(jnp.float32), note)
    note_ref[...] = note
    for out, (height, width) in zip(outs, block_shapes(nz, nx, tile)):
        fill = out.shape[0] - NOTE[0] - height
        if fill:
            out[height : height + fill, :] = jnp.zeros((fill, width), jnp.float32)
        out[height + fill :, : NOTE[1]] = note
    for copy in copies:
        copy.wait()


def read_notes(notes, smems, sems):
    copies = [pltpu.make_async_copy(note, smem, sems.at[k]) for k, (note, smem) in enumerate(zip(notes, smems))]
    for copy in copies:
        copy.start()
    return copies


def note_of(block):
    return block.at[pl.ds(block.shape[0] - NOTE[0], NOTE[0]), pl.ds(0, NOTE[1])]


def offset_in(note, j):
    return note[0, 2 * j].astype(jnp.int32), note[0, 2 * j + 1].astype(jnp.int32)


def fetch_kernel(*refs):
    *refs, table_a, table_b, sems = refs
    count = len(refs) // 2
    *sources, waves = refs[: count + 1]
    copies = [pltpu.make_async_copy(src, refs[count + 1 + k], sems.at[k]) for k, src in enumerate(sources)]
    for copy in copies:
        copy.start()
    cosine, sine, minus = (waves[k] for k in range(3))
    size = cosine.shape[0]
    for table, blocks in ((table_a, (cosine, sine, minus, cosine)), (table_b, (cosine, minus, sine, cosine))):
        for k, block in enumerate(blocks):
            at, left = k // 2 * size, k % 2 * size
            table[at : at + size, left : left + size] = block
    for copy in copies:
        copy.wait()


def cut_patches(note, padded, out):
    npos, size, _ = out.shape
    lane = lax.broadcasted_iota(jnp.int32, (size + 8, size), 1)
    for j in range(npos):
        row, col = offset_in(note, j)
        base, shift = aligned(row)
        rows = padded[pl.ds(base, size + 8), :]
        mixed = rows_up(jnp.where(lane >= col, rows[:, :size], rows[:, size:]), shift)
        out[j] = pltpu.roll(mixed, lax.rem(size - col, size), axis=1)


def patches_kernel(nz, nx, ours, note_ref, unused_ref, spec_ref, *refs):
    z, x, c = (lax.axis_index(a) for a in GROUP)
    *blocks, out, padded, note, sems = refs
    copies = read_notes([note_ref], [note], sems)
    tile = spec_ref.shape[1]
    margin = (padded.shape[0] - tile) // 2
    padded[margin : margin + tile, margin : margin + tile] = spec_ref[c if ours else 1 - c]
    if len(ways_of(nx)) == 1:
        far_cols = pl.ds(pl.multiple_of((1 - side_of(x, 0)) * (margin + tile), margin), margin)
        padded[:, far_cols] = jnp.zeros((padded.shape[0], margin), jnp.float32)
    places = block_places(z, x, nz, nx, margin, margin + tile, margin)
    shapes = block_shapes(nz, nx, tile)
    corners, along_z, along_x = packing_order(nz, nx)
    pieces = {k: [(block, 0)] for k, block in zip(along_x, blocks[2:])}
    for which, array in zip((corners, along_z), blocks):
        for k, places_of in zip(which, packed_places([shapes[k] for k in which])):
            pieces[k] = [(array, at) for at, _, _ in places_of]
    for k, ((height, width), (rows, cols), ok) in enumerate(zip(shapes, places, block_valid(z, x, nz, nx))):

        @pl.when(ok)
        def _():
            if ours:
                padded[rows, cols] = blocks[k][:height, :]
            else:
                parts = [array[at : at + height, :] for array, at in pieces[k]]
                padded[rows, cols] = parts[0] if len(parts) == 1 else jnp.concatenate(parts, axis=1)

        @pl.when(jnp.logical_not(ok))
        def _():
            padded[rows, cols] = jnp.zeros((height, width), jnp.float32)

    copies[0].wait()
    cut_patches(note, padded, out)


def pack_kernel(shapes, waits, *refs):
    *blocks, out = refs[waits:]
    for block, pieces in zip(blocks, packed_places(shapes)):
        for at, col, height in pieces:
            out[at : at + height, :] = block[:height, col : col + out.shape[1]]


def positions_kernel(patch_ref, patch_other_ref, probe_ref, amp_ref, ta_ref, tb_ref, own_ref, other_ref, probe_own_ref, probe_other_ref):
    first = lax.axis_index("pos") == 0
    npos, size, _ = patch_ref.shape
    table_a = ta_ref[...]
    table_b = tb_ref[...]
    probe_real = probe_ref[0]
    probe_imag = probe_ref[1]

    def side_by_side(both):
        return jnp.concatenate([both[:size], both[size:]], axis=1)

    grad_real = jnp.zeros((size, size), jnp.float32)
    grad_imag = jnp.zeros((size, size), jnp.float32)
    for j in range(npos):
        patch_real = jnp.where(first, patch_ref[j], patch_other_ref[j])
        patch_imag = jnp.where(first, patch_other_ref[j], patch_ref[j])
        exit_real = probe_real * patch_real - probe_imag * patch_imag
        exit_imag = probe_real * patch_imag + probe_imag * patch_real
        wave = jnp.concatenate([exit_real, exit_imag], axis=0).astype(jnp.bfloat16)
        half = jnp.dot(table_a, wave, preferred_element_type=jnp.float32).astype(jnp.bfloat16)
        far = jnp.dot(side_by_side(half), table_b, preferred_element_type=jnp.float32)
        far_real, far_imag = far[:, :size], far[:, size:]
        power = far_real * far_real + far_imag * far_imag
        ratio = amp_ref[j].astype(jnp.float32) * jnp.minimum(lax.rsqrt(power), 1.0 / 0.2)
        projected = jnp.concatenate([far_real * ratio, far_imag * ratio], axis=0).astype(jnp.bfloat16)
        back_half = jnp.dot(table_b, projected, preferred_element_type=jnp.float32).astype(jnp.bfloat16)
        back = jnp.dot(side_by_side(back_half), table_a, preferred_element_type=jnp.float32)
        diff_real = back[:, :size] - exit_real
        diff_imag = back[:, size:] - exit_imag
        term_real = probe_real * diff_real + probe_imag * diff_imag
        term_imag = probe_real * diff_imag - probe_imag * diff_real
        own_ref[j] = jnp.where(first, term_real, term_imag)
        other_ref[j] = jnp.where(first, term_imag, term_real)
        grad_real += patch_real * diff_real + patch_imag * diff_imag
        grad_imag += patch_real * diff_imag - patch_imag * diff_real
    probe_own_ref[...] = jnp.where(first, grad_real, grad_imag)
    probe_other_ref[...] = jnp.where(first, grad_imag, grad_real)


def half_of(z, x, c):
    return jnp.where(c == 0, lax.rem(x, 2), lax.rem(z, 2))


def halve_kernel(own_ref, recv_ref, unused_ref, unused_light_ref, keep_ref, give_ref, handed_on_ref):
    half = half_of(*(lax.axis_index(a) for a in GROUP))
    rows = keep_ref.shape[0]
    for at, out in ((half, keep_ref), (1 - half, give_ref)):
        span = pl.ds(pl.multiple_of(at * rows, rows), rows)
        out[...] = own_ref[span, :] + recv_ref[span, :]


def gather_kernel(nx, note_ref, other_note_ref, own_ref, recv_ref, unused_ref, middle_ref, *refs):
    x = lax.axis_index("scany")
    *blocks, grad, note, other_note, sems = refs
    copies = read_notes([note_ref, other_note_ref], [note, other_note], sems)
    npos, size, _ = own_ref.shape
    lane = lax.broadcasted_iota(jnp.int32, (size + 8, size), 1)
    grad[...] = jnp.zeros_like(grad)
    for copy, offs, terms in zip(copies, (note, other_note), (own_ref, recv_ref)):
        copy.wait()
        for j in range(npos):
            row, col = offset_in(offs, j)
            base, shift = aligned(row)
            term = rows_down(pltpu.roll(terms[j], col, axis=1), shift)
            low = jnp.where(lane >= col, term, 0.0)
            rows = pl.ds(base, size + 8)
            grad[rows, :size] += low
            grad[rows, size:] += term - low
    tile = middle_ref.shape[1]
    margin = (middle_ref.shape[0] - tile) // 2
    middle_ref[...] = grad[:, margin : margin + tile]
    for block, way in zip(blocks, ways_of(nx)):
        block[...] = grad[:, pl.ds(pl.multiple_of(side_of(x, way) * (margin + tile), margin), margin)]


def fold_kernel(nz, nx, unused_ref, middle_ref, *refs):
    z, x = lax.axis_index("scanx"), lax.axis_index("scany")
    ways = ways_of(nx)
    blocks, (center_ref, *edges, total) = refs[: len(ways)], refs[len(ways) :]
    tile = center_ref.shape[0]
    margin = (middle_ref.shape[0] - tile) // 2
    total[...] = middle_ref[...]
    for block, way in zip(blocks, ways):
        at = pl.multiple_of(side_of(x, way) * (tile - margin), margin)

        @pl.when(valid_of(x, way, nx))
        def _():
            total[:, pl.ds(at, margin)] += block[...]

    center_ref[...] = total[margin : margin + tile, :]
    for way, edge in enumerate(edges):
        edge[...] = total[pl.ds(pl.multiple_of(side_of(z, way) * (margin + tile), margin), margin), :]


def update_kernel(nz, unused_ref, spec_ref, center_ref, light_ref, other_light_ref, edge_a, edge_b, *refs):
    z, c = lax.axis_index("scanx"), lax.axis_index("pos")
    upper_ref, lower_ref, grad = refs
    tile = center_ref.shape[0]
    grad[...] = center_ref[...]
    for way, edge in enumerate((edge_a, edge_b)):
        margin = edge.shape[0]
        at = pl.multiple_of(side_of(z, way) * (tile - margin), margin)

        @pl.when(valid_of(z, way, nz))
        def _():
            grad[pl.ds(at, margin), :] += edge[...]

    for at, out in ((0, upper_ref), (tile // 2, lower_ref)):
        span = pl.ds(at, tile // 2)
        out[...] = spec_ref[c, span, :] + grad[span, :] / (light_ref[span, :] + other_light_ref[span, :] + 1.0)


def add_kernel(a_ref, b_ref, *refs):
    refs[-1][...] = a_ref[...] + b_ref[...]


def specimen_kernel(upper_ref, lower_ref, other_upper_ref, other_lower_ref, out_ref, done_ref):
    c = lax.axis_index("pos")
    rows = upper_ref.shape[0]
    for part, upper, lower in ((c, upper_ref, lower_ref), (1 - c, other_upper_ref, other_lower_ref)):
        out_ref[part, :rows, :] = upper[...]
        out_ref[part, rows:, :] = lower[...]
    done_ref[...] = jnp.zeros(done_ref.shape, done_ref.dtype)


def probe_kernel(step_size, probe_ref, keep_ref, away_ref, keep_other_ref, away_other_ref, unused_ref, out_ref):
    z, x, c = (lax.axis_index(a) for a in GROUP)
    rows = keep_ref.shape[0]
    for part, keep, away in ((c, keep_ref, away_ref), (1 - c, keep_other_ref, away_other_ref)):
        half = half_of(z, x, part)
        for at, term in ((half, keep), (1 - half, away)):
            span = pl.ds(pl.multiple_of(at * rows, rows), rows)
            out_ref[part, span, :] = probe_ref[part, span, :] + term[...] * step_size


def light_kernel(npos, nz, nx, which, note_ref, probe_ref, before_ref, unused_ref, *refs):
    z, x, c = (lax.axis_index(a) for a in GROUP)
    blocks, (light_ref, power_ref, total, *notes, sems) = refs[: len(which)], refs[len(which) :]
    own = len(notes) > len(which)
    copies = read_notes(([note_ref] if own else []) + [note_of(b) for b in blocks], notes, sems)
    size = probe_ref.shape[1]
    margin = size // 2
    tile = light_ref.shape[0]
    power_ref[...] = probe_ref[0] * probe_ref[0] + probe_ref[1] * probe_ref[1]
    total[...] = jnp.zeros_like(total)
    lane = lax.broadcasted_iota(jnp.int32, (size, size), 1)

    def add(row, col, ok):
        ok = jnp.logical_and(ok, jnp.logical_and(jnp.abs(row) < tile, jnp.abs(col) < tile))

        @pl.when(ok)
        def _():
            base, shift = aligned(row + tile)
            moved = pltpu.roll(power_ref[...], lax.rem(col + size, size), axis=1)
            keep = jnp.logical_and(lane >= col, lane < col + size)
            total[pl.ds(base, size + 8), :] += rows_down(jnp.where(keep, moved, 0.0), shift)

    ways, valid = block_ways(nz, nx), block_valid(z, x, nz, nx)
    places = [((None, None), True)] * own + [(ways[k], valid[k]) for k in which]
    for copy, note, ((zway, xway), ok) in zip(copies, notes, places):
        copy.wait()
        down = 0 if zway is None else (2 * side_of(z, zway) - 1) * tile
        right = 0 if xway is None else (2 * side_of(x, xway) - 1) * tile
        for j in range(npos):
            row, col = offset_in(note, j)
            add(row + down - margin, col + right - margin, ok)
    if own:
        light_ref[...] = total[tile : 2 * tile, :]
    else:
        light_ref[...] = before_ref[...] + total[tile : 2 * tile, :]


def call(kernel, out_shape, specs, *operands, scratch=(), outs=None, aliases={}, vmem=16 * 1024 * 1024):
    return pl.pallas_call(
        kernel,
        out_shape=out_shape,
        in_specs=specs,
        out_specs=outs or [VMEM] * len(out_shape),
        scratch_shapes=list(scratch),
        input_output_aliases=aliases,
        compiler_params=pltpu.CompilerParams(vmem_limit_bytes=vmem),
    )(*operands)


def dma(count):
    return pltpu.SemaphoreType.DMA((count,))


def shards(sizes, specimen, probe_wave, amplitudes, offsets):
    nz, nx, nc = sizes
    size = probe_wave.shape[1]
    margin = size // 2
    tile = specimen.shape[1]
    npos = offsets.shape[0]
    ways = block_ways(nz, nx)
    xways = ways_of(nx)
    targets = block_targets(nz, nx)

    def send(value, target):
        return lax.ppermute(value, GROUP, permutation(sizes, target))

    def to_core(value):
        return lax.ppermute(value, "pos", PART_SWAP)

    shapes = block_shapes(nz, nx, tile)
    *blocks, note = call(
        functools.partial(halo_blocks_kernel, nz, nx),
        [f32(h + NOTE[0] + (FILL_ROWS if v is None else 0), w) for (h, w), (v, _) in zip(shapes, ways)] + [f32(*NOTE)],
        [HBM, HBM],
        offsets,
        specimen,
        scratch=[pltpu.SMEM(offsets.shape, jnp.int32), dma(len(ways) + 1)],
        vmem=KEEP_IN_HBM,
    )
    recv = [send(block, target) for block, target in zip(blocks, targets)]

    waves = jnp.asarray(dft_waves(size))
    late = (note, specimen, probe_wave, amplitudes)
    note, specimen_v, probe_v, amp_v, ta_v, tb_v = call(
        fetch_kernel,
        [jax.ShapeDtypeStruct(a.shape, a.dtype) for a in late]
        + [jax.ShapeDtypeStruct((2 * size, 2 * size), jnp.bfloat16)] * 2,
        [ANY] * len(late) + [VMEM],
        *late,
        waves,
        scratch=[dma(len(late))],
    )
    def patches_from(ours, after, *arrays):
        return call(
            functools.partial(patches_kernel, nz, nx, ours),
            [f32(npos, size, size)],
            [VMEM, ANY] + [VMEM] * (1 + len(arrays)),
            note,
            after,
            specimen_v,
            *arrays,
            scratch=[pltpu.VMEM((tile + size, tile + size), jnp.float32), NOTE_SMEM, dma(1)],
        )[0]

    def light_from(which, own, before, after):
        return call(
            functools.partial(light_kernel, npos, nz, nx, which),
            [f32(tile, tile)],
            [VMEM, VMEM, ANY if own else VMEM, ANY] + [VMEM] * len(which),
            note,
            probe_v,
            before,
            after,
            *[recv[k] for k in which],
            scratch=[
                pltpu.VMEM((size, size), jnp.float32),
                pltpu.VMEM((3 * tile, size), jnp.float32),
                *[NOTE_SMEM] * (own + len(which)),
                dma(own + len(which)),
            ],
        )[0]

    corners, along_z, along_x = packing_order(nz, nx)
    def packed(which, *after):
        chosen = [shapes[k] for k in which]
        return call(
            functools.partial(pack_kernel, chosen, len(after)),
            [f32(sum(h * w for h, w in chosen) // margin, margin)],
            [ANY] * len(after) + [VMEM] * len(which),
            *after,
            *[recv[k] for k in which],
        )[0]

    other_corners = to_core(packed(corners, probe_v))
    light = light_from(corners + along_x, True, probe_v, probe_v)
    packed_z = packed(along_z, light, other_corners)
    patches = patches_from(True, packed_z, *recv)
    patches_other = patches_from(False, patches, other_corners, to_core(packed_z), *[to_core(recv[k]) for k in along_x])
    own, other, probe_own, probe_other = call(
        positions_kernel,
        [f32(npos, size, size)] * 2 + [f32(size, size)] * 2,
        [VMEM] * 6,
        patches,
        patches_other,
        probe_v,
        amp_v,
        ta_v,
        tb_v,
    )
    other_note = to_core(note)
    light = light_from(along_z, False, light, own)

    zbits = [("z", 1 << k) for k in range(nz.bit_length() - 1)]
    xbits = [("x", 1 << k) for k in range(nx.bit_length() - 1)]
    orders = (xbits[:1] + zbits + xbits[1:], zbits + xbits)

    def stage(k):
        def target(z, x, c):
            axis, bit = orders[c][k]
            return (z ^ bit, x, c) if axis == "z" else (z, x ^ bit, c)

        return target

    half = f32(size // 2, size)
    keep, away, other = call(
        halve_kernel,
        [half] * 2 + [f32(npos, size, size)],
        [VMEM, VMEM, ANY, ANY],
        probe_own,
        to_core(probe_other),
        other,
        light,
        outs=[VMEM, VMEM, ANY],
        aliases={2: 2},
    )
    terms = to_core(other)
    middle, *beyond = call(
        functools.partial(gather_kernel, nx),
        [f32(tile + size, tile)] + [f32(tile + size, margin)] * len(xways),
        [VMEM] * 4 + [ANY],
        note,
        other_note,
        own,
        terms,
        keep,
        scratch=[pltpu.VMEM((tile + size, tile + size), jnp.float32), NOTE_SMEM, NOTE_SMEM, dma(2)],
    )
    (keep,) = call(add_kernel, [half], [VMEM] * 2 + [ANY], keep, send(away, stage(0)), middle)
    beside = [send(piece, targets[ways.index((None, way))]) for piece, way in zip(beyond, xways)]
    (keep,) = call(add_kernel, [half], [VMEM] * 2, keep, send(keep, stage(1)))
    center, *edges = call(
        functools.partial(fold_kernel, nz, nx),
        [f32(tile, tile)] + [f32(margin, tile)] * 2,
        [ANY] + [VMEM] * (1 + len(beside)),
        keep,
        middle,
        *beside,
        scratch=[pltpu.VMEM((tile + size, tile), jnp.float32)],
    )
    arrived = [send(edge, targets[ways.index((way, None))]) for way, edge in enumerate(edges)]
    for k in range(2, len(orders[0])):
        (keep,) = call(add_kernel, [half], [VMEM] * 2, keep, send(keep, stage(k)))
    updated = call(
        functools.partial(update_kernel, nz),
        [f32(tile // 2, tile)] * 2,
        [ANY] + [VMEM] * (4 + len(arrived)),
        keep,
        specimen_v,
        center,
        light,
        to_core(light),
        *arrived,
        scratch=[pltpu.VMEM((tile, tile), jnp.float32)],
    )
    away = send(keep, stage(0))
    new_specimen, done = call(
        specimen_kernel, [f32(2, tile, tile), f32(*NOTE)], [VMEM] * 4, *updated, *[to_core(u) for u in updated]
    )
    step_size = 1.0 / math.sqrt(npos * nz * nx * nc)
    (new_probe,) = call(
        functools.partial(probe_kernel, step_size),
        [f32(2, size, size)],
        [VMEM] * 5 + [ANY],
        probe_v,
        keep,
        away,
        to_core(keep),
        to_core(away),
        done,
    )
    return (new_specimen, new_probe)


def solution(mesh):
    sizes = tuple(mesh.shape[a] for a in GROUP)
    placed = (
        P(None, ("groups", "scanx"), "scany"),
        P(None, "groups", None),
        P(("groups", "scanx", "scany", "pos"), None, None),
        P(("groups", "scanx", "scany", "pos"), None),
    )
    return jax.shard_map(
        functools.partial(shards, sizes),
        mesh=mesh,
        in_specs=placed,
        out_specs=(P(None, ("groups", "scanx"), "scany"), P(None, "groups", None)),
        check_vma=False,
    )
```

```python
import functools
import math

import jax
import jax.numpy as jnp
import numpy as np
from jax import lax
from jax.experimental import pallas as pl
from jax.experimental.pallas import tpu as pltpu
from jax.sharding import PartitionSpec as P

GROUP = ("scanx", "scany", "pos")
KEEP_IN_HBM = 64 * 1024 * 1024 - 448 * 1024
PART_SWAP = ((0, 1), (1, 0))
VMEM = pl.BlockSpec(memory_space=pltpu.VMEM)
ANY = pl.BlockSpec(memory_space=pl.ANY)
HBM = pl.BlockSpec(memory_space=pltpu.HBM)
NOTE = (8, 128)
FILL_ROWS = 16
NOTE_SMEM = pltpu.SMEM(NOTE, jnp.float32)


def f32(*shape):
    return jax.ShapeDtypeStruct(shape, jnp.float32)


def ways_of(count):
    return (0,) if count == 2 else (0, 1)


def side_of(index, way):
    return lax.rem(index + way + 1, 2)


def valid_of(index, way, count):
    neighbour = index + 2 * side_of(index, way) - 1
    return jnp.logical_and(neighbour >= 0, neighbour < count)


def block_ways(nz, nx):
    xways, zways = ways_of(nx), (0, 1)
    order = [(None, w) for w in xways] + [(w, None) for w in zways]
    return order + [(v, w) for w in xways for v in zways]


def block_places(z, x, nz, nx, origin, extent, margin):
    places = []
    for zway, xway in block_ways(nz, nx):
        span = []
        for index, way in ((z, zway), (x, xway)):
            if way is None:
                span.append(pl.ds(origin, 2 * margin))
            else:
                span.append(pl.ds(pl.multiple_of(side_of(index, way) * extent, margin), margin))
        places.append(tuple(span))
    return places


def block_shapes(nz, nx, tile):
    return [tuple(tile if way is None else tile // 2 for way in ways) for ways in block_ways(nz, nx)]


def packing_order(nz, nx):
    ways = block_ways(nz, nx)
    kinds = [(v is not None, w is not None) for v, w in ways]
    return [[k for k, kind in enumerate(kinds) if kind == which] for which in ((True, True), (True, False), (False, True))]


def packed_places(shapes):
    lanes = min(min(shape) for shape in shapes)
    at, places = 0, []
    for height, width in shapes:
        places.append([])
        for col in range(0, width, lanes):
            places[-1].append((at, col, height))
            at += height
    return places


def block_valid(z, x, nz, nx):
    result = []
    for zway, xway in block_ways(nz, nx):
        ok = True
        if zway is not None:
            ok = valid_of(z, zway, nz)
        if xway is not None:
            ok = jnp.logical_and(ok, valid_of(x, xway, nx))
        result.append(ok)
    return result


def block_targets(nz, nx):
    def step(index, way, count):
        if way is None:
            return index
        to = index + (1 if (index + way) % 2 == 0 else -1)
        return to if 0 <= to < count else None

    def target(ways, z, x, c):
        tz, tx = step(z, ways[0], nz), step(x, ways[1], nx)
        return (z, x, 1 - c) if tz is None or tx is None else (tz, tx, c)

    return [functools.partial(target, ways) for ways in block_ways(nz, nx)]


def permutation(sizes, target):
    nz, nx, nc = sizes
    pairs = []
    for z in range(nz):
        for x in range(nx):
            for c in range(nc):
                tz, tx, tc = target(z, x, c)
                pairs.append(((z * nx + x) * nc + c, (tz * nx + tx) * nc + tc))
    return pairs


def dft_waves(length):
    index = np.arange(length, dtype=np.int32)
    phase = (index[:, None] * index[None, :]) % length
    angle = phase.astype(np.float32) * np.float32(2.0 * math.pi / length)
    scale = np.float32(1.0 / math.sqrt(length))
    sine = np.sin(angle) * scale
    return np.stack([np.cos(angle) * scale, sine, -sine]).astype(jnp.bfloat16)


def aligned(row):
    return pl.multiple_of((row // 8) * 8, 8), lax.rem(row, 8)


def rows_up(block, shift):
    count, width = block.shape
    groups = pltpu.roll(block.reshape(count // 8, 8, width), lax.rem(8 - shift, 8), axis=1)
    at = lax.broadcasted_iota(jnp.int32, (count // 8 - 1, 8, width), 1)
    return jnp.where(at < 8 - shift, groups[:-1], groups[1:]).reshape(count - 8, width)


def rows_down(block, shift):
    count, width = block.shape
    groups = pltpu.roll(block.reshape(count // 8, 8, width), shift, axis=1)
    blank = jnp.zeros((1, 8, width), block.dtype)
    at = lax.broadcasted_iota(jnp.int32, (count // 8 + 1, 8, width), 1)
    early = jnp.concatenate([groups, blank])
    late = jnp.concatenate([blank, groups])
    return jnp.where(at >= shift, early, late).reshape(count + 8, width)


def halo_blocks_kernel(nz, nx, off_hbm, spec_ref, *refs):
    z, x, c = (lax.axis_index(a) for a in GROUP)
    *outs, note_ref, off_ref, sems = refs
    tile = spec_ref.shape[1]
    margin = tile // 2
    off_copy = pltpu.make_async_copy(off_hbm, off_ref, sems.at[len(outs)])
    off_copy.start()
    copies = []
    places = block_places(z, x, nz, nx, 0, margin, margin)
    for k, (out, (height, _), (rows, cols)) in enumerate(zip(outs, block_shapes(nz, nx, tile), places)):
        copies.append(pltpu.make_async_copy(spec_ref.at[c, rows, cols], out.at[pl.ds(0, height), :], sems.at[k]))
        copies[-1].start()
    off_copy.wait()
    lane = lax.broadcasted_iota(jnp.int32, NOTE, 1)
    note = jnp.zeros(NOTE, jnp.float32)
    for j in range(off_ref.shape[0]):
        for k in range(2):
            note = jnp.where(lane == 2 * j + k, off_ref[j, k].astype(jnp.float32), note)
    note_ref[...] = note
    for out, (height, width) in zip(outs, block_shapes(nz, nx, tile)):
        fill = out.shape[0] - NOTE[0] - height
        if fill:
            out[height : height + fill, :] = jnp.zeros((fill, width), jnp.float32)
        out[height + fill :, : NOTE[1]] = note
    for copy in copies:
        copy.wait()


def read_notes(notes, smems, sems):
    copies = [pltpu.make_async_copy(note, smem, sems.at[k]) for k, (note, smem) in enumerate(zip(notes, smems))]
    for copy in copies:
        copy.start()
    return copies


def note_of(block):
    return block.at[pl.ds(block.shape[0] - NOTE[0], NOTE[0]), pl.ds(0, NOTE[1])]


def offset_in(note, j):
    return note[0, 2 * j].astype(jnp.int32), note[0, 2 * j + 1].astype(jnp.int32)


def fetch_kernel(*refs):
    *refs, table_a, table_b, sems = refs
    count = len(refs) // 2
    *sources, waves = refs[: count + 1]
    copies = [pltpu.make_async_copy(src, refs[count + 1 + k], sems.at[k]) for k, src in enumerate(sources)]
    for copy in copies:
        copy.start()
    cosine, sine, minus = (waves[k] for k in range(3))
    size = cosine.shape[0]
    for table, blocks in ((table_a, (cosine, sine, minus, cosine)), (table_b, (cosine, minus, sine, cosine))):
        for k, block in enumerate(blocks):
            at, left = k // 2 * size, k % 2 * size
            table[at : at + size, left : left + size] = block
    for copy in copies:
        copy.wait()


def cut_patches(note, padded, out):
    npos, size, _ = out.shape
    lane = lax.broadcasted_iota(jnp.int32, (size + 8, size), 1)
    for j in range(npos):
        row, col = offset_in(note, j)
        base, shift = aligned(row)
        rows = padded[pl.ds(base, size + 8), :]
        mixed = rows_up(jnp.where(lane >= col, rows[:, :size], rows[:, size:]), shift)
        out[j] = pltpu.roll(mixed, lax.rem(size - col, size), axis=1)


def patches_kernel(nz, nx, ours, note_ref, unused_ref, spec_ref, *refs):
    z, x, c = (lax.axis_index(a) for a in GROUP)
    *blocks, out, padded, note, sems = refs
    copies = read_notes([note_ref], [note], sems)
    tile = spec_ref.shape[1]
    margin = (padded.shape[0] - tile) // 2
    padded[margin : margin + tile, margin : margin + tile] = spec_ref[c if ours else 1 - c]
    if len(ways_of(nx)) == 1:
        far_cols = pl.ds(pl.multiple_of((1 - side_of(x, 0)) * (margin + tile), margin), margin)
        padded[:, far_cols] = jnp.zeros((padded.shape[0], margin), jnp.float32)
    places = block_places(z, x, nz, nx, margin, margin + tile, margin)
    shapes = block_shapes(nz, nx, tile)
    corners, along_z, along_x = packing_order(nz, nx)
    pieces = {k: [(block, 0)] for k, block in zip(along_x, blocks[2:])}
    for which, array in zip((corners, along_z), blocks):
        for k, places_of in zip(which, packed_places([shapes[k] for k in which])):
            pieces[k] = [(array, at) for at, _, _ in places_of]
    for k, ((height, width), (rows, cols), ok) in enumerate(zip(shapes, places, block_valid(z, x, nz, nx))):

        @pl.when(ok)
        def _():
            if ours:
                padded[rows, cols] = blocks[k][:height, :]
            else:
                parts = [array[at : at + height, :] for array, at in pieces[k]]
                padded[rows, cols] = parts[0] if len(parts) == 1 else jnp.concatenate(parts, axis=1)

        @pl.when(jnp.logical_not(ok))
        def _():
            padded[rows, cols] = jnp.zeros((height, width), jnp.float32)

    copies[0].wait()
    cut_patches(note, padded, out)


def pack_kernel(shapes, waits, *refs):
    *blocks, out = refs[waits:]
    for block, pieces in zip(blocks, packed_places(shapes)):
        for at, col, height in pieces:
            out[at : at + height, :] = block[:height, col : col + out.shape[1]]


def positions_kernel(patch_ref, patch_other_ref, probe_ref, amp_ref, ta_ref, tb_ref, own_ref, other_ref, probe_own_ref, probe_other_ref):
    first = lax.axis_index("pos") == 0
    npos, size, _ = patch_ref.shape
    table_a = ta_ref[...]
    table_b = tb_ref[...]
    probe_real = probe_ref[0]
    probe_imag = probe_ref[1]

    def side_by_side(both):
        return jnp.concatenate([both[:size], both[size:]], axis=1)

    grad_real = jnp.zeros((size, size), jnp.float32)
    grad_imag = jnp.zeros((size, size), jnp.float32)
    for j in range(npos):
        patch_real = jnp.where(first, patch_ref[j], patch_other_ref[j])
        patch_imag = jnp.where(first, patch_other_ref[j], patch_ref[j])
        exit_real = probe_real * patch_real - probe_imag * patch_imag
        exit_imag = probe_real * patch_imag + probe_imag * patch_real
        wave = jnp.concatenate([exit_real, exit_imag], axis=0).astype(jnp.bfloat16)
        half = jnp.dot(table_a, wave, preferred_element_type=jnp.float32).astype(jnp.bfloat16)
        far = jnp.dot(side_by_side(half), table_b, preferred_element_type=jnp.float32)
        far_real, far_imag = far[:, :size], far[:, size:]
        power = far_real * far_real + far_imag * far_imag
        ratio = amp_ref[j].astype(jnp.float32) * jnp.minimum(lax.rsqrt(power), 1.0 / 0.2)
        projected = jnp.concatenate([far_real * ratio, far_imag * ratio], axis=0).astype(jnp.bfloat16)
        back_half = jnp.dot(table_b, projected, preferred_element_type=jnp.float32).astype(jnp.bfloat16)
        back = jnp.dot(side_by_side(back_half), table_a, preferred_element_type=jnp.float32)
        diff_real = back[:, :size] - exit_real
        diff_imag = back[:, size:] - exit_imag
        term_real = probe_real * diff_real + probe_imag * diff_imag
        term_imag = probe_real * diff_imag - probe_imag * diff_real
        own_ref[j] = jnp.where(first, term_real, term_imag)
        other_ref[j] = jnp.where(first, term_imag, term_real)
        grad_real += patch_real * diff_real + patch_imag * diff_imag
        grad_imag += patch_real * diff_imag - patch_imag * diff_real
    probe_own_ref[...] = jnp.where(first, grad_real, grad_imag)
    probe_other_ref[...] = jnp.where(first, grad_imag, grad_real)


def half_of(z, x, c):
    return jnp.where(c == 0, lax.rem(x, 2), lax.rem(z, 2))


def halve_kernel(own_ref, recv_ref, unused_ref, unused_light_ref, keep_ref, give_ref, handed_on_ref):
    half = half_of(*(lax.axis_index(a) for a in GROUP))
    rows = keep_ref.shape[0]
    for at, out in ((half, keep_ref), (1 - half, give_ref)):
        span = pl.ds(pl.multiple_of(at * rows, rows), rows)
        out[...] = own_ref[span, :] + recv_ref[span, :]


def gather_kernel(nx, note_ref, other_note_ref, own_ref, recv_ref, unused_ref, middle_ref, *refs):
    x = lax.axis_index("scany")
    *blocks, grad, note, other_note, sems = refs
    copies = read_notes([note_ref, other_note_ref], [note, other_note], sems)
    npos, size, _ = own_ref.shape
    lane = lax.broadcasted_iota(jnp.int32, (size + 8, size), 1)
    grad[...] = jnp.zeros_like(grad)
    for copy, offs, terms in zip(copies, (note, other_note), (own_ref, recv_ref)):
        copy.wait()
        for j in range(npos):
            row, col = offset_in(offs, j)
            base, shift = aligned(row)
            term = rows_down(pltpu.roll(terms[j], col, axis=1), shift)
            low = jnp.where(lane >= col, term, 0.0)
            rows = pl.ds(base, size + 8)
            grad[rows, :size] += low
            grad[rows, size:] += term - low
    tile = middle_ref.shape[1]
    margin = (middle_ref.shape[0] - tile) // 2
    middle_ref[...] = grad[:, margin : margin + tile]
    for block, way in zip(blocks, ways_of(nx)):
        block[...] = grad[:, pl.ds(pl.multiple_of(side_of(x, way) * (margin + tile), margin), margin)]


def fold_kernel(nz, nx, unused_ref, middle_ref, *refs):
    z, x = lax.axis_index("scanx"), lax.axis_index("scany")
    ways = ways_of(nx)
    blocks, (center_ref, *edges, total) = refs[: len(ways)], refs[len(ways) :]
    tile = center_ref.shape[0]
    margin = (middle_ref.shape[0] - tile) // 2
    total[...] = middle_ref[...]
    for block, way in zip(blocks, ways):
        at = pl.multiple_of(side_of(x, way) * (tile - margin), margin)

        @pl.when(valid_of(x, way, nx))
        def _():
            total[:, pl.ds(at, margin)] += block[...]

    center_ref[...] = total[margin : margin + tile, :]
    for way, edge in enumerate(edges):
        edge[...] = total[pl.ds(pl.multiple_of(side_of(z, way) * (margin + tile), margin), margin), :]


def update_kernel(nz, unused_ref, spec_ref, center_ref, light_ref, other_light_ref, edge_a, edge_b, *refs):
    z, c = lax.axis_index("scanx"), lax.axis_index("pos")
    upper_ref, lower_ref, grad = refs
    tile = center_ref.shape[0]
    grad[...] = center_ref[...]
    for way, edge in enumerate((edge_a, edge_b)):
        margin = edge.shape[0]
        at = pl.multiple_of(side_of(z, way) * (tile - margin), margin)

        @pl.when(valid_of(z, way, nz))
        def _():
            grad[pl.ds(at, margin), :] += edge[...]

    for at, out in ((0, upper_ref), (tile // 2, lower_ref)):
        span = pl.ds(at, tile // 2)
        out[...] = spec_ref[c, span, :] + grad[span, :] / (light_ref[span, :] + other_light_ref[span, :] + 1.0)


def add_kernel(a_ref, b_ref, *refs):
    refs[-1][...] = a_ref[...] + b_ref[...]


def specimen_kernel(upper_ref, lower_ref, other_upper_ref, other_lower_ref, out_ref, done_ref):
    c = lax.axis_index("pos")
    rows = upper_ref.shape[0]
    for part, upper, lower in ((c, upper_ref, lower_ref), (1 - c, other_upper_ref, other_lower_ref)):
        out_ref[part, :rows, :] = upper[...]
        out_ref[part, rows:, :] = lower[...]
    done_ref[...] = jnp.zeros(done_ref.shape, done_ref.dtype)


def probe_kernel(step_size, probe_ref, keep_ref, away_ref, keep_other_ref, away_other_ref, unused_ref, out_ref):
    z, x, c = (lax.axis_index(a) for a in GROUP)
    rows = keep_ref.shape[0]
    for part, keep, away in ((c, keep_ref, away_ref), (1 - c, keep_other_ref, away_other_ref)):
        half = half_of(z, x, part)
        for at, term in ((half, keep), (1 - half, away)):
            span = pl.ds(pl.multiple_of(at * rows, rows), rows)
            out_ref[part, span, :] = probe_ref[part, span, :] + term[...] * step_size


def light_kernel(npos, nz, nx, which, note_ref, probe_ref, before_ref, unused_ref, *refs):
    z, x, c = (lax.axis_index(a) for a in GROUP)
    blocks, (light_ref, power_ref, total, *notes, sems) = refs[: len(which)], refs[len(which) :]
    own = len(notes) > len(which)
    copies = read_notes(([note_ref] if own else []) + [note_of(b) for b in blocks], notes, sems)
    size = probe_ref.shape[1]
    margin = size // 2
    tile = light_ref.shape[0]
    power_ref[...] = probe_ref[0] * probe_ref[0] + probe_ref[1] * probe_ref[1]
    total[...] = jnp.zeros_like(total)
    lane = lax.broadcasted_iota(jnp.int32, (size, size), 1)

    def add(row, col, ok):
        ok = jnp.logical_and(ok, jnp.logical_and(jnp.abs(row) < tile, jnp.abs(col) < tile))

        @pl.when(ok)
        def _():
            base, shift = aligned(row + tile)
            moved = pltpu.roll(power_ref[...], lax.rem(col + size, size), axis=1)
            keep = jnp.logical_and(lane >= col, lane < col + size)
            total[pl.ds(base, size + 8), :] += rows_down(jnp.where(keep, moved, 0.0), shift)

    ways, valid = block_ways(nz, nx), block_valid(z, x, nz, nx)
    places = [((None, None), True)] * own + [(ways[k], valid[k]) for k in which]
    for copy, note, ((zway, xway), ok) in zip(copies, notes, places):
        copy.wait()
        down = 0 if zway is None else (2 * side_of(z, zway) - 1) * tile
        right = 0 if xway is None else (2 * side_of(x, xway) - 1) * tile
        for j in range(npos):
            row, col = offset_in(note, j)
            add(row + down - margin, col + right - margin, ok)
    if own:
        light_ref[...] = total[tile : 2 * tile, :]
    else:
        light_ref[...] = before_ref[...] + total[tile : 2 * tile, :]


def call(kernel, out_shape, specs, *operands, scratch=(), outs=None, aliases={}, vmem=16 * 1024 * 1024):
    return pl.pallas_call(
        kernel,
        out_shape=out_shape,
        in_specs=specs,
        out_specs=outs or [VMEM] * len(out_shape),
        scratch_shapes=list(scratch),
        input_output_aliases=aliases,
        compiler_params=pltpu.CompilerParams(vmem_limit_bytes=vmem),
    )(*operands)


def dma(count):
    return pltpu.SemaphoreType.DMA((count,))


def shards(sizes, specimen, probe_wave, amplitudes, offsets):
    nz, nx, nc = sizes
    size = probe_wave.shape[1]
    margin = size // 2
    tile = specimen.shape[1]
    npos = offsets.shape[0]
    ways = block_ways(nz, nx)
    xways = ways_of(nx)
    targets = block_targets(nz, nx)

    def send(value, target):
        return lax.ppermute(value, GROUP, permutation(sizes, target))

    def to_core(value):
        return lax.ppermute(value, "pos", PART_SWAP)

    shapes = block_shapes(nz, nx, tile)
    *blocks, note = call(
        functools.partial(halo_blocks_kernel, nz, nx),
        [f32(h + NOTE[0] + (FILL_ROWS if v is None else 0), w) for (h, w), (v, _) in zip(shapes, ways)] + [f32(*NOTE)],
        [HBM, HBM],
        offsets,
        specimen,
        scratch=[pltpu.SMEM(offsets.shape, jnp.int32), dma(len(ways) + 1)],
        vmem=KEEP_IN_HBM,
    )
    recv = [send(block, target) for block, target in zip(blocks, targets)]

    waves = jnp.asarray(dft_waves(size))
    late = (note, specimen, probe_wave, amplitudes)
    note, specimen_v, probe_v, amp_v, ta_v, tb_v = call(
        fetch_kernel,
        [jax.ShapeDtypeStruct(a.shape, a.dtype) for a in late]
        + [jax.ShapeDtypeStruct((2 * size, 2 * size), jnp.bfloat16)] * 2,
        [ANY] * len(late) + [VMEM],
        *late,
        waves,
        scratch=[dma(len(late))],
    )
    def patches_from(ours, after, *arrays):
        return call(
            functools.partial(patches_kernel, nz, nx, ours),
            [f32(npos, size, size)],
            [VMEM, ANY] + [VMEM] * (1 + len(arrays)),
            note,
            after,
            specimen_v,
            *arrays,
            scratch=[pltpu.VMEM((tile + size, tile + size), jnp.float32), NOTE_SMEM, dma(1)],
        )[0]

    def light_from(which, own, before, after):
        return call(
            functools.partial(light_kernel, npos, nz, nx, which),
            [f32(tile, tile)],
            [VMEM, VMEM, ANY if own else VMEM, ANY] + [VMEM] * len(which),
            note,
            probe_v,
            before,
            after,
            *[recv[k] for k in which],
            scratch=[
                pltpu.VMEM((size, size), jnp.float32),
                pltpu.VMEM((3 * tile, size), jnp.float32),
                *[NOTE_SMEM] * (own + len(which)),
                dma(own + len(which)),
            ],
        )[0]

    corners, along_z, along_x = packing_order(nz, nx)
    def packed(which, *after):
        chosen = [shapes[k] for k in which]
        return call(
            functools.partial(pack_kernel, chosen, len(after)),
            [f32(sum(h * w for h, w in chosen) // margin, margin)],
            [ANY] * len(after) + [VMEM] * len(which),
            *after,
            *[recv[k] for k in which],
        )[0]

    packed_corners = packed(corners, probe_v, *[recv[k] for k in along_x])
    other_corners = to_core(packed_corners)
    light = light_from(corners + along_x, True, packed_corners, packed_corners)
    packed_z = packed(along_z, light, other_corners)
    patches = patches_from(True, packed_z, *recv)
    patches_other = patches_from(False, patches, other_corners, to_core(packed_z), *[to_core(recv[k]) for k in along_x])
    own, other, probe_own, probe_other = call(
        positions_kernel,
        [f32(npos, size, size)] * 2 + [f32(size, size)] * 2,
        [VMEM] * 6,
        patches,
        patches_other,
        probe_v,
        amp_v,
        ta_v,
        tb_v,
    )
    other_note = to_core(note)
    light = light_from(along_z, False, light, own)

    zbits = [("z", 1 << k) for k in range(nz.bit_length() - 1)]
    xbits = [("x", 1 << k) for k in range(nx.bit_length() - 1)]
    orders = (xbits[:1] + zbits + xbits[1:], zbits + xbits)

    def stage(k):
        def target(z, x, c):
            axis, bit = orders[c][k]
            return (z ^ bit, x, c) if axis == "z" else (z, x ^ bit, c)

        return target

    half = f32(size // 2, size)
    keep, away, other = call(
        halve_kernel,
        [half] * 2 + [f32(npos, size, size)],
        [VMEM, VMEM, ANY, ANY],
        probe_own,
        to_core(probe_other),
        other,
        light,
        outs=[VMEM, VMEM, ANY],
        aliases={2: 2},
    )
    terms = to_core(other)
    middle, *beyond = call(
        functools.partial(gather_kernel, nx),
        [f32(tile + size, tile)] + [f32(tile + size, margin)] * len(xways),
        [VMEM] * 4 + [ANY],
        note,
        other_note,
        own,
        terms,
        keep,
        scratch=[pltpu.VMEM((tile + size, tile + size), jnp.float32), NOTE_SMEM, NOTE_SMEM, dma(2)],
    )
    (keep,) = call(add_kernel, [half], [VMEM] * 2 + [ANY], keep, send(away, stage(0)), middle)
    beside = [send(piece, targets[ways.index((None, way))]) for piece, way in zip(beyond, xways)]
    (keep,) = call(add_kernel, [half], [VMEM] * 2, keep, send(keep, stage(1)))
    center, *edges = call(
        functools.partial(fold_kernel, nz, nx),
        [f32(tile, tile)] + [f32(margin, tile)] * 2,
        [ANY] + [VMEM] * (1 + len(beside)),
        keep,
        middle,
        *beside,
        scratch=[pltpu.VMEM((tile + size, tile), jnp.float32)],
    )
    arrived = [send(edge, targets[ways.index((way, None))]) for way, edge in enumerate(edges)]
    for k in range(2, len(orders[0])):
        (keep,) = call(add_kernel, [half], [VMEM] * 2, keep, send(keep, stage(k)))
    updated = call(
        functools.partial(update_kernel, nz),
        [f32(tile // 2, tile)] * 2,
        [ANY] + [VMEM] * (4 + len(arrived)),
        keep,
        specimen_v,
        center,
        light,
        to_core(light),
        *arrived,
        scratch=[pltpu.VMEM((tile, tile), jnp.float32)],
    )
    away = send(keep, stage(0))
    new_specimen, done = call(
        specimen_kernel, [f32(2, tile, tile), f32(*NOTE)], [VMEM] * 4, *updated, *[to_core(u) for u in updated]
    )
    step_size = 1.0 / math.sqrt(npos * nz * nx * nc)
    (new_probe,) = call(
        functools.partial(probe_kernel, step_size),
        [f32(2, size, size)],
        [VMEM] * 5 + [ANY],
        probe_v,
        keep,
        away,
        to_core(keep),
        to_core(away),
        done,
    )
    return (new_specimen, new_probe)


def solution(mesh):
    sizes = tuple(mesh.shape[a] for a in GROUP)
    placed = (
        P(None, ("groups", "scanx"), "scany"),
        P(None, "groups", None),
        P(("groups", "scanx", "scany", "pos"), None, None),
        P(("groups", "scanx", "scany", "pos"), None),
    )
    return jax.shard_map(
        functools.partial(shards, sizes),
        mesh=mesh,
        in_specs=placed,
        out_specs=(P(None, ("groups", "scanx"), "scany"), P(None, "groups", None)),
        check_vma=False,
    )
```

```python
import functools
import math

import jax
import jax.numpy as jnp
import numpy as np
from jax import lax
from jax.experimental import pallas as pl
from jax.experimental.pallas import tpu as pltpu
from jax.sharding import PartitionSpec as P

GROUP = ("scanx", "scany", "pos")
KEEP_IN_HBM = 64 * 1024 * 1024 - 448 * 1024
PART_SWAP = ((0, 1), (1, 0))
VMEM = pl.BlockSpec(memory_space=pltpu.VMEM)
ANY = pl.BlockSpec(memory_space=pl.ANY)
HBM = pl.BlockSpec(memory_space=pltpu.HBM)
NOTE = (8, 128)
FILL_ROWS = 16
NOTE_SMEM = pltpu.SMEM(NOTE, jnp.float32)


def f32(*shape):
    return jax.ShapeDtypeStruct(shape, jnp.float32)


def ways_of(count):
    return (0,) if count == 2 else (0, 1)


def side_of(index, way):
    return lax.rem(index + way + 1, 2)


def valid_of(index, way, count):
    neighbour = index + 2 * side_of(index, way) - 1
    return jnp.logical_and(neighbour >= 0, neighbour < count)


def block_ways(nz, nx):
    xways, zways = ways_of(nx), (0, 1)
    order = [(None, w) for w in xways] + [(w, None) for w in zways]
    return order + [(v, w) for w in xways for v in zways]


def block_places(z, x, nz, nx, origin, extent, margin):
    places = []
    for zway, xway in block_ways(nz, nx):
        span = []
        for index, way in ((z, zway), (x, xway)):
            if way is None:
                span.append(pl.ds(origin, 2 * margin))
            else:
                span.append(pl.ds(pl.multiple_of(side_of(index, way) * extent, margin), margin))
        places.append(tuple(span))
    return places


def block_shapes(nz, nx, tile):
    return [tuple(tile if way is None else tile // 2 for way in ways) for ways in block_ways(nz, nx)]


def packing_order(nz, nx):
    ways = block_ways(nz, nx)
    kinds = [(v is not None, w is not None) for v, w in ways]
    return [[k for k, kind in enumerate(kinds) if kind == which] for which in ((True, True), (True, False), (False, True))]


def packed_places(shapes):
    lanes = min(min(shape) for shape in shapes)
    at, places = 0, []
    for height, width in shapes:
        places.append([])
        for col in range(0, width, lanes):
            places[-1].append((at, col, height))
            at += height
    return places


def block_valid(z, x, nz, nx):
    result = []
    for zway, xway in block_ways(nz, nx):
        ok = True
        if zway is not None:
            ok = valid_of(z, zway, nz)
        if xway is not None:
            ok = jnp.logical_and(ok, valid_of(x, xway, nx))
        result.append(ok)
    return result


def block_targets(nz, nx):
    def step(index, way, count):
        if way is None:
            return index
        to = index + (1 if (index + way) % 2 == 0 else -1)
        return to if 0 <= to < count else None

    def target(ways, z, x, c):
        tz, tx = step(z, ways[0], nz), step(x, ways[1], nx)
        return (z, x, 1 - c) if tz is None or tx is None else (tz, tx, c)

    return [functools.partial(target, ways) for ways in block_ways(nz, nx)]


def permutation(sizes, target):
    nz, nx, nc = sizes
    pairs = []
    for z in range(nz):
        for x in range(nx):
            for c in range(nc):
                tz, tx, tc = target(z, x, c)
                pairs.append(((z * nx + x) * nc + c, (tz * nx + tx) * nc + tc))
    return pairs


def dft_waves(length):
    index = np.arange(length, dtype=np.int32)
    phase = (index[:, None] * index[None, :]) % length
    angle = phase.astype(np.float32) * np.float32(2.0 * math.pi / length)
    scale = np.float32(1.0 / math.sqrt(length))
    sine = np.sin(angle) * scale
    return np.stack([np.cos(angle) * scale, sine, -sine]).astype(jnp.bfloat16)


def aligned(row):
    return pl.multiple_of((row // 8) * 8, 8), lax.rem(row, 8)


def rows_up(block, shift):
    count, width = block.shape
    groups = pltpu.roll(block.reshape(count // 8, 8, width), lax.rem(8 - shift, 8), axis=1)
    at = lax.broadcasted_iota(jnp.int32, (count // 8 - 1, 8, width), 1)
    return jnp.where(at < 8 - shift, groups[:-1], groups[1:]).reshape(count - 8, width)


def rows_down(block, shift):
    count, width = block.shape
    groups = pltpu.roll(block.reshape(count // 8, 8, width), shift, axis=1)
    blank = jnp.zeros((1, 8, width), block.dtype)
    at = lax.broadcasted_iota(jnp.int32, (count // 8 + 1, 8, width), 1)
    early = jnp.concatenate([groups, blank])
    late = jnp.concatenate([blank, groups])
    return jnp.where(at >= shift, early, late).reshape(count + 8, width)


def halo_blocks_kernel(nz, nx, off_hbm, spec_ref, *refs):
    z, x, c = (lax.axis_index(a) for a in GROUP)
    *outs, note_ref, off_ref, sems = refs
    tile = spec_ref.shape[1]
    margin = tile // 2
    off_copy = pltpu.make_async_copy(off_hbm, off_ref, sems.at[len(outs)])
    off_copy.start()
    copies = []
    places = block_places(z, x, nz, nx, 0, margin, margin)
    for k, (out, (height, _), (rows, cols)) in enumerate(zip(outs, block_shapes(nz, nx, tile), places)):
        copies.append(pltpu.make_async_copy(spec_ref.at[c, rows, cols], out.at[pl.ds(0, height), :], sems.at[k]))
        copies[-1].start()
    off_copy.wait()
    lane = lax.broadcasted_iota(jnp.int32, NOTE, 1)
    note = jnp.zeros(NOTE, jnp.float32)
    for j in range(off_ref.shape[0]):
        for k in range(2):
            note = jnp.where(lane == 2 * j + k, off_ref[j, k].astype(jnp.float32), note)
    note_ref[...] = note
    for out, (height, width) in zip(outs, block_shapes(nz, nx, tile)):
        fill = out.shape[0] - NOTE[0] - height
        if fill:
            out[height : height + fill, :] = jnp.zeros((fill, width), jnp.float32)
        out[height + fill :, : NOTE[1]] = note
    for copy in copies:
        copy.wait()


def read_notes(notes, smems, sems):
    copies = [pltpu.make_async_copy(note, smem, sems.at[k]) for k, (note, smem) in enumerate(zip(notes, smems))]
    for copy in copies:
        copy.start()
    return copies


def note_of(block):
    return block.at[pl.ds(block.shape[0] - NOTE[0], NOTE[0]), pl.ds(0, NOTE[1])]


def offset_in(note, j):
    return note[0, 2 * j].astype(jnp.int32), note[0, 2 * j + 1].astype(jnp.int32)


def fetch_kernel(*refs):
    *refs, table_a, table_b, sems = refs
    count = len(refs) // 2
    *sources, waves = refs[: count + 1]
    copies = [pltpu.make_async_copy(src, refs[count + 1 + k], sems.at[k]) for k, src in enumerate(sources)]
    for copy in copies:
        copy.start()
    cosine, sine, minus = (waves[k] for k in range(3))
    size = cosine.shape[0]
    for table, blocks in ((table_a, (cosine, sine, minus, cosine)), (table_b, (cosine, minus, sine, cosine))):
        for k, block in enumerate(blocks):
            at, left = k // 2 * size, k % 2 * size
            table[at : at + size, left : left + size] = block
    for copy in copies:
        copy.wait()


def cut_patches(note, padded, out):
    npos, size, _ = out.shape
    lane = lax.broadcasted_iota(jnp.int32, (size + 8, size), 1)
    for j in range(npos):
        row, col = offset_in(note, j)
        base, shift = aligned(row)
        rows = padded[pl.ds(base, size + 8), :]
        mixed = rows_up(jnp.where(lane >= col, rows[:, :size], rows[:, size:]), shift)
        out[j] = pltpu.roll(mixed, lax.rem(size - col, size), axis=1)


def patches_kernel(nz, nx, ours, note_ref, unused_ref, spec_ref, *refs):
    z, x, c = (lax.axis_index(a) for a in GROUP)
    *blocks, out, padded, note, sems = refs
    copies = read_notes([note_ref], [note], sems)
    tile = spec_ref.shape[1]
    margin = (padded.shape[0] - tile) // 2
    padded[margin : margin + tile, margin : margin + tile] = spec_ref[c if ours else 1 - c]
    if len(ways_of(nx)) == 1:
        far_cols = pl.ds(pl.multiple_of((1 - side_of(x, 0)) * (margin + tile), margin), margin)
        padded[:, far_cols] = jnp.zeros((padded.shape[0], margin), jnp.float32)
    places = block_places(z, x, nz, nx, margin, margin + tile, margin)
    shapes = block_shapes(nz, nx, tile)
    corners, along_z, along_x = packing_order(nz, nx)
    pieces = {k: [(block, 0)] for k, block in zip(along_x, blocks[2:])}
    for which, array in zip((corners, along_z), blocks):
        for k, places_of in zip(which, packed_places([shapes[k] for k in which])):
            pieces[k] = [(array, at) for at, _, _ in places_of]
    for k, ((height, width), (rows, cols), ok) in enumerate(zip(shapes, places, block_valid(z, x, nz, nx))):

        @pl.when(ok)
        def _():
            if ours:
                padded[rows, cols] = blocks[k][:height, :]
            else:
                parts = [array[at : at + height, :] for array, at in pieces[k]]
                padded[rows, cols] = parts[0] if len(parts) == 1 else jnp.concatenate(parts, axis=1)

        @pl.when(jnp.logical_not(ok))
        def _():
            padded[rows, cols] = jnp.zeros((height, width), jnp.float32)

    copies[0].wait()
    cut_patches(note, padded, out)


def pack_kernel(shapes, waits, *refs):
    *blocks, out = refs[waits:]
    for block, pieces in zip(blocks, packed_places(shapes)):
        for at, col, height in pieces:
            out[at : at + height, :] = block[:height, col : col + out.shape[1]]


def positions_kernel(patch_ref, patch_other_ref, probe_ref, amp_ref, ta_ref, tb_ref, own_ref, other_ref, probe_own_ref, probe_other_ref):
    first = lax.axis_index("pos") == 0
    npos, size, _ = patch_ref.shape
    table_a = ta_ref[...]
    table_b = tb_ref[...]
    probe_real = probe_ref[0]
    probe_imag = probe_ref[1]

    def side_by_side(both):
        return jnp.concatenate([both[:size], both[size:]], axis=1)

    grad_real = jnp.zeros((size, size), jnp.float32)
    grad_imag = jnp.zeros((size, size), jnp.float32)
    for j in range(npos):
        patch_real = jnp.where(first, patch_ref[j], patch_other_ref[j])
        patch_imag = jnp.where(first, patch_other_ref[j], patch_ref[j])
        exit_real = probe_real * patch_real - probe_imag * patch_imag
        exit_imag = probe_real * patch_imag + probe_imag * patch_real
        wave = jnp.concatenate([exit_real, exit_imag], axis=0).astype(jnp.bfloat16)
        half = jnp.dot(table_a, wave, preferred_element_type=jnp.float32).astype(jnp.bfloat16)
        far = jnp.dot(side_by_side(half), table_b, preferred_element_type=jnp.float32)
        far_real, far_imag = far[:, :size], far[:, size:]
        power = far_real * far_real + far_imag * far_imag
        ratio = amp_ref[j].astype(jnp.float32) * jnp.minimum(lax.rsqrt(power), 1.0 / 0.2)
        projected = jnp.concatenate([far_real * ratio, far_imag * ratio], axis=0).astype(jnp.bfloat16)
        back_half = jnp.dot(table_b, projected, preferred_element_type=jnp.float32).astype(jnp.bfloat16)
        back = jnp.dot(side_by_side(back_half), table_a, preferred_element_type=jnp.float32)
        diff_real = back[:, :size] - exit_real
        diff_imag = back[:, size:] - exit_imag
        term_real = probe_real * diff_real + probe_imag * diff_imag
        term_imag = probe_real * diff_imag - probe_imag * diff_real
        own_ref[j] = jnp.where(first, term_real, term_imag)
        other_ref[j] = jnp.where(first, term_imag, term_real)
        grad_real += patch_real * diff_real + patch_imag * diff_imag
        grad_imag += patch_real * diff_imag - patch_imag * diff_real
    probe_own_ref[...] = jnp.where(first, grad_real, grad_imag)
    probe_other_ref[...] = jnp.where(first, grad_imag, grad_real)


def half_of(z, x, c):
    return jnp.where(c == 0, lax.rem(x, 2), lax.rem(z, 2))


def halve_kernel(own_ref, recv_ref, unused_ref, unused_light_ref, keep_ref, give_ref, handed_on_ref):
    half = half_of(*(lax.axis_index(a) for a in GROUP))
    rows = keep_ref.shape[0]
    for at, out in ((half, keep_ref), (1 - half, give_ref)):
        span = pl.ds(pl.multiple_of(at * rows, rows), rows)
        out[...] = own_ref[span, :] + recv_ref[span, :]


def gather_kernel(nx, note_ref, other_note_ref, own_ref, recv_ref, unused_ref, middle_ref, *refs):
    x = lax.axis_index("scany")
    *blocks, grad, note, other_note, sems = refs
    copies = read_notes([note_ref, other_note_ref], [note, other_note], sems)
    npos, size, _ = own_ref.shape
    lane = lax.broadcasted_iota(jnp.int32, (size + 8, size), 1)
    grad[...] = jnp.zeros_like(grad)
    for copy, offs, terms in zip(copies, (note, other_note), (own_ref, recv_ref)):
        copy.wait()
        for j in range(npos):
            row, col = offset_in(offs, j)
            base, shift = aligned(row)
            term = rows_down(pltpu.roll(terms[j], col, axis=1), shift)
            low = jnp.where(lane >= col, term, 0.0)
            rows = pl.ds(base, size + 8)
            grad[rows, :size] += low
            grad[rows, size:] += term - low
    tile = middle_ref.shape[1]
    margin = (middle_ref.shape[0] - tile) // 2
    middle_ref[...] = grad[:, margin : margin + tile]
    for block, way in zip(blocks, ways_of(nx)):
        block[...] = grad[:, pl.ds(pl.multiple_of(side_of(x, way) * (margin + tile), margin), margin)]


def fold_kernel(nz, nx, unused_ref, middle_ref, *refs):
    z, x = lax.axis_index("scanx"), lax.axis_index("scany")
    ways = ways_of(nx)
    blocks, (center_ref, *edges, total) = refs[: len(ways)], refs[len(ways) :]
    tile = center_ref.shape[0]
    margin = (middle_ref.shape[0] - tile) // 2
    total[...] = middle_ref[...]
    for block, way in zip(blocks, ways):
        at = pl.multiple_of(side_of(x, way) * (tile - margin), margin)

        @pl.when(valid_of(x, way, nx))
        def _():
            total[:, pl.ds(at, margin)] += block[...]

    center_ref[...] = total[margin : margin + tile, :]
    for way, edge in enumerate(edges):
        edge[...] = total[pl.ds(pl.multiple_of(side_of(z, way) * (margin + tile), margin), margin), :]


def update_kernel(nz, unused_ref, spec_ref, center_ref, light_ref, other_light_ref, edge_a, edge_b, *refs):
    z, c = lax.axis_index("scanx"), lax.axis_index("pos")
    upper_ref, lower_ref, grad = refs
    tile = center_ref.shape[0]
    grad[...] = center_ref[...]
    for way, edge in enumerate((edge_a, edge_b)):
        margin = edge.shape[0]
        at = pl.multiple_of(side_of(z, way) * (tile - margin), margin)

        @pl.when(valid_of(z, way, nz))
        def _():
            grad[pl.ds(at, margin), :] += edge[...]

    for at, out in ((0, upper_ref), (tile // 2, lower_ref)):
        span = pl.ds(at, tile // 2)
        out[...] = spec_ref[c, span, :] + grad[span, :] / (light_ref[span, :] + other_light_ref[span, :] + 1.0)


def add_kernel(a_ref, b_ref, *refs):
    refs[-1][...] = a_ref[...] + b_ref[...]


def specimen_kernel(upper_ref, lower_ref, other_upper_ref, other_lower_ref, out_ref, done_ref):
    c = lax.axis_index("pos")
    rows = upper_ref.shape[0]
    for part, upper, lower in ((c, upper_ref, lower_ref), (1 - c, other_upper_ref, other_lower_ref)):
        out_ref[part, :rows, :] = upper[...]
        out_ref[part, rows:, :] = lower[...]
    done_ref[...] = jnp.zeros(done_ref.shape, done_ref.dtype)


def probe_kernel(step_size, probe_ref, keep_ref, away_ref, keep_other_ref, away_other_ref, unused_ref, out_ref):
    z, x, c = (lax.axis_index(a) for a in GROUP)
    rows = keep_ref.shape[0]
    for part, keep, away in ((c, keep_ref, away_ref), (1 - c, keep_other_ref, away_other_ref)):
        half = half_of(z, x, part)
        for at, term in ((half, keep), (1 - half, away)):
            span = pl.ds(pl.multiple_of(at * rows, rows), rows)
            out_ref[part, span, :] = probe_ref[part, span, :] + term[...] * step_size


def light_kernel(npos, nz, nx, which, note_ref, probe_ref, before_ref, unused_ref, *refs):
    z, x, c = (lax.axis_index(a) for a in GROUP)
    blocks, (light_ref, power_ref, total, *notes, sems) = refs[: len(which)], refs[len(which) :]
    own = len(notes) > len(which)
    copies = read_notes(([note_ref] if own else []) + [note_of(b) for b in blocks], notes, sems)
    size = probe_ref.shape[1]
    margin = size // 2
    tile = light_ref.shape[0]
    power_ref[...] = probe_ref[0] * probe_ref[0] + probe_ref[1] * probe_ref[1]
    total[...] = jnp.zeros_like(total)
    lane = lax.broadcasted_iota(jnp.int32, (size, size), 1)

    def add(row, col, ok):
        ok = jnp.logical_and(ok, jnp.logical_and(jnp.abs(row) < tile, jnp.abs(col) < tile))

        @pl.when(ok)
        def _():
            base, shift = aligned(row + tile)
            moved = pltpu.roll(power_ref[...], lax.rem(col + size, size), axis=1)
            keep = jnp.logical_and(lane >= col, lane < col + size)
            total[pl.ds(base, size + 8), :] += rows_down(jnp.where(keep, moved, 0.0), shift)

    ways, valid = block_ways(nz, nx), block_valid(z, x, nz, nx)
    places = [((None, None), True)] * own + [(ways[k], valid[k]) for k in which]
    for copy, note, ((zway, xway), ok) in zip(copies, notes, places):
        copy.wait()
        down = 0 if zway is None else (2 * side_of(z, zway) - 1) * tile
        right = 0 if xway is None else (2 * side_of(x, xway) - 1) * tile
        for j in range(npos):
            row, col = offset_in(note, j)
            add(row + down - margin, col + right - margin, ok)
    if own:
        light_ref[...] = total[tile : 2 * tile, :]
    else:
        light_ref[...] = before_ref[...] + total[tile : 2 * tile, :]


def call(kernel, out_shape, specs, *operands, scratch=(), outs=None, aliases={}, vmem=16 * 1024 * 1024):
    return pl.pallas_call(
        kernel,
        out_shape=out_shape,
        in_specs=specs,
        out_specs=outs or [VMEM] * len(out_shape),
        scratch_shapes=list(scratch),
        input_output_aliases=aliases,
        compiler_params=pltpu.CompilerParams(vmem_limit_bytes=vmem),
    )(*operands)


def dma(count):
    return pltpu.SemaphoreType.DMA((count,))


def shards(sizes, specimen, probe_wave, amplitudes, offsets):
    nz, nx, nc = sizes
    size = probe_wave.shape[1]
    margin = size // 2
    tile = specimen.shape[1]
    npos = offsets.shape[0]
    ways = block_ways(nz, nx)
    xways = ways_of(nx)
    targets = block_targets(nz, nx)

    def send(value, target):
        return lax.ppermute(value, GROUP, permutation(sizes, target))

    def to_core(value):
        return lax.ppermute(value, "pos", PART_SWAP)

    shapes = block_shapes(nz, nx, tile)
    *blocks, note = call(
        functools.partial(halo_blocks_kernel, nz, nx),
        [f32(h + NOTE[0] + (FILL_ROWS if v is None else 0), w) for (h, w), (v, _) in zip(shapes, ways)] + [f32(*NOTE)],
        [HBM, HBM],
        offsets,
        specimen,
        scratch=[pltpu.SMEM(offsets.shape, jnp.int32), dma(len(ways) + 1)],
        vmem=KEEP_IN_HBM,
    )
    recv = [send(block, target) for block, target in zip(blocks, targets)]

    waves = jnp.asarray(dft_waves(size))
    late = (note, probe_wave)
    note, probe_v, ta_v, tb_v = call(
        fetch_kernel,
        [jax.ShapeDtypeStruct(a.shape, a.dtype) for a in late]
        + [jax.ShapeDtypeStruct((2 * size, 2 * size), jnp.bfloat16)] * 2,
        [ANY] * len(late) + [VMEM],
        *late,
        waves,
        scratch=[dma(len(late))],
    )
    def patches_from(ours, after, *arrays):
        return call(
            functools.partial(patches_kernel, nz, nx, ours),
            [f32(npos, size, size)],
            [VMEM, ANY] + [VMEM] * (1 + len(arrays)),
            note,
            after,
            specimen,
            *arrays,
            scratch=[pltpu.VMEM((tile + size, tile + size), jnp.float32), NOTE_SMEM, dma(1)],
        )[0]

    def light_from(which, own, before, after):
        return call(
            functools.partial(light_kernel, npos, nz, nx, which),
            [f32(tile, tile)],
            [VMEM, VMEM, ANY if own else VMEM, ANY] + [VMEM] * len(which),
            note,
            probe_v,
            before,
            after,
            *[recv[k] for k in which],
            scratch=[
                pltpu.VMEM((size, size), jnp.float32),
                pltpu.VMEM((3 * tile, size), jnp.float32),
                *[NOTE_SMEM] * (own + len(which)),
                dma(own + len(which)),
            ],
        )[0]

    corners, along_z, along_x = packing_order(nz, nx)
    def packed(which, *after):
        chosen = [shapes[k] for k in which]
        return call(
            functools.partial(pack_kernel, chosen, len(after)),
            [f32(sum(h * w for h, w in chosen) // margin, margin)],
            [ANY] * len(after) + [VMEM] * len(which),
            *after,
            *[recv[k] for k in which],
        )[0]

    packed_corners = packed(corners, probe_v, *[recv[k] for k in along_x])
    other_corners = to_core(packed_corners)
    light = light_from(corners + along_x, True, packed_corners, packed_corners)
    packed_z = packed(along_z, light, other_corners)
    patches = patches_from(True, packed_z, *recv)
    patches_other = patches_from(False, patches, other_corners, to_core(packed_z), *[to_core(recv[k]) for k in along_x])
    own, other, probe_own, probe_other = call(
        positions_kernel,
        [f32(npos, size, size)] * 2 + [f32(size, size)] * 2,
        [VMEM] * 6,
        patches,
        patches_other,
        probe_v,
        amplitudes,
        ta_v,
        tb_v,
    )
    other_note = to_core(note)
    light = light_from(along_z, False, light, own)

    zbits = [("z", 1 << k) for k in range(nz.bit_length() - 1)]
    xbits = [("x", 1 << k) for k in range(nx.bit_length() - 1)]
    orders = (xbits[:1] + zbits + xbits[1:], zbits + xbits)

    def stage(k):
        def target(z, x, c):
            axis, bit = orders[c][k]
            return (z ^ bit, x, c) if axis == "z" else (z, x ^ bit, c)

        return target

    half = f32(size // 2, size)
    keep, away, other = call(
        halve_kernel,
        [half] * 2 + [f32(npos, size, size)],
        [VMEM, VMEM, ANY, ANY],
        probe_own,
        to_core(probe_other),
        other,
        light,
        outs=[VMEM, VMEM, ANY],
        aliases={2: 2},
    )
    terms = to_core(other)
    middle, *beyond = call(
        functools.partial(gather_kernel, nx),
        [f32(tile + size, tile)] + [f32(tile + size, margin)] * len(xways),
        [VMEM] * 4 + [ANY],
        note,
        other_note,
        own,
        terms,
        keep,
        scratch=[pltpu.VMEM((tile + size, tile + size), jnp.float32), NOTE_SMEM, NOTE_SMEM, dma(2)],
    )
    (keep,) = call(add_kernel, [half], [VMEM] * 2 + [ANY], keep, send(away, stage(0)), middle)
    beside = [send(piece, targets[ways.index((None, way))]) for piece, way in zip(beyond, xways)]
    (keep,) = call(add_kernel, [half], [VMEM] * 2, keep, send(keep, stage(1)))
    center, *edges = call(
        functools.partial(fold_kernel, nz, nx),
        [f32(tile, tile)] + [f32(margin, tile)] * 2,
        [ANY] + [VMEM] * (1 + len(beside)),
        keep,
        middle,
        *beside,
        scratch=[pltpu.VMEM((tile + size, tile), jnp.float32)],
    )
    arrived = [send(edge, targets[ways.index((way, None))]) for way, edge in enumerate(edges)]
    for k in range(2, len(orders[0])):
        (keep,) = call(add_kernel, [half], [VMEM] * 2, keep, send(keep, stage(k)))
    updated = call(
        functools.partial(update_kernel, nz),
        [f32(tile // 2, tile)] * 2,
        [ANY] + [VMEM] * (4 + len(arrived)),
        keep,
        specimen,
        center,
        light,
        to_core(light),
        *arrived,
        scratch=[pltpu.VMEM((tile, tile), jnp.float32)],
    )
    away = send(keep, stage(0))
    new_specimen, done = call(
        specimen_kernel, [f32(2, tile, tile), f32(*NOTE)], [VMEM] * 4, *updated, *[to_core(u) for u in updated]
    )
    step_size = 1.0 / math.sqrt(npos * nz * nx * nc)
    (new_probe,) = call(
        functools.partial(probe_kernel, step_size),
        [f32(2, size, size)],
        [VMEM] * 5 + [ANY],
        probe_v,
        keep,
        away,
        to_core(keep),
        to_core(away),
        done,
    )
    return (new_specimen, new_probe)


def solution(mesh):
    sizes = tuple(mesh.shape[a] for a in GROUP)
    placed = (
        P(None, ("groups", "scanx"), "scany"),
        P(None, "groups", None),
        P(("groups", "scanx", "scany", "pos"), None, None),
        P(("groups", "scanx", "scany", "pos"), None),
    )
    return jax.shard_map(
        functools.partial(shards, sizes),
        mesh=mesh,
        in_specs=placed,
        out_specs=(P(None, ("groups", "scanx"), "scany"), P(None, "groups", None)),
        check_vma=False,
    )
```

```python
import functools
import math

import jax
import jax.numpy as jnp
import numpy as np
from jax import lax
from jax.experimental import pallas as pl
from jax.experimental.pallas import tpu as pltpu
from jax.sharding import PartitionSpec as P

GROUP = ("scanx", "scany", "pos")
KEEP_IN_HBM = 64 * 1024 * 1024 - 448 * 1024
PART_SWAP = ((0, 1), (1, 0))
VMEM = pl.BlockSpec(memory_space=pltpu.VMEM)
ANY = pl.BlockSpec(memory_space=pl.ANY)
HBM = pl.BlockSpec(memory_space=pltpu.HBM)
NOTE = (8, 128)
FILL_ROWS = 16
NOTE_SMEM = pltpu.SMEM(NOTE, jnp.float32)


def f32(*shape):
    return jax.ShapeDtypeStruct(shape, jnp.float32)


def ways_of(count):
    return (0,) if count == 2 else (0, 1)


def side_of(index, way):
    return lax.rem(index + way + 1, 2)


def valid_of(index, way, count):
    neighbour = index + 2 * side_of(index, way) - 1
    return jnp.logical_and(neighbour >= 0, neighbour < count)


def block_ways(nz, nx):
    xways, zways = ways_of(nx), (0, 1)
    order = [(None, w) for w in xways] + [(w, None) for w in zways]
    return order + [(v, w) for w in xways for v in zways]


def block_places(z, x, nz, nx, origin, extent, margin):
    places = []
    for zway, xway in block_ways(nz, nx):
        span = []
        for index, way in ((z, zway), (x, xway)):
            if way is None:
                span.append(pl.ds(origin, 2 * margin))
            else:
                span.append(pl.ds(pl.multiple_of(side_of(index, way) * extent, margin), margin))
        places.append(tuple(span))
    return places


def block_shapes(nz, nx, tile):
    return [tuple(tile if way is None else tile // 2 for way in ways) for ways in block_ways(nz, nx)]


def packing_order(nz, nx):
    ways = block_ways(nz, nx)
    kinds = [(v is not None, w is not None) for v, w in ways]
    return [[k for k, kind in enumerate(kinds) if kind == which] for which in ((True, True), (True, False), (False, True))]


def packed_places(shapes):
    lanes = min(min(shape) for shape in shapes)
    at, places = 0, []
    for height, width in shapes:
        places.append([])
        for col in range(0, width, lanes):
            places[-1].append((at, col, height))
            at += height
    return places


def block_valid(z, x, nz, nx):
    result = []
    for zway, xway in block_ways(nz, nx):
        ok = True
        if zway is not None:
            ok = valid_of(z, zway, nz)
        if xway is not None:
            ok = jnp.logical_and(ok, valid_of(x, xway, nx))
        result.append(ok)
    return result


def block_targets(nz, nx):
    def step(index, way, count):
        if way is None:
            return index
        to = index + (1 if (index + way) % 2 == 0 else -1)
        return to if 0 <= to < count else None

    def target(ways, z, x, c):
        tz, tx = step(z, ways[0], nz), step(x, ways[1], nx)
        return (z, x, 1 - c) if tz is None or tx is None else (tz, tx, c)

    return [functools.partial(target, ways) for ways in block_ways(nz, nx)]


def permutation(sizes, target):
    nz, nx, nc = sizes
    pairs = []
    for z in range(nz):
        for x in range(nx):
            for c in range(nc):
                tz, tx, tc = target(z, x, c)
                pairs.append(((z * nx + x) * nc + c, (tz * nx + tx) * nc + tc))
    return pairs


def dft_waves(length):
    index = np.arange(length, dtype=np.int32)
    phase = (index[:, None] * index[None, :]) % length
    angle = phase.astype(np.float32) * np.float32(2.0 * math.pi / length)
    scale = np.float32(1.0 / math.sqrt(length))
    sine = np.sin(angle) * scale
    return np.stack([np.cos(angle) * scale, sine, -sine]).astype(jnp.bfloat16)


def aligned(row):
    return pl.multiple_of((row // 8) * 8, 8), lax.rem(row, 8)


def rows_up(block, shift):
    count, width = block.shape
    groups = pltpu.roll(block.reshape(count // 8, 8, width), lax.rem(8 - shift, 8), axis=1)
    at = lax.broadcasted_iota(jnp.int32, (count // 8 - 1, 8, width), 1)
    return jnp.where(at < 8 - shift, groups[:-1], groups[1:]).reshape(count - 8, width)


def rows_down(block, shift):
    count, width = block.shape
    groups = pltpu.roll(block.reshape(count // 8, 8, width), shift, axis=1)
    blank = jnp.zeros((1, 8, width), block.dtype)
    at = lax.broadcasted_iota(jnp.int32, (count // 8 + 1, 8, width), 1)
    early = jnp.concatenate([groups, blank])
    late = jnp.concatenate([blank, groups])
    return jnp.where(at >= shift, early, late).reshape(count + 8, width)


def halo_blocks_kernel(nz, nx, off_hbm, spec_ref, *refs):
    z, x, c = (lax.axis_index(a) for a in GROUP)
    *outs, note_ref, off_ref, sems = refs
    tile = spec_ref.shape[1]
    margin = tile // 2
    off_copy = pltpu.make_async_copy(off_hbm, off_ref, sems.at[len(outs)])
    off_copy.start()
    copies = []
    places = block_places(z, x, nz, nx, 0, margin, margin)
    for k, (out, (height, _), (rows, cols)) in enumerate(zip(outs, block_shapes(nz, nx, tile), places)):
        copies.append(pltpu.make_async_copy(spec_ref.at[c, rows, cols], out.at[pl.ds(0, height), :], sems.at[k]))
        copies[-1].start()
    off_copy.wait()
    lane = lax.broadcasted_iota(jnp.int32, NOTE, 1)
    note = jnp.zeros(NOTE, jnp.float32)
    for j in range(off_ref.shape[0]):
        for k in range(2):
            note = jnp.where(lane == 2 * j + k, off_ref[j, k].astype(jnp.float32), note)
    note_ref[...] = note
    for out, (height, width) in zip(outs, block_shapes(nz, nx, tile)):
        fill = out.shape[0] - NOTE[0] - height
        if fill:
            out[height : height + fill, :] = jnp.zeros((fill, width), jnp.float32)
        out[height + fill :, : NOTE[1]] = note
    for copy in copies:
        copy.wait()


def read_notes(notes, smems, sems):
    copies = [pltpu.make_async_copy(note, smem, sems.at[k]) for k, (note, smem) in enumerate(zip(notes, smems))]
    for copy in copies:
        copy.start()
    return copies


def note_of(block):
    return block.at[pl.ds(block.shape[0] - NOTE[0], NOTE[0]), pl.ds(0, NOTE[1])]


def offset_in(note, j):
    return note[0, 2 * j].astype(jnp.int32), note[0, 2 * j + 1].astype(jnp.int32)


def fetch_kernel(*refs):
    *refs, table_a, table_b, sems = refs
    count = len(refs) // 2
    *sources, waves = refs[: count + 1]
    copies = [pltpu.make_async_copy(src, refs[count + 1 + k], sems.at[k]) for k, src in enumerate(sources)]
    for copy in copies:
        copy.start()
    cosine, sine, minus = (waves[k] for k in range(3))
    size = cosine.shape[0]
    for table, blocks in ((table_a, (cosine, sine, minus, cosine)), (table_b, (cosine, minus, sine, cosine))):
        for k, block in enumerate(blocks):
            at, left = k // 2 * size, k % 2 * size
            table[at : at + size, left : left + size] = block
    for copy in copies:
        copy.wait()


def cut_patches(note, padded, out):
    npos, size, _ = out.shape
    lane = lax.broadcasted_iota(jnp.int32, (size + 8, size), 1)
    for j in range(npos):
        row, col = offset_in(note, j)
        base, shift = aligned(row)
        rows = padded[pl.ds(base, size + 8), :]
        mixed = rows_up(jnp.where(lane >= col, rows[:, :size], rows[:, size:]), shift)
        out[j] = pltpu.roll(mixed, lax.rem(size - col, size), axis=1)


def patches_kernel(nz, nx, ours, note_ref, unused_ref, spec_ref, *refs):
    z, x, c = (lax.axis_index(a) for a in GROUP)
    *blocks, out, padded, note, sems = refs
    copies = read_notes([note_ref], [note], sems)
    tile = spec_ref.shape[1]
    margin = (padded.shape[0] - tile) // 2
    padded[margin : margin + tile, margin : margin + tile] = spec_ref[c if ours else 1 - c]
    if len(ways_of(nx)) == 1:
        far_cols = pl.ds(pl.multiple_of((1 - side_of(x, 0)) * (margin + tile), margin), margin)
        padded[:, far_cols] = jnp.zeros((padded.shape[0], margin), jnp.float32)
    places = block_places(z, x, nz, nx, margin, margin + tile, margin)
    shapes = block_shapes(nz, nx, tile)
    pieces = {}
    for which, array in zip(packing_order(nz, nx), blocks):
        for k, places_of in zip(which, packed_places([shapes[k] for k in which])):
            pieces[k] = [(array, at) for at, _, _ in places_of]
    for k, ((height, width), (rows, cols), ok) in enumerate(zip(shapes, places, block_valid(z, x, nz, nx))):

        @pl.when(ok)
        def _():
            if ours:
                padded[rows, cols] = blocks[k][:height, :]
            else:
                parts = [array[at : at + height, :] for array, at in pieces[k]]
                padded[rows, cols] = parts[0] if len(parts) == 1 else jnp.concatenate(parts, axis=1)

        @pl.when(jnp.logical_not(ok))
        def _():
            padded[rows, cols] = jnp.zeros((height, width), jnp.float32)

    copies[0].wait()
    cut_patches(note, padded, out)


def pack_kernel(shapes, waits, *refs):
    *blocks, out = refs[waits:]
    for block, pieces in zip(blocks, packed_places(shapes)):
        for at, col, height in pieces:
            out[at : at + height, :] = block[:height, col : col + out.shape[1]]


def positions_kernel(patch_ref, patch_other_ref, probe_ref, amp_ref, ta_ref, tb_ref, own_ref, other_ref, probe_own_ref, probe_other_ref):
    first = lax.axis_index("pos") == 0
    npos, size, _ = patch_ref.shape
    table_a = ta_ref[...]
    table_b = tb_ref[...]
    probe_real = probe_ref[0]
    probe_imag = probe_ref[1]

    def side_by_side(both):
        return jnp.concatenate([both[:size], both[size:]], axis=1)

    grad_real = jnp.zeros((size, size), jnp.float32)
    grad_imag = jnp.zeros((size, size), jnp.float32)
    for j in range(npos):
        patch_real = jnp.where(first, patch_ref[j], patch_other_ref[j])
        patch_imag = jnp.where(first, patch_other_ref[j], patch_ref[j])
        exit_real = probe_real * patch_real - probe_imag * patch_imag
        exit_imag = probe_real * patch_imag + probe_imag * patch_real
        wave = jnp.concatenate([exit_real, exit_imag], axis=0).astype(jnp.bfloat16)
        half = jnp.dot(table_a, wave, preferred_element_type=jnp.float32).astype(jnp.bfloat16)
        far = jnp.dot(side_by_side(half), table_b, preferred_element_type=jnp.float32)
        far_real, far_imag = far[:, :size], far[:, size:]
        power = far_real * far_real + far_imag * far_imag
        ratio = amp_ref[j].astype(jnp.float32) * jnp.minimum(lax.rsqrt(power), 1.0 / 0.2)
        projected = jnp.concatenate([far_real * ratio, far_imag * ratio], axis=0).astype(jnp.bfloat16)
        back_half = jnp.dot(table_b, projected, preferred_element_type=jnp.float32).astype(jnp.bfloat16)
        back = jnp.dot(side_by_side(back_half), table_a, preferred_element_type=jnp.float32)
        diff_real = back[:, :size] - exit_real
        diff_imag = back[:, size:] - exit_imag
        term_real = probe_real * diff_real + probe_imag * diff_imag
        term_imag = probe_real * diff_imag - probe_imag * diff_real
        own_ref[j] = jnp.where(first, term_real, term_imag)
        other_ref[j] = jnp.where(first, term_imag, term_real)
        grad_real += patch_real * diff_real + patch_imag * diff_imag
        grad_imag += patch_real * diff_imag - patch_imag * diff_real
    probe_own_ref[...] = jnp.where(first, grad_real, grad_imag)
    probe_other_ref[...] = jnp.where(first, grad_imag, grad_real)


def half_of(z, x, c):
    return jnp.where(c == 0, lax.rem(x, 2), lax.rem(z, 2))


def halve_kernel(own_ref, recv_ref, unused_ref, unused_light_ref, keep_ref, give_ref, handed_on_ref):
    half = half_of(*(lax.axis_index(a) for a in GROUP))
    rows = keep_ref.shape[0]
    for at, out in ((half, keep_ref), (1 - half, give_ref)):
        span = pl.ds(pl.multiple_of(at * rows, rows), rows)
        out[...] = own_ref[span, :] + recv_ref[span, :]


def gather_kernel(nx, note_ref, other_note_ref, own_ref, recv_ref, unused_ref, middle_ref, *refs):
    x = lax.axis_index("scany")
    *blocks, grad, note, other_note, sems = refs
    copies = read_notes([note_ref, other_note_ref], [note, other_note], sems)
    npos, size, _ = own_ref.shape
    lane = lax.broadcasted_iota(jnp.int32, (size + 8, size), 1)
    grad[...] = jnp.zeros_like(grad)
    for copy, offs, terms in zip(copies, (note, other_note), (own_ref, recv_ref)):
        copy.wait()
        for j in range(npos):
            row, col = offset_in(offs, j)
            base, shift = aligned(row)
            term = rows_down(pltpu.roll(terms[j], col, axis=1), shift)
            low = jnp.where(lane >= col, term, 0.0)
            rows = pl.ds(base, size + 8)
            grad[rows, :size] += low
            grad[rows, size:] += term - low
    tile = middle_ref.shape[1]
    margin = (middle_ref.shape[0] - tile) // 2
    middle_ref[...] = grad[:, margin : margin + tile]
    for block, way in zip(blocks, ways_of(nx)):
        block[...] = grad[:, pl.ds(pl.multiple_of(side_of(x, way) * (margin + tile), margin), margin)]


def fold_kernel(nz, nx, unused_ref, middle_ref, *refs):
    z, x = lax.axis_index("scanx"), lax.axis_index("scany")
    ways = ways_of(nx)
    blocks, (center_ref, *edges, total) = refs[: len(ways)], refs[len(ways) :]
    tile = center_ref.shape[0]
    margin = (middle_ref.shape[0] - tile) // 2
    total[...] = middle_ref[...]
    for block, way in zip(blocks, ways):
        at = pl.multiple_of(side_of(x, way) * (tile - margin), margin)

        @pl.when(valid_of(x, way, nx))
        def _():
            total[:, pl.ds(at, margin)] += block[...]

    center_ref[...] = total[margin : margin + tile, :]
    for way, edge in enumerate(edges):
        edge[...] = total[pl.ds(pl.multiple_of(side_of(z, way) * (margin + tile), margin), margin), :]


def update_kernel(nz, unused_ref, spec_ref, center_ref, light_ref, other_light_ref, edge_a, edge_b, *refs):
    z, c = lax.axis_index("scanx"), lax.axis_index("pos")
    upper_ref, lower_ref, grad = refs
    tile = center_ref.shape[0]
    grad[...] = center_ref[...]
    for way, edge in enumerate((edge_a, edge_b)):
        margin = edge.shape[0]
        at = pl.multiple_of(side_of(z, way) * (tile - margin), margin)

        @pl.when(valid_of(z, way, nz))
        def _():
            grad[pl.ds(at, margin), :] += edge[...]

    for at, out in ((0, upper_ref), (tile // 2, lower_ref)):
        span = pl.ds(at, tile // 2)
        out[...] = spec_ref[c, span, :] + grad[span, :] / (light_ref[span, :] + other_light_ref[span, :] + 1.0)


def add_kernel(a_ref, b_ref, *refs):
    refs[-1][...] = a_ref[...] + b_ref[...]


def specimen_kernel(upper_ref, lower_ref, other_upper_ref, other_lower_ref, out_ref, done_ref):
    c = lax.axis_index("pos")
    rows = upper_ref.shape[0]
    for part, upper, lower in ((c, upper_ref, lower_ref), (1 - c, other_upper_ref, other_lower_ref)):
        out_ref[part, :rows, :] = upper[...]
        out_ref[part, rows:, :] = lower[...]
    done_ref[...] = jnp.zeros(done_ref.shape, done_ref.dtype)


def probe_kernel(step_size, probe_ref, keep_ref, away_ref, keep_other_ref, away_other_ref, unused_ref, out_ref):
    z, x, c = (lax.axis_index(a) for a in GROUP)
    rows = keep_ref.shape[0]
    for part, keep, away in ((c, keep_ref, away_ref), (1 - c, keep_other_ref, away_other_ref)):
        half = half_of(z, x, part)
        for at, term in ((half, keep), (1 - half, away)):
            span = pl.ds(pl.multiple_of(at * rows, rows), rows)
            out_ref[part, span, :] = probe_ref[part, span, :] + term[...] * step_size


def light_kernel(npos, nz, nx, which, note_ref, probe_ref, before_ref, unused_ref, *refs):
    z, x, c = (lax.axis_index(a) for a in GROUP)
    blocks, (light_ref, power_ref, total, *notes, sems) = refs[: len(which)], refs[len(which) :]
    own = len(notes) > len(which)
    copies = read_notes(([note_ref] if own else []) + [note_of(b) for b in blocks], notes, sems)
    size = probe_ref.shape[1]
    margin = size // 2
    tile = light_ref.shape[0]
    power_ref[...] = probe_ref[0] * probe_ref[0] + probe_ref[1] * probe_ref[1]
    total[...] = jnp.zeros_like(total)
    lane = lax.broadcasted_iota(jnp.int32, (size, size), 1)

    def add(row, col, ok):
        ok = jnp.logical_and(ok, jnp.logical_and(jnp.abs(row) < tile, jnp.abs(col) < tile))

        @pl.when(ok)
        def _():
            base, shift = aligned(row + tile)
            moved = pltpu.roll(power_ref[...], lax.rem(col + size, size), axis=1)
            keep = jnp.logical_and(lane >= col, lane < col + size)
            total[pl.ds(base, size + 8), :] += rows_down(jnp.where(keep, moved, 0.0), shift)

    ways, valid = block_ways(nz, nx), block_valid(z, x, nz, nx)
    places = [((None, None), True)] * own + [(ways[k], valid[k]) for k in which]
    for copy, note, ((zway, xway), ok) in zip(copies, notes, places):
        copy.wait()
        down = 0 if zway is None else (2 * side_of(z, zway) - 1) * tile
        right = 0 if xway is None else (2 * side_of(x, xway) - 1) * tile
        for j in range(npos):
            row, col = offset_in(note, j)
            add(row + down - margin, col + right - margin, ok)
    if own:
        light_ref[...] = total[tile : 2 * tile, :]
    else:
        light_ref[...] = before_ref[...] + total[tile : 2 * tile, :]


def call(kernel, out_shape, specs, *operands, scratch=(), outs=None, aliases={}, vmem=16 * 1024 * 1024):
    return pl.pallas_call(
        kernel,
        out_shape=out_shape,
        in_specs=specs,
        out_specs=outs or [VMEM] * len(out_shape),
        scratch_shapes=list(scratch),
        input_output_aliases=aliases,
        compiler_params=pltpu.CompilerParams(vmem_limit_bytes=vmem),
    )(*operands)


def dma(count):
    return pltpu.SemaphoreType.DMA((count,))


def shards(sizes, specimen, probe_wave, amplitudes, offsets):
    nz, nx, nc = sizes
    size = probe_wave.shape[1]
    margin = size // 2
    tile = specimen.shape[1]
    npos = offsets.shape[0]
    ways = block_ways(nz, nx)
    xways = ways_of(nx)
    targets = block_targets(nz, nx)

    def send(value, target):
        return lax.ppermute(value, GROUP, permutation(sizes, target))

    def to_core(value):
        return lax.ppermute(value, "pos", PART_SWAP)

    shapes = block_shapes(nz, nx, tile)
    *blocks, note = call(
        functools.partial(halo_blocks_kernel, nz, nx),
        [f32(h + NOTE[0] + (FILL_ROWS if v is None else 0), w) for (h, w), (v, _) in zip(shapes, ways)] + [f32(*NOTE)],
        [HBM, HBM],
        offsets,
        specimen,
        scratch=[pltpu.SMEM(offsets.shape, jnp.int32), dma(len(ways) + 1)],
        vmem=KEEP_IN_HBM,
    )
    recv = [send(block, target) for block, target in zip(blocks, targets)]

    waves = jnp.asarray(dft_waves(size))
    late = (note, probe_wave)
    note, probe_v, ta_v, tb_v = call(
        fetch_kernel,
        [jax.ShapeDtypeStruct(a.shape, a.dtype) for a in late]
        + [jax.ShapeDtypeStruct((2 * size, 2 * size), jnp.bfloat16)] * 2,
        [ANY] * len(late) + [VMEM],
        *late,
        waves,
        scratch=[dma(len(late))],
    )
    def patches_from(ours, after, *arrays):
        return call(
            functools.partial(patches_kernel, nz, nx, ours),
            [f32(npos, size, size)],
            [VMEM, ANY] + [VMEM] * (1 + len(arrays)),
            note,
            after,
            specimen,
            *arrays,
            scratch=[pltpu.VMEM((tile + size, tile + size), jnp.float32), NOTE_SMEM, dma(1)],
        )[0]

    def light_from(which, own, before, after):
        return call(
            functools.partial(light_kernel, npos, nz, nx, which),
            [f32(tile, tile)],
            [VMEM, VMEM, ANY if own else VMEM, ANY] + [VMEM] * len(which),
            note,
            probe_v,
            before,
            after,
            *[recv[k] for k in which],
            scratch=[
                pltpu.VMEM((size, size), jnp.float32),
                pltpu.VMEM((3 * tile, size), jnp.float32),
                *[NOTE_SMEM] * (own + len(which)),
                dma(own + len(which)),
            ],
        )[0]

    corners, along_z, along_x = packing_order(nz, nx)
    def packed(which, *after):
        chosen = [shapes[k] for k in which]
        return call(
            functools.partial(pack_kernel, chosen, len(after)),
            [f32(sum(h * w for h, w in chosen) // margin, margin)],
            [ANY] * len(after) + [VMEM] * len(which),
            *after,
            *[recv[k] for k in which],
        )[0]

    packed_corners = packed(corners, probe_v, *[recv[k] for k in along_x])
    other_corners = to_core(packed_corners)
    light = light_from(corners + along_x, True, packed_corners, packed_corners)
    other_x = to_core(packed(along_x, packed_corners))
    packed_z = packed(along_z, light, other_corners, other_x)
    patches = patches_from(True, packed_z, *recv)
    patches_other = patches_from(False, patches, other_corners, to_core(packed_z), other_x)
    own, other, probe_own, probe_other = call(
        positions_kernel,
        [f32(npos, size, size)] * 2 + [f32(size, size)] * 2,
        [VMEM] * 6,
        patches,
        patches_other,
        probe_v,
        amplitudes,
        ta_v,
        tb_v,
    )
    other_note = to_core(note)
    light = light_from(along_z, False, light, own)

    zbits = [("z", 1 << k) for k in range(nz.bit_length() - 1)]
    xbits = [("x", 1 << k) for k in range(nx.bit_length() - 1)]
    orders = (xbits[:1] + zbits + xbits[1:], zbits + xbits)

    def stage(k):
        def target(z, x, c):
            axis, bit = orders[c][k]
            return (z ^ bit, x, c) if axis == "z" else (z, x ^ bit, c)

        return target

    half = f32(size // 2, size)
    keep, away, other = call(
        halve_kernel,
        [half] * 2 + [f32(npos, size, size)],
        [VMEM, VMEM, ANY, ANY],
        probe_own,
        to_core(probe_other),
        other,
        light,
        outs=[VMEM, VMEM, ANY],
        aliases={2: 2},
    )
    terms = to_core(other)
    middle, *beyond = call(
        functools.partial(gather_kernel, nx),
        [f32(tile + size, tile)] + [f32(tile + size, margin)] * len(xways),
        [VMEM] * 4 + [ANY],
        note,
        other_note,
        own,
        terms,
        keep,
        scratch=[pltpu.VMEM((tile + size, tile + size), jnp.float32), NOTE_SMEM, NOTE_SMEM, dma(2)],
    )
    (keep,) = call(add_kernel, [half], [VMEM] * 2 + [ANY], keep, send(away, stage(0)), middle)
    beside = [send(piece, targets[ways.index((None, way))]) for piece, way in zip(beyond, xways)]
    (keep,) = call(add_kernel, [half], [VMEM] * 2, keep, send(keep, stage(1)))
    center, *edges = call(
        functools.partial(fold_kernel, nz, nx),
        [f32(tile, tile)] + [f32(margin, tile)] * 2,
        [ANY] + [VMEM] * (1 + len(beside)),
        keep,
        middle,
        *beside,
        scratch=[pltpu.VMEM((tile + size, tile), jnp.float32)],
    )
    arrived = [send(edge, targets[ways.index((way, None))]) for way, edge in enumerate(edges)]
    for k in range(2, len(orders[0])):
        (keep,) = call(add_kernel, [half], [VMEM] * 2, keep, send(keep, stage(k)))
    updated = call(
        functools.partial(update_kernel, nz),
        [f32(tile // 2, tile)] * 2,
        [ANY] + [VMEM] * (4 + len(arrived)),
        keep,
        specimen,
        center,
        light,
        to_core(light),
        *arrived,
        scratch=[pltpu.VMEM((tile, tile), jnp.float32)],
    )
    away = send(keep, stage(0))
    new_specimen, done = call(
        specimen_kernel, [f32(2, tile, tile), f32(*NOTE)], [VMEM] * 4, *updated, *[to_core(u) for u in updated]
    )
    step_size = 1.0 / math.sqrt(npos * nz * nx * nc)
    (new_probe,) = call(
        functools.partial(probe_kernel, step_size),
        [f32(2, size, size)],
        [VMEM] * 5 + [ANY],
        probe_v,
        keep,
        away,
        to_core(keep),
        to_core(away),
        done,
    )
    return (new_specimen, new_probe)


def solution(mesh):
    sizes = tuple(mesh.shape[a] for a in GROUP)
    placed = (
        P(None, ("groups", "scanx"), "scany"),
        P(None, "groups", None),
        P(("groups", "scanx", "scany", "pos"), None, None),
        P(("groups", "scanx", "scany", "pos"), None),
    )
    return jax.shard_map(
        functools.partial(shards, sizes),
        mesh=mesh,
        in_specs=placed,
        out_specs=(P(None, ("groups", "scanx"), "scany"), P(None, "groups", None)),
        check_vma=False,
    )
```

```python
import functools
import math

import jax
import jax.numpy as jnp
import numpy as np
from jax import lax
from jax.experimental import pallas as pl
from jax.experimental.pallas import tpu as pltpu
from jax.sharding import PartitionSpec as P

GROUP = ("scanx", "scany", "pos")
KEEP_IN_HBM = 64 * 1024 * 1024 - 448 * 1024
PART_SWAP = ((0, 1), (1, 0))
VMEM = pl.BlockSpec(memory_space=pltpu.VMEM)
ANY = pl.BlockSpec(memory_space=pl.ANY)
HBM = pl.BlockSpec(memory_space=pltpu.HBM)
NOTE = (8, 128)
FILL_ROWS = 16
NOTE_SMEM = pltpu.SMEM(NOTE, jnp.float32)


def f32(*shape):
    return jax.ShapeDtypeStruct(shape, jnp.float32)


def ways_of(count):
    return (0,) if count == 2 else (0, 1)


def side_of(index, way):
    return lax.rem(index + way + 1, 2)


def valid_of(index, way, count):
    neighbour = index + 2 * side_of(index, way) - 1
    return jnp.logical_and(neighbour >= 0, neighbour < count)


def block_ways(nz, nx):
    xways, zways = ways_of(nx), (0, 1)
    order = [(None, w) for w in xways] + [(w, None) for w in zways]
    return order + [(v, w) for w in xways for v in zways]


def block_places(z, x, nz, nx, origin, extent, margin):
    places = []
    for zway, xway in block_ways(nz, nx):
        span = []
        for index, way in ((z, zway), (x, xway)):
            if way is None:
                span.append(pl.ds(origin, 2 * margin))
            else:
                span.append(pl.ds(pl.multiple_of(side_of(index, way) * extent, margin), margin))
        places.append(tuple(span))
    return places


def block_shapes(nz, nx, tile):
    return [tuple(tile if way is None else tile // 2 for way in ways) for ways in block_ways(nz, nx)]


def packing_order(nz, nx):
    ways = block_ways(nz, nx)
    kinds = [(v is not None, w is not None) for v, w in ways]
    return [[k for k, kind in enumerate(kinds) if kind == which] for which in ((True, True), (True, False), (False, True))]


def packed_places(shapes):
    lanes = min(min(shape) for shape in shapes)
    at, places = 0, []
    for height, width in shapes:
        places.append([])
        for col in range(0, width, lanes):
            places[-1].append((at, col, height))
            at += height
    return places


def block_valid(z, x, nz, nx):
    result = []
    for zway, xway in block_ways(nz, nx):
        ok = True
        if zway is not None:
            ok = valid_of(z, zway, nz)
        if xway is not None:
            ok = jnp.logical_and(ok, valid_of(x, xway, nx))
        result.append(ok)
    return result


def block_targets(nz, nx):
    def step(index, way, count):
        if way is None:
            return index
        to = index + (1 if (index + way) % 2 == 0 else -1)
        return to if 0 <= to < count else None

    def target(ways, z, x, c):
        tz, tx = step(z, ways[0], nz), step(x, ways[1], nx)
        return (z, x, 1 - c) if tz is None or tx is None else (tz, tx, c)

    return [functools.partial(target, ways) for ways in block_ways(nz, nx)]


def permutation(sizes, target):
    nz, nx, nc = sizes
    pairs = []
    for z in range(nz):
        for x in range(nx):
            for c in range(nc):
                tz, tx, tc = target(z, x, c)
                pairs.append(((z * nx + x) * nc + c, (tz * nx + tx) * nc + tc))
    return pairs


def dft_waves(length):
    index = np.arange(length, dtype=np.int32)
    phase = (index[:, None] * index[None, :]) % length
    angle = phase.astype(np.float32) * np.float32(2.0 * math.pi / length)
    scale = np.float32(1.0 / math.sqrt(length))
    sine = np.sin(angle) * scale
    return np.stack([np.cos(angle) * scale, sine, -sine]).astype(jnp.bfloat16)


def aligned(row):
    return pl.multiple_of((row // 8) * 8, 8), lax.rem(row, 8)


def rows_up(block, shift):
    count, width = block.shape
    groups = pltpu.roll(block.reshape(count // 8, 8, width), lax.rem(8 - shift, 8), axis=1)
    at = lax.broadcasted_iota(jnp.int32, (count // 8 - 1, 8, width), 1)
    return jnp.where(at < 8 - shift, groups[:-1], groups[1:]).reshape(count - 8, width)


def rows_down(block, shift):
    count, width = block.shape
    groups = pltpu.roll(block.reshape(count // 8, 8, width), shift, axis=1)
    blank = jnp.zeros((1, 8, width), block.dtype)
    at = lax.broadcasted_iota(jnp.int32, (count // 8 + 1, 8, width), 1)
    early = jnp.concatenate([groups, blank])
    late = jnp.concatenate([blank, groups])
    return jnp.where(at >= shift, early, late).reshape(count + 8, width)


def halo_blocks_kernel(nz, nx, off_hbm, spec_ref, *refs):
    z, x, c = (lax.axis_index(a) for a in GROUP)
    *outs, note_ref, off_ref, sems = refs
    tile = spec_ref.shape[1]
    margin = tile // 2
    off_copy = pltpu.make_async_copy(off_hbm, off_ref, sems.at[len(outs)])
    off_copy.start()
    copies = []
    places = block_places(z, x, nz, nx, 0, margin, margin)
    for k, (out, (height, _), (rows, cols)) in enumerate(zip(outs, block_shapes(nz, nx, tile), places)):
        copies.append(pltpu.make_async_copy(spec_ref.at[c, rows, cols], out.at[pl.ds(0, height), :], sems.at[k]))
        copies[-1].start()
    off_copy.wait()
    lane = lax.broadcasted_iota(jnp.int32, NOTE, 1)
    note = jnp.zeros(NOTE, jnp.float32)
    for j in range(off_ref.shape[0]):
        for k in range(2):
            note = jnp.where(lane == 2 * j + k, off_ref[j, k].astype(jnp.float32), note)
    note_ref[...] = note
    for out, (height, width) in zip(outs, block_shapes(nz, nx, tile)):
        fill = out.shape[0] - NOTE[0] - height
        if fill:
            out[height : height + fill, :] = jnp.zeros((fill, width), jnp.float32)
        out[height + fill :, : NOTE[1]] = note
    for copy in copies:
        copy.wait()


def read_notes(notes, smems, sems):
    copies = [pltpu.make_async_copy(note, smem, sems.at[k]) for k, (note, smem) in enumerate(zip(notes, smems))]
    for copy in copies:
        copy.start()
    return copies


def note_of(block):
    return block.at[pl.ds(block.shape[0] - NOTE[0], NOTE[0]), pl.ds(0, NOTE[1])]


def offset_in(note, j):
    return note[0, 2 * j].astype(jnp.int32), note[0, 2 * j + 1].astype(jnp.int32)


def fetch_kernel(*refs):
    *refs, table_a, table_b, sems = refs
    count = len(refs) // 2
    *sources, waves = refs[: count + 1]
    copies = [pltpu.make_async_copy(src, refs[count + 1 + k], sems.at[k]) for k, src in enumerate(sources)]
    for copy in copies:
        copy.start()
    cosine, sine, minus = (waves[k] for k in range(3))
    size = cosine.shape[0]
    for table, blocks in ((table_a, (cosine, sine, minus, cosine)), (table_b, (cosine, minus, sine, cosine))):
        for k, block in enumerate(blocks):
            at, left = k // 2 * size, k % 2 * size
            table[at : at + size, left : left + size] = block
    for copy in copies:
        copy.wait()


def cut_patches(note, padded, out):
    npos, size, _ = out.shape
    lane = lax.broadcasted_iota(jnp.int32, (size + 8, size), 1)
    for j in range(npos):
        row, col = offset_in(note, j)
        base, shift = aligned(row)
        rows = padded[pl.ds(base, size + 8), :]
        mixed = rows_up(jnp.where(lane >= col, rows[:, :size], rows[:, size:]), shift)
        out[j] = pltpu.roll(mixed, lax.rem(size - col, size), axis=1)


def patches_kernel(nz, nx, ours, note_ref, unused_ref, spec_ref, *refs):
    z, x, c = (lax.axis_index(a) for a in GROUP)
    *blocks, out, padded, note, sems = refs
    copies = read_notes([note_ref], [note], sems)
    tile = spec_ref.shape[1]
    margin = (padded.shape[0] - tile) // 2
    padded[margin : margin + tile, margin : margin + tile] = spec_ref[c if ours else 1 - c]
    if len(ways_of(nx)) == 1:
        far_cols = pl.ds(pl.multiple_of((1 - side_of(x, 0)) * (margin + tile), margin), margin)
        padded[:, far_cols] = jnp.zeros((padded.shape[0], margin), jnp.float32)
    places = block_places(z, x, nz, nx, margin, margin + tile, margin)
    shapes = block_shapes(nz, nx, tile)
    pieces = {}
    for which, array in zip(packing_order(nz, nx), blocks):
        for k, places_of in zip(which, packed_places([shapes[k] for k in which])):
            pieces[k] = [(array, at) for at, _, _ in places_of]
    for k, ((height, width), (rows, cols), ok) in enumerate(zip(shapes, places, block_valid(z, x, nz, nx))):

        @pl.when(ok)
        def _():
            if ours:
                padded[rows, cols] = blocks[k][:height, :]
            else:
                parts = [array[at : at + height, :] for array, at in pieces[k]]
                padded[rows, cols] = parts[0] if len(parts) == 1 else jnp.concatenate(parts, axis=1)

        @pl.when(jnp.logical_not(ok))
        def _():
            padded[rows, cols] = jnp.zeros((height, width), jnp.float32)

    copies[0].wait()
    cut_patches(note, padded, out)


def pack_kernel(shapes, waits, *refs):
    *blocks, out = refs[waits:]
    for block, pieces in zip(blocks, packed_places(shapes)):
        for at, col, height in pieces:
            out[at : at + height, :] = block[:height, col : col + out.shape[1]]


def positions_kernel(patch_ref, patch_other_ref, probe_ref, amp_ref, ta_ref, tb_ref, own_ref, other_ref, probe_own_ref, probe_other_ref):
    first = lax.axis_index("pos") == 0
    npos, size, _ = patch_ref.shape
    table_a = ta_ref[...]
    table_b = tb_ref[...]
    probe_real = probe_ref[0]
    probe_imag = probe_ref[1]

    def side_by_side(both):
        return jnp.concatenate([both[:size], both[size:]], axis=1)

    grad_real = jnp.zeros((size, size), jnp.float32)
    grad_imag = jnp.zeros((size, size), jnp.float32)
    for j in range(npos):
        patch_real = jnp.where(first, patch_ref[j], patch_other_ref[j])
        patch_imag = jnp.where(first, patch_other_ref[j], patch_ref[j])
        exit_real = probe_real * patch_real - probe_imag * patch_imag
        exit_imag = probe_real * patch_imag + probe_imag * patch_real
        wave = jnp.concatenate([exit_real, exit_imag], axis=0).astype(jnp.bfloat16)
        half = jnp.dot(table_a, wave, preferred_element_type=jnp.float32).astype(jnp.bfloat16)
        far = jnp.dot(side_by_side(half), table_b, preferred_element_type=jnp.float32)
        far_real, far_imag = far[:, :size], far[:, size:]
        power = far_real * far_real + far_imag * far_imag
        ratio = amp_ref[j].astype(jnp.float32) * jnp.minimum(lax.rsqrt(power), 1.0 / 0.2)
        projected = jnp.concatenate([far_real * ratio, far_imag * ratio], axis=0).astype(jnp.bfloat16)
        back_half = jnp.dot(table_b, projected, preferred_element_type=jnp.float32).astype(jnp.bfloat16)
        back = jnp.dot(side_by_side(back_half), table_a, preferred_element_type=jnp.float32)
        diff_real = back[:, :size] - exit_real
        diff_imag = back[:, size:] - exit_imag
        term_real = probe_real * diff_real + probe_imag * diff_imag
        term_imag = probe_real * diff_imag - probe_imag * diff_real
        own_ref[j] = jnp.where(first, term_real, term_imag)
        other_ref[j] = jnp.where(first, term_imag, term_real)
        grad_real += patch_real * diff_real + patch_imag * diff_imag
        grad_imag += patch_real * diff_imag - patch_imag * diff_real
    probe_own_ref[...] = jnp.where(first, grad_real, grad_imag)
    probe_other_ref[...] = jnp.where(first, grad_imag, grad_real)


def half_of(z, x, c):
    return jnp.where(c == 0, lax.rem(x, 2), lax.rem(z, 2))


def halve_kernel(own_ref, recv_ref, unused_ref, unused_light_ref, keep_ref, give_ref, handed_on_ref):
    half = half_of(*(lax.axis_index(a) for a in GROUP))
    rows = keep_ref.shape[0]
    for at, out in ((half, keep_ref), (1 - half, give_ref)):
        span = pl.ds(pl.multiple_of(at * rows, rows), rows)
        out[...] = own_ref[span, :] + recv_ref[span, :]


def gather_kernel(nx, note_ref, other_note_ref, own_ref, recv_ref, unused_ref, middle_ref, *refs):
    x = lax.axis_index("scany")
    *blocks, grad, note, other_note, sems = refs
    copies = read_notes([note_ref, other_note_ref], [note, other_note], sems)
    npos, size, _ = own_ref.shape
    lane = lax.broadcasted_iota(jnp.int32, (size + 8, size), 1)
    grad[...] = jnp.zeros_like(grad)
    for copy, offs, terms in zip(copies, (note, other_note), (own_ref, recv_ref)):
        copy.wait()
        for j in range(npos):
            row, col = offset_in(offs, j)
            base, shift = aligned(row)
            term = rows_down(pltpu.roll(terms[j], col, axis=1), shift)
            low = jnp.where(lane >= col, term, 0.0)
            rows = pl.ds(base, size + 8)
            grad[rows, :size] += low
            grad[rows, size:] += term - low
    tile = middle_ref.shape[1]
    margin = (middle_ref.shape[0] - tile) // 2
    middle_ref[...] = grad[:, margin : margin + tile]
    for block, way in zip(blocks, ways_of(nx)):
        block[...] = grad[:, pl.ds(pl.multiple_of(side_of(x, way) * (margin + tile), margin), margin)]


def fold_kernel(nz, nx, unused_ref, middle_ref, *refs):
    z, x = lax.axis_index("scanx"), lax.axis_index("scany")
    ways = ways_of(nx)
    blocks, (center_ref, *edges, total) = refs[: len(ways)], refs[len(ways) :]
    tile = center_ref.shape[0]
    margin = (middle_ref.shape[0] - tile) // 2
    total[...] = middle_ref[...]
    for block, way in zip(blocks, ways):
        at = pl.multiple_of(side_of(x, way) * (tile - margin), margin)

        @pl.when(valid_of(x, way, nx))
        def _():
            total[:, pl.ds(at, margin)] += block[...]

    center_ref[...] = total[margin : margin + tile, :]
    for way, edge in enumerate(edges):
        edge[...] = total[pl.ds(pl.multiple_of(side_of(z, way) * (margin + tile), margin), margin), :]


def update_kernel(nz, unused_ref, spec_ref, center_ref, light_ref, other_light_ref, edge_a, edge_b, *refs):
    z, c = lax.axis_index("scanx"), lax.axis_index("pos")
    upper_ref, lower_ref, grad = refs
    tile = center_ref.shape[0]
    grad[...] = center_ref[...]
    for way, edge in enumerate((edge_a, edge_b)):
        margin = edge.shape[0]
        at = pl.multiple_of(side_of(z, way) * (tile - margin), margin)

        @pl.when(valid_of(z, way, nz))
        def _():
            grad[pl.ds(at, margin), :] += edge[...]

    for at, out in ((0, upper_ref), (tile // 2, lower_ref)):
        span = pl.ds(at, tile // 2)
        out[...] = spec_ref[c, span, :] + grad[span, :] / (light_ref[span, :] + other_light_ref[span, :] + 1.0)


def add_kernel(a_ref, b_ref, *refs):
    refs[-1][...] = a_ref[...] + b_ref[...]


def specimen_kernel(upper_ref, lower_ref, other_upper_ref, other_lower_ref, out_ref, done_ref):
    c = lax.axis_index("pos")
    rows = upper_ref.shape[0]
    for part, upper, lower in ((c, upper_ref, lower_ref), (1 - c, other_upper_ref, other_lower_ref)):
        out_ref[part, :rows, :] = upper[...]
        out_ref[part, rows:, :] = lower[...]
    done_ref[...] = jnp.zeros(done_ref.shape, done_ref.dtype)


def probe_kernel(step_size, probe_ref, keep_ref, away_ref, keep_other_ref, away_other_ref, unused_ref, out_ref):
    z, x, c = (lax.axis_index(a) for a in GROUP)
    rows = keep_ref.shape[0]
    for part, keep, away in ((c, keep_ref, away_ref), (1 - c, keep_other_ref, away_other_ref)):
        half = half_of(z, x, part)
        for at, term in ((half, keep), (1 - half, away)):
            span = pl.ds(pl.multiple_of(at * rows, rows), rows)
            out_ref[part, span, :] = probe_ref[part, span, :] + term[...] * step_size


def light_kernel(npos, nz, nx, which, note_ref, probe_ref, before_ref, unused_ref, *refs):
    z, x, c = (lax.axis_index(a) for a in GROUP)
    blocks, (light_ref, power_ref, total, *notes, sems) = refs[: len(which)], refs[len(which) :]
    own = len(notes) > len(which)
    copies = read_notes(([note_ref] if own else []) + [note_of(b) for b in blocks], notes, sems)
    size = probe_ref.shape[1]
    margin = size // 2
    tile = light_ref.shape[0]
    power_ref[...] = probe_ref[0] * probe_ref[0] + probe_ref[1] * probe_ref[1]
    total[...] = jnp.zeros_like(total)
    lane = lax.broadcasted_iota(jnp.int32, (size, size), 1)

    def add(row, col, ok):
        ok = jnp.logical_and(ok, jnp.logical_and(jnp.abs(row) < tile, jnp.abs(col) < tile))

        @pl.when(ok)
        def _():
            base, shift = aligned(row + tile)
            moved = pltpu.roll(power_ref[...], lax.rem(col + size, size), axis=1)
            keep = jnp.logical_and(lane >= col, lane < col + size)
            total[pl.ds(base, size + 8), :] += rows_down(jnp.where(keep, moved, 0.0), shift)

    ways, valid = block_ways(nz, nx), block_valid(z, x, nz, nx)
    places = [((None, None), True)] * own + [(ways[k], valid[k]) for k in which]
    for copy, note, ((zway, xway), ok) in zip(copies, notes, places):
        copy.wait()
        down = 0 if zway is None else (2 * side_of(z, zway) - 1) * tile
        right = 0 if xway is None else (2 * side_of(x, xway) - 1) * tile
        for j in range(npos):
            row, col = offset_in(note, j)
            add(row + down - margin, col + right - margin, ok)
    if own:
        light_ref[...] = total[tile : 2 * tile, :]
    else:
        light_ref[...] = before_ref[...] + total[tile : 2 * tile, :]


def call(kernel, out_shape, specs, *operands, scratch=(), outs=None, aliases={}, vmem=16 * 1024 * 1024):
    return pl.pallas_call(
        kernel,
        out_shape=out_shape,
        in_specs=specs,
        out_specs=outs or [VMEM] * len(out_shape),
        scratch_shapes=list(scratch),
        input_output_aliases=aliases,
        compiler_params=pltpu.CompilerParams(vmem_limit_bytes=vmem),
    )(*operands)


def dma(count):
    return pltpu.SemaphoreType.DMA((count,))


def shards(sizes, specimen, probe_wave, amplitudes, offsets):
    nz, nx, nc = sizes
    size = probe_wave.shape[1]
    margin = size // 2
    tile = specimen.shape[1]
    npos = offsets.shape[0]
    ways = block_ways(nz, nx)
    xways = ways_of(nx)
    targets = block_targets(nz, nx)

    def send(value, target):
        return lax.ppermute(value, GROUP, permutation(sizes, target))

    def to_core(value):
        return lax.ppermute(value, "pos", PART_SWAP)

    shapes = block_shapes(nz, nx, tile)
    *blocks, note = call(
        functools.partial(halo_blocks_kernel, nz, nx),
        [f32(h + NOTE[0] + (FILL_ROWS if v is None else 0), w) for (h, w), (v, _) in zip(shapes, ways)] + [f32(*NOTE)],
        [HBM, HBM],
        offsets,
        specimen,
        scratch=[pltpu.SMEM(offsets.shape, jnp.int32), dma(len(ways) + 1)],
        vmem=KEEP_IN_HBM,
    )
    recv = [send(block, target) for block, target in zip(blocks, targets)]

    waves = jnp.asarray(dft_waves(size))
    late = (note, specimen, probe_wave)
    note, specimen_v, probe_v, ta_v, tb_v = call(
        fetch_kernel,
        [jax.ShapeDtypeStruct(a.shape, a.dtype) for a in late]
        + [jax.ShapeDtypeStruct((2 * size, 2 * size), jnp.bfloat16)] * 2,
        [ANY] * len(late) + [VMEM],
        *late,
        waves,
        scratch=[dma(len(late))],
    )
    def patches_from(ours, after, *arrays):
        return call(
            functools.partial(patches_kernel, nz, nx, ours),
            [f32(npos, size, size)],
            [VMEM, ANY] + [VMEM] * (1 + len(arrays)),
            note,
            after,
            specimen,
            *arrays,
            scratch=[pltpu.VMEM((tile + size, tile + size), jnp.float32), NOTE_SMEM, dma(1)],
        )[0]

    def light_from(which, own, before, after):
        return call(
            functools.partial(light_kernel, npos, nz, nx, which),
            [f32(tile, tile)],
            [VMEM, VMEM, ANY if own else VMEM, ANY] + [VMEM] * len(which),
            note,
            probe_v,
            before,
            after,
            *[recv[k] for k in which],
            scratch=[
                pltpu.VMEM((size, size), jnp.float32),
                pltpu.VMEM((3 * tile, size), jnp.float32),
                *[NOTE_SMEM] * (own + len(which)),
                dma(own + len(which)),
            ],
        )[0]

    corners, along_z, along_x = packing_order(nz, nx)
    def packed(which, *after):
        chosen = [shapes[k] for k in which]
        return call(
            functools.partial(pack_kernel, chosen, len(after)),
            [f32(sum(h * w for h, w in chosen) // margin, margin)],
            [ANY] * len(after) + [VMEM] * len(which),
            *after,
            *[recv[k] for k in which],
        )[0]

    packed_corners = packed(corners, probe_v, *[recv[k] for k in along_x])
    other_corners = to_core(packed_corners)
    light = light_from(corners + along_x, True, packed_corners, packed_corners)
    other_x = to_core(packed(along_x, packed_corners))
    packed_z = packed(along_z, light, other_corners, other_x)
    patches = patches_from(True, packed_z, *recv)
    patches_other = patches_from(False, patches, other_corners, to_core(packed_z), other_x)
    own, other, probe_own, probe_other = call(
        positions_kernel,
        [f32(npos, size, size)] * 2 + [f32(size, size)] * 2,
        [VMEM] * 6,
        patches,
        patches_other,
        probe_v,
        amplitudes,
        ta_v,
        tb_v,
    )
    other_note = to_core(note)
    light = light_from(along_z, False, light, own)

    zbits = [("z", 1 << k) for k in range(nz.bit_length() - 1)]
    xbits = [("x", 1 << k) for k in range(nx.bit_length() - 1)]
    orders = (xbits[:1] + zbits + xbits[1:], zbits + xbits)

    def stage(k):
        def target(z, x, c):
            axis, bit = orders[c][k]
            return (z ^ bit, x, c) if axis == "z" else (z, x ^ bit, c)

        return target

    half = f32(size // 2, size)
    keep, away, other = call(
        halve_kernel,
        [half] * 2 + [f32(npos, size, size)],
        [VMEM, VMEM, ANY, ANY],
        probe_own,
        to_core(probe_other),
        other,
        light,
        outs=[VMEM, VMEM, ANY],
        aliases={2: 2},
    )
    terms = to_core(other)
    middle, *beyond = call(
        functools.partial(gather_kernel, nx),
        [f32(tile + size, tile)] + [f32(tile + size, margin)] * len(xways),
        [VMEM] * 4 + [ANY],
        note,
        other_note,
        own,
        terms,
        keep,
        scratch=[pltpu.VMEM((tile + size, tile + size), jnp.float32), NOTE_SMEM, NOTE_SMEM, dma(2)],
    )
    (keep,) = call(add_kernel, [half], [VMEM] * 2 + [ANY], keep, send(away, stage(0)), middle)
    beside = [send(piece, targets[ways.index((None, way))]) for piece, way in zip(beyond, xways)]
    (keep,) = call(add_kernel, [half], [VMEM] * 2, keep, send(keep, stage(1)))
    center, *edges = call(
        functools.partial(fold_kernel, nz, nx),
        [f32(tile, tile)] + [f32(margin, tile)] * 2,
        [ANY] + [VMEM] * (1 + len(beside)),
        keep,
        middle,
        *beside,
        scratch=[pltpu.VMEM((tile + size, tile), jnp.float32)],
    )
    arrived = [send(edge, targets[ways.index((way, None))]) for way, edge in enumerate(edges)]
    for k in range(2, len(orders[0])):
        (keep,) = call(add_kernel, [half], [VMEM] * 2, keep, send(keep, stage(k)))
    updated = call(
        functools.partial(update_kernel, nz),
        [f32(tile // 2, tile)] * 2,
        [ANY] + [VMEM] * (4 + len(arrived)),
        keep,
        specimen_v,
        center,
        light,
        to_core(light),
        *arrived,
        scratch=[pltpu.VMEM((tile, tile), jnp.float32)],
    )
    away = send(keep, stage(0))
    new_specimen, done = call(
        specimen_kernel, [f32(2, tile, tile), f32(*NOTE)], [VMEM] * 4, *updated, *[to_core(u) for u in updated]
    )
    step_size = 1.0 / math.sqrt(npos * nz * nx * nc)
    (new_probe,) = call(
        functools.partial(probe_kernel, step_size),
        [f32(2, size, size)],
        [VMEM] * 5 + [ANY],
        probe_v,
        keep,
        away,
        to_core(keep),
        to_core(away),
        done,
    )
    return (new_specimen, new_probe)


def solution(mesh):
    sizes = tuple(mesh.shape[a] for a in GROUP)
    placed = (
        P(None, ("groups", "scanx"), "scany"),
        P(None, "groups", None),
        P(("groups", "scanx", "scany", "pos"), None, None),
        P(("groups", "scanx", "scany", "pos"), None),
    )
    return jax.shard_map(
        functools.partial(shards, sizes),
        mesh=mesh,
        in_specs=placed,
        out_specs=(P(None, ("groups", "scanx"), "scany"), P(None, "groups", None)),
        check_vma=False,
    )
```
